128 devices in a mesh: gx: 4 (over z), gy: 4 (over y_hi, core), gz: 8 (over y_lo, x).
Axes of the slice: x: 4, y: 4 (y_hi: 2, y_lo: 2; y = y_hi * 2 + y_lo), z: 4, core: 2. Of those that a mesh axis runs over, the one named last changes fastest.
Arguments:
- wavefunctions: float32 [28, 28, 112, 128], P('gx', 'gy', 'gz'), may hold values from -6 to 6
- hamiltonians: float32 [4, 4, 16, 512, 512], P('gx', 'gy', 'gz'), as said below
- cell_order: int32 [4, 4, 16, 512], P('gx', 'gy', 'gz'), may hold values from 0 to 511, each once within a row
Outputs:
- rotated: float32 [28, 28, 112, 128], P('gx', 'gy', 'gz')
The draws below stay inside these ranges and needn't reach their ends.
Inputs may be any that keep to these rules, and one draw needn't show every extreme that they name: `cell_order`: each cell's row holds every lattice position of the cell once. `hamiltonians`: each cell's matrix is symmetric.
All inputs are finite; a program needn't handle non-finite values.
Results may differ from the reference program's by a relative error of at most 0.00014.
Values sent between devices are 32-bit elements; how exact they have to be, the bound alone decides.
A program may use at most 64 MiB of HBM per device.

```python
import jax
import jax.numpy as jnp
from jax import lax

NPE = 8
CDOF = 512
STATES = 128
DEGREE = 6
NS_STEPS = 12
GCX = 4
GCY = 4
GCZ = 16
NX = 28
NY = 28
NZ = 112
NODES = 87808


def draw_hamiltonians(key, part):
    key = jax.random.fold_in(key, 7)
    array_shape = (GCX, GCY, GCZ, CDOF, CDOF)
    spread = 1.0 / 48.0
    samples = jax.random.normal(key, array_shape, jnp.float32) * spread
    return 0.5 * (samples + jnp.swapaxes(samples, -1, -2))


def steps_of(own_key, dims, shards, low, high):
    factor_of = 1.0
    for dim, blocks in shards:
        heights = jax.random.uniform(jax.random.fold_in(jax.random.fold_in(own_key, 6), dim), (blocks,), jnp.float32, low / len(shards), high / len(shards))
        factor_of = factor_of * jnp.repeat(jnp.exp(heights), dims[dim] // blocks).reshape((-1,) + (1,) * (len(dims) - 1 - dim))
    return factor_of


def scatter_about(rng, dims, width, most, split=(), kind=jnp.bfloat16):
    values = jax.random.normal(rng, dims, jnp.float32) * width
    if len(split) > 0:
        values = steps_of(rng, dims, split, -0.22, 0.18) * values
    return jnp.clip(values, min=-most, max=most).astype(kind)


def setup_inputs(seed: int = 0) -> dict:
    splits = jax.random.split(jax.random.key(seed), 4)
    return {
        "wavefunctions": scatter_about(splits[0], (NX, NY, NZ, STATES), 1.0, 6.0, ((0, 4), (1, 4), (2, 8)), jnp.float32),
        "hamiltonians": draw_hamiltonians(jax.random.fold_in(splits[3], 71), 0),
        "cell_order": jax.vmap(lambda own: jax.random.permutation(own, CDOF))(jax.random.split(splits[2], GCX * GCY * GCZ)).reshape((GCX, GCY, GCZ, CDOF)).astype(jnp.int32),
    }


highest = lax.Precision.HIGHEST
center_value = 0.4
half_width = 0.7

def split_axis(array, axis_dim, outer, inner):
    return array.reshape(array.shape[:axis_dim] + (outer, inner) + array.shape[axis_dim + 1:])

def merge_axis(array, axis_dim):
    return array.reshape(array.shape[:axis_dim] + (array.shape[axis_dim] * array.shape[axis_dim + 1],) + array.shape[axis_dim + 2:])

def take_range(array, start, limit, axis_dim, stride=1):
    return lax.slice_in_dim(array, start, limit, stride, axis_dim)

def cells_from_nodes(extended, edge_nodes):
    for axis_dim in range(3):
        length = extended.shape[axis_dim] - 1
        count_cells = length // (edge_nodes - 1)
        leading = split_axis(take_range(extended, 0, length, axis_dim), axis_dim, count_cells, edge_nodes - 1)
        closing = split_axis(take_range(extended, edge_nodes - 1, length + 1, axis_dim, edge_nodes - 1), axis_dim, count_cells, 1)
        extended = merge_axis(jnp.concatenate([leading, closing], axis=axis_dim + 1), axis_dim)
    return extended

def lattice_hamiltonians(hamiltonians, cell_order):
    matrices = hamiltonians.reshape((-1,) + hamiltonians.shape[-2:])
    orders = cell_order.reshape((-1, cell_order.shape[-1]))
    inverse = jnp.argsort(orders, axis=-1).astype(jnp.int32)

    def relabel(matrix, positions):
        return matrix[positions][:, positions]
    return jax.vmap(relabel)(matrices, inverse)

def cell_products(field, lattice_ham, edge_nodes):
    cells_x = field.shape[0] // edge_nodes
    cells_y = field.shape[1] // edge_nodes
    cells_z = field.shape[2] // edge_nodes
    states = field.shape[3]
    blocks = field.reshape(cells_x, edge_nodes, cells_y, edge_nodes, cells_z, edge_nodes, states)
    blocks = blocks.transpose(0, 2, 4, 1, 3, 5, 6).reshape(cells_x * cells_y * cells_z, edge_nodes ** 3, states)
    products = jnp.einsum('cjk,cks->cjs', lattice_ham, blocks, precision=highest)
    products = products.reshape(cells_x, cells_y, cells_z, edge_nodes, edge_nodes, edge_nodes, states)
    return products.transpose(0, 3, 1, 4, 2, 5, 6).reshape(field.shape)

def fold_cells(field, axis_dim, edge_nodes):
    count_cells = field.shape[axis_dim] // edge_nodes
    grouped = split_axis(field, axis_dim, count_cells, edge_nodes)
    interior = take_range(grouped, 0, edge_nodes - 1, axis_dim + 1)
    endpoint = take_range(grouped, edge_nodes - 1, edge_nodes, axis_dim + 1)
    top_plane = take_range(endpoint, count_cells - 1, count_cells, axis_dim)
    incoming = jnp.concatenate([top_plane, take_range(endpoint, 0, count_cells - 1, axis_dim)], axis=axis_dim)
    opening = take_range(interior, 0, 1, axis_dim + 1) + incoming
    interior = jnp.concatenate([opening, take_range(interior, 1, edge_nodes - 1, axis_dim + 1)], axis=axis_dim + 1)
    return merge_axis(interior, axis_dim)

def chebyshev(apply_operator, start, degree):
    previous = start
    current = (apply_operator(start) - center_value * start) / half_width
    for counter in range(degree - 1):
        following = 2.0 * (apply_operator(current) - center_value * current) / half_width - previous
        previous, current = (current, following)
    return current

def inverse_root(gram, steps):
    trace_value = jnp.trace(gram)
    scaled = gram / trace_value
    identity = jnp.eye(gram.shape[0], dtype=gram.dtype)

    def newton_step(counter, iterate_pair):
        square_root, inverse = iterate_pair
        middle = 3.0 * identity - jnp.dot(inverse, square_root, precision=highest)
        return (0.5 * jnp.dot(square_root, middle, precision=highest), 0.5 * jnp.dot(middle, inverse, precision=highest))
    square_root, inverse = lax.fori_loop(0, steps, newton_step, (scaled, identity))
    return inverse / jnp.sqrt(trace_value)

def reference(wavefunctions, hamiltonians, cell_order):
    lattice_ham = lattice_hamiltonians(hamiltonians, cell_order)

    def apply_operator(field):
        extended = field
        for axis_dim in range(3):
            extended = jnp.concatenate([extended, take_range(extended, 0, 1, axis_dim)], axis=axis_dim)
        summed = cell_products(cells_from_nodes(extended, NPE), lattice_ham, NPE)
        for axis_dim in range(3):
            summed = fold_cells(summed, axis_dim, NPE)
        return summed
    filtered = chebyshev(apply_operator, wavefunctions, DEGREE)
    columns = filtered.reshape(-1, filtered.shape[3])
    gram = jnp.dot(columns.T, columns, precision=highest) / NODES
    rotated = jnp.dot(columns, inverse_root(gram, NS_STEPS), precision=highest)
    return rotated.reshape(wavefunctions.shape)
```

```python
import functools
import itertools

import jax
import jax.numpy as jnp
from jax import lax
from jax.experimental import pallas as pl
from jax.experimental.pallas import tpu as pltpu
from jax.sharding import PartitionSpec as P

NPE = 8
CDOF = 512
STATES = 128
DEGREE = 6
NS_STEPS = 12
CENTER = 0.4
HALF_WIDTH = 0.7
AXES = ("gx", "gy", "gz")
MESH = pl.DeviceIdType.MESH
F32 = jnp.float32
BF16 = jnp.bfloat16

DIRECTIONS = sorted(
    (d for d in itertools.product((-1, 0, 1), repeat=3) if any(d)),
    key=lambda d: (-sum(map(abs, d)), d[2] == 0, d[1] == 0),
)
DOWN = [d for d in DIRECTIONS if max(d) <= 0]
UP = [d for d in DIRECTIONS if min(d) >= 0]


def split(value):
    high = value.astype(BF16)
    low = (value - high.astype(F32)).astype(BF16)
    return high, low


def product(left, right):
    rows, columns = left.shape[0], right.shape[1]
    all_four = jnp.dot(
        jnp.concatenate(split(left), axis=0),
        jnp.concatenate(split(right), axis=1),
        preferred_element_type=F32,
    )
    return (
        all_four[:rows, :columns]
        + (all_four[:rows, columns:] + all_four[rows:, :columns])
        + all_four[rows:, columns:]
    )


def side(step):
    return (step + 1) // 2


def kind_and_place(d):
    dx, dy, dz = d
    if dz == 0:
        if dy == 0:
            return "x", side(dx)
        if dx == 0:
            return "y", side(dy)
        return "xy", side(dx) * 2 + side(dy)
    if dx == 0 and dy == 0:
        return "z", side(dz)
    if dy == 0:
        return "xz", side(dx) * 2 + side(dz)
    if dx == 0:
        return "yz", side(dy) * 2 + side(dz)
    return "xyz", side(dx) * 4 + side(dy) * 2 + side(dz)


KINDS = ("xyz", "yz", "xz", "xy", "y", "x", "z")


def kernel(
    sizes,
    wave_ref,
    ham_ref,
    order_ref,
    out_ref,
    ham_raw,
    ham_bf,
    field,
    summed,
    y_pack,
    z_pack,
    yz_pack,
    r_x,
    r_y,
    r_z,
    r_xy,
    r_xz,
    r_yz,
    r_xyz,
    gram,
    r_scatter,
    r_reduce,
    r_gather,
    ham_sem,
    send_sem,
    recv_sem,
    sum_send,
    sum_recv,
):
    me = tuple(lax.axis_index(a) for a in AXES)
    nx, ny, nz = sizes
    plane = nx * ny
    received = dict(x=r_x, y=r_y, z=r_z, xy=r_xy, xz=r_xz, yz=r_yz, xyz=r_xyz)

    def neighbour(d):
        return tuple(lax.rem(m + (s + n), n) for m, s, n in zip(me, d, sizes))

    def along_z(j):
        return (me[0], me[1], lax.rem(me[2] + j, nz))

    def in_plane(j):
        other = lax.rem(me[0] * ny + me[1] + j, plane)
        return (other // ny, lax.rem(other, ny), me[2])

    for c in range(2):
        pltpu.make_async_copy(ham_ref.at[c], ham_raw.at[c], ham_sem.at[c]).start()

    barrier = pltpu.get_barrier_semaphore()
    greeted = [neighbour(d) for d in DIRECTIONS]
    greeted += [along_z(j) for j in range(2, nz - 1)]
    greeted += [in_plane(j) for j in range(1, plane)]
    for device in greeted:
        pl.semaphore_signal(barrier, inc=1, device_id=device, device_id_type=MESH)

    field[0] = jnp.zeros((2, CDOF, STATES), F32)
    summed[...] = jnp.zeros_like(summed)
    for x in range(NPE - 1):
        for y in range(NPE - 1):
            row = (x * NPE + y) * NPE
            summed[0, row : row + 8, :] = wave_ref[x, y, 0:8, :]
            summed[1, row : row + 7, :] = wave_ref[x, y, 7:14, :]

    def pack():
        for s, z in ((0, 0), (1, 7)):
            z_pack[s] = summed[s, pl.ds(z, 64, stride=8), :]
            for t, y in ((0, 0), (1, 7)):
                yz_pack[t * 2 + s] = z_pack[s, pl.ds(y, 8, stride=8), :]
        for t, y in ((0, 0), (1, 7)):
            for c in range(2):
                for x in range(NPE):
                    row = (x * NPE + y) * NPE
                    y_pack[t, c, x * 8 : x * 8 + 8, :] = summed[c, row : row + 8, :]

    def message(d, slot):
        dx, dy, dz = d
        kind, place = kind_and_place(d)
        ix, iy = 7 * side(dx), 7 * side(dy)
        if kind == "x":
            source = summed.at[:, pl.ds(ix * 64, 64)]
        elif kind == "y":
            source = y_pack.at[place]
        elif kind == "z":
            source = z_pack.at[place]
        elif kind == "xy":
            source = summed.at[:, pl.ds(ix * 64 + iy * 8, 8)]
        elif kind == "xz":
            source = z_pack.at[side(dz), pl.ds(ix * 8, 8)]
        elif kind == "yz":
            source = yz_pack.at[place]
        else:
            source = z_pack.at[side(dz), pl.ds(ix * 8 + iy, 1)]
        if kind == "xyz":
            target = r_xyz.at[slot, pl.ds(place, 1)]
        else:
            target = received[kind].at[slot, place]
        k = KINDS.index(kind)
        return pltpu.make_async_remote_copy(
            src_ref=source,
            dst_ref=target,
            send_sem=send_sem.at[k],
            recv_sem=recv_sem.at[slot, k],
            device_id=neighbour(d),
            device_id_type=MESH,
        )

    def send(directions, slot):
        for d in directions:
            message(d, slot).start()

    def every(kind, directions, slot):
        count = sum(kind_and_place(d)[0] == kind for d in directions)
        whole = received[kind].at[slot, pl.ds(0, count)]
        k = KINDS.index(kind)
        return pltpu.make_async_remote_copy(
            src_ref=whole,
            dst_ref=whole,
            send_sem=send_sem.at[k],
            recv_sem=recv_sem.at[slot, k],
            device_id=neighbour((1, 0, 0)),
            device_id_type=MESH,
        )

    def wait_sent(directions, slot):
        for kind in KINDS:
            every(kind, directions, slot).wait_send()

    def collect(total, directions, slot, scale):
        for kind in KINDS:
            every(kind, directions, slot).wait_recv()
            for d in directions:
                if kind_and_place(d)[0] != kind:
                    continue
                dx, dy, dz = d
                place = kind_and_place(d)[1]
                ix, iy = 7 * (1 - side(dx)), 7 * (1 - side(dy))
                c, iz = (0, 0) if dz > 0 else (1, 7)
                if kind == "x":
                    total[:, ix * 64 : ix * 64 + 64, :] += scale * r_x[slot, place]
                elif kind == "y":
                    for x in range(NPE):
                        row = (x * NPE + iy) * NPE
                        total[:, row : row + 8, :] += (
                            scale * r_y[slot, place, :, x * 8 : x * 8 + 8, :]
                        )
                elif kind == "xy":
                    row = (ix * NPE + iy) * NPE
                    total[:, row : row + 8, :] += scale * r_xy[slot, place]
                elif kind == "z":
                    total[c, pl.ds(iz, 64, stride=8), :] += scale * r_z[slot, place]
                elif kind == "xz":
                    rows = pl.ds(ix * 64 + iz, 8, stride=8)
                    total[c, rows, :] += scale * r_xz[slot, place]
                elif kind == "yz":
                    rows = pl.ds(iy * 8 + iz, 8, stride=64)
                    total[c, rows, :] += scale * r_yz[slot, place]
                else:
                    row = (ix * NPE + iy) * NPE + iz
                    total[c, row : row + 1, :] += (
                        scale * r_xyz[slot, place : place + 1, :]
                    )

    pack()
    pl.semaphore_wait(barrier, len(greeted))
    send(DOWN, 0)

    for c in range(2):
        pltpu.make_async_copy(ham_ref.at[c], ham_raw.at[c], ham_sem.at[c]).wait()
        rows = lax.broadcasted_iota(jnp.int32, (CDOF, CDOF), 0)
        chosen = (rows == order_ref[c : c + 1, :]).astype(F32).astype(BF16)
        for part, value in enumerate(split(ham_raw[c])):
            half = jnp.dot(chosen, value, preferred_element_type=F32).astype(BF16)
            ham_bf[c, part * CDOF : (part + 1) * CDOF, :] = lax.dot_general(
                half, chosen, (((1,), (1,)), ((), ())), preferred_element_type=F32
            ).astype(BF16)

    field[0] = summed[...]
    collect(field.at[0], DOWN, 0, 1.0)
    wait_sent(DOWN, 0)

    def multiply(now):
        for c in range(2):
            value = jnp.concatenate(split(field[now, c]), axis=1)
            all_four = jnp.dot(ham_bf[c], value, preferred_element_type=F32)
            summed[c] = (
                all_four[:CDOF, :STATES]
                + (all_four[:CDOF, STATES:] + all_four[CDOF:, :STATES])
                + all_four[CDOF:, STATES:]
            )
        middle = summed[0, pl.ds(7, 64, stride=8), :] + summed[1, pl.ds(0, 64, stride=8), :]
        summed[0, pl.ds(7, 64, stride=8), :] = middle
        summed[1, pl.ds(0, 64, stride=8), :] = middle

    def advance(now, later, gain, shift, keep):
        for c in range(2):
            fresh = gain * summed[c] + shift * field[now, c]
            if keep:
                fresh = fresh - field[later, c]
            field[later, c] = fresh

    def apply(now, later, slot, directions, factor, keep):
        gain = factor / HALF_WIDTH
        multiply(now)
        pack()
        send(directions, slot)
        advance(now, later, gain, -factor * CENTER / HALF_WIDTH, keep)
        collect(field.at[later], directions, slot, gain)
        wait_sent(directions, slot)

    apply(0, 1, 1, DIRECTIONS, 1.0, False)

    def step(k, carry):
        now = lax.rem(k, 2)
        apply(now, 1 - now, 1 - now, DIRECTIONS, 2.0, True)
        return carry

    lax.fori_loop(1, DEGREE - 1, step, 0)
    last = DEGREE % 2
    apply(1 - last, last, last, UP, 2.0, True)

    owned_z = lax.broadcasted_iota(jnp.int32, (7 * 8, STATES), 0) % 8 < 7
    blocks = []
    for c in range(2):
        for x in range(NPE - 1):
            block = field[last, c, x * 64 : x * 64 + 56, :]
            blocks.append(jnp.where(owned_z, block, 0.0))
    columns = jnp.concatenate(blocks, axis=0)
    high, low = split(columns)
    both = lax.dot_general(
        high,
        jnp.concatenate([high, low], axis=1),
        (((0,), (0,)), ((), ())),
        preferred_element_type=F32,
    )
    cross = both[:, STATES:]
    gram[...] = both[:, :STATES] + (cross + cross.T)

    piece = STATES // nz
    mine = pl.ds(pl.multiple_of(me[2] * piece, piece), piece)
    index = me[0] * ny + me[1]

    def scatter(j):
        rows = pl.ds(pl.multiple_of(lax.rem(me[2] + j, nz) * piece, piece), piece)
        return pltpu.make_async_remote_copy(
            src_ref=gram.at[rows],
            dst_ref=r_scatter.at[j - 1],
            send_sem=sum_send.at[0],
            recv_sem=sum_recv.at[0],
            device_id=along_z(j),
            device_id_type=MESH,
        )

    def reduce(j):
        return pltpu.make_async_remote_copy(
            src_ref=r_reduce.at[index],
            dst_ref=r_reduce.at[index],
            send_sem=sum_send.at[1],
            recv_sem=sum_recv.at[1],
            device_id=in_plane(j),
            device_id_type=MESH,
        )

    def gather(j):
        return pltpu.make_async_remote_copy(
            src_ref=r_gather.at[mine],
            dst_ref=r_gather.at[mine],
            send_sem=sum_send.at[2],
            recv_sem=sum_recv.at[2],
            device_id=along_z(j),
            device_id_type=MESH,
        )

    def waiter(ref, k):
        return pltpu.make_async_remote_copy(
            src_ref=ref,
            dst_ref=ref,
            send_sem=sum_send.at[k],
            recv_sem=sum_recv.at[k],
            device_id=along_z(1),
            device_id_type=MESH,
        )

    for j in range(1, nz):
        scatter(j).start()
    waiter(r_scatter, 0).wait_recv()
    r_reduce[index] = gram[mine, :] + jnp.sum(r_scatter[...], axis=0)
    for j in range(1, plane):
        reduce(j).start()
    waiter(r_scatter, 0).wait_send()
    waiter(r_reduce.at[pl.ds(0, plane - 1)], 1).wait_recv()
    nodes = 686 * nx * ny * nz
    r_gather[mine, :] = jnp.sum(r_reduce[...], axis=0) * (1.0 / nodes)
    for j in range(1, nz):
        gather(j).start()
    waiter(r_reduce.at[pl.ds(0, plane - 1)], 1).wait_send()
    rest = r_gather.at[pl.ds(0, piece * (nz - 1))]
    waiter(rest, 2).wait_recv()

    total = r_gather[...]
    diagonal = lax.broadcasted_iota(jnp.int32, (STATES, STATES), 0) == (
        lax.broadcasted_iota(jnp.int32, (STATES, STATES), 1)
    )
    trace = jnp.sum(jnp.where(diagonal, total, 0.0), keepdims=True)
    three = jnp.where(diagonal, 3.0, 0.0)

    def newton(k, pair):
        root, inverse = pair
        middle = three - product(inverse, root)
        return 0.5 * product(root, middle), 0.5 * product(middle, inverse)

    _, inverse = lax.fori_loop(
        0, NS_STEPS, newton, (total / trace, jnp.where(diagonal, 1.0, 0.0))
    )
    rotation = inverse / jnp.sqrt(trace)
    for c in range(2):
        for x in range(NPE - 1):
            turned = product(field[last, c, x * 64 : x * 64 + 56, :], rotation)
            for y in range(NPE - 1):
                out_ref[x, y, c * 7 : c * 7 + 7, :] = turned[y * 8 : y * 8 + 7, :]
    waiter(rest, 2).wait_send()


def shards(wavefunctions, hamiltonians, cell_order):
    sizes = tuple(lax.axis_size(a) for a in AXES)
    plane = sizes[0] * sizes[1]
    piece = STATES // sizes[2]
    matrices = hamiltonians.reshape((2, CDOF, CDOF))
    orders = cell_order.reshape((2, CDOF))
    vmem = pl.BlockSpec(memory_space=pltpu.VMEM)

    return pl.pallas_call(
        functools.partial(kernel, sizes),
        out_shape=jax.ShapeDtypeStruct(wavefunctions.shape, F32),
        in_specs=[vmem, pl.BlockSpec(memory_space=pl.ANY), vmem],
        out_specs=vmem,
        scratch_shapes=[
            pltpu.VMEM((2, CDOF, CDOF), F32),
            pltpu.VMEM((2, 2 * CDOF, CDOF), BF16),
            pltpu.VMEM((2, 2, CDOF, STATES), F32),
            pltpu.VMEM((2, CDOF, STATES), F32),
            pltpu.VMEM((2, 2, 64, STATES), F32),
            pltpu.VMEM((2, 64, STATES), F32),
            pltpu.VMEM((4, 8, STATES), F32),
            pltpu.VMEM((2, 2, 2, 64, STATES), F32),
            pltpu.VMEM((2, 2, 2, 64, STATES), F32),
            pltpu.VMEM((2, 2, 64, STATES), F32),
            pltpu.VMEM((2, 4, 2, 8, STATES), F32),
            pltpu.VMEM((2, 4, 8, STATES), F32),
            pltpu.VMEM((2, 4, 8, STATES), F32),
            pltpu.VMEM((2, 8, STATES), F32),
            pltpu.VMEM((STATES, STATES), F32),
            pltpu.VMEM((sizes[2] - 1, piece, STATES), F32),
            pltpu.VMEM((plane, piece, STATES), F32),
            pltpu.VMEM((STATES, STATES), F32),
            pltpu.SemaphoreType.DMA((2,)),
            pltpu.SemaphoreType.DMA((len(KINDS),)),
            pltpu.SemaphoreType.DMA((2, len(KINDS))),
            pltpu.SemaphoreType.DMA((3,)),
            pltpu.SemaphoreType.DMA((3,)),
        ],
        compiler_params=pltpu.CompilerParams(
            collective_id=0, has_side_effects=True, vmem_limit_bytes=48 << 20
        ),
    )(wavefunctions, matrices, orders)


def solution(mesh):
    in_specs = (
        P("gx", "gy", "gz", None),
        P("gx", "gy", "gz", None, None),
        P("gx", "gy", "gz", None),
    )
    out_specs = P("gx", "gy", "gz", None)
    return jax.shard_map(
        shards, mesh=mesh, in_specs=in_specs, out_specs=out_specs, check_vma=False
    )
```

```python
import functools
import itertools

import jax
import jax.numpy as jnp
from jax import lax
from jax.experimental import pallas as pl
from jax.experimental.pallas import tpu as pltpu
from jax.sharding import PartitionSpec as P

NPE = 8
CDOF = 512
STATES = 128
DEGREE = 6
NS_STEPS = 12
CENTER = 0.4
HALF_WIDTH = 0.7
AXES = ("gx", "gy", "gz")
MESH = pl.DeviceIdType.MESH
F32 = jnp.float32
BF16 = jnp.bfloat16

NEAR, FAR = 1, 2
HOPS = {0: 0, NEAR: 0, FAR: 2}
ALL = sorted(
    (d for d in itertools.product((-1, 0, 1), (0, NEAR, FAR), (-1, 0, 1)) if any(d)),
    key=lambda d: -(2 * (abs(d[0]) + HOPS[d[1]] + abs(d[2])) + sum(map(bool, d))),
)
DOWN = [d for d in itertools.product((-1, 0), repeat=3) if any(d)]
UP = [d for d in itertools.product((1, 0), repeat=3) if any(d)]

KINDS = ("x", "z", "xz", "y", "xy", "yz", "xyz")
Z_ROWS, Y_ROWS, X_ROWS, SENT = 0, 64, 192, 320
INNER = 36 * 8


def split(value):
    high = value.astype(BF16)
    low = (value - high.astype(F32)).astype(BF16)
    return high, low


def product(left, right):
    rows, columns = left.shape[0], right.shape[1]
    all_four = jnp.dot(
        jnp.concatenate(split(left), axis=0),
        jnp.concatenate(split(right), axis=1),
        preferred_element_type=F32,
    )
    return (
        all_four[:rows, :columns]
        + (all_four[:rows, columns:] + all_four[rows:, :columns])
        + all_four[rows:, columns:]
    )


def side(step):
    return (step + 1) // 2


def kind_of(d):
    return "".join(name for name, step in zip("xyz", d) if not (isinstance(step, int) and step == 0))


def kernel(
    sizes,
    wave_hbm,
    ham_hbm,
    order_hbm,
    out_ref,
    wave_ref,
    ham_raw,
    order_ref,
    ham_sent,
    ham_inner,
    field,
    sent,
    inner,
    yz_pack,
    r_x,
    r_y,
    r_z,
    r_xy,
    r_xz,
    r_yz,
    r_xyz,
    gram,
    r_scatter,
    r_reduce,
    r_gather,
    load_sem,
    send_sem,
    recv_sem,
    sum_send,
    sum_recv,
):
    me = tuple(lax.axis_index(a) for a in AXES)
    nx, ny, nz = sizes
    plane = nx * ny
    received = dict(x=r_x, y=r_y, z=r_z, xy=r_xy, xz=r_xz, yz=r_yz, xyz=r_xyz)

    loads = [
        pltpu.make_async_copy(wave_hbm, wave_ref, load_sem.at[0]),
        pltpu.make_async_copy(order_hbm, order_ref, load_sem.at[1]),
        pltpu.make_async_copy(ham_hbm.at[0], ham_raw.at[0], load_sem.at[2]),
        pltpu.make_async_copy(ham_hbm.at[1], ham_raw.at[1], load_sem.at[3]),
    ]
    for load in loads:
        load.start()

    def neighbour(d):
        return tuple(lax.rem(m + (s + n), n) for m, s, n in zip(me, d, sizes))

    def along_z(j):
        return (me[0], me[1], lax.rem(me[2] + j, nz))

    def in_plane(j):
        other = lax.rem(me[0] * ny + me[1] + j, plane)
        return (other // ny, lax.rem(other, ny), me[2])

    barrier = pltpu.get_barrier_semaphore()
    for d in UP + DOWN:
        pl.semaphore_signal(barrier, inc=1, device_id=neighbour(d), device_id_type=MESH)

    far = 2 * lax.rem(me[1], 2) - 1

    def resolve(d):
        step = {0: 0, FAR: far, NEAR: -far}[d[1]]
        return d[0], step, d[2]

    every_way = [resolve(d) for d in ALL]

    def message(d, slot):
        dx, dy, dz = d
        kind = kind_of(d)
        sx, sy, sz = side(dx), side(dy), side(dz)
        if kind == "x":
            source, place = sent.at[:, pl.ds(X_ROWS + sx * 64, 64)], sx
        elif kind == "y":
            source, place = sent.at[:, pl.ds(Y_ROWS + sy * 64, 64)], sy
        elif kind == "z":
            source, place = sent.at[sz, pl.ds(Z_ROWS, 64)], sz
        elif kind == "xy":
            source = sent.at[:, pl.ds(X_ROWS + sx * 64 + sy * 56, 8)]
            place = sx * 2 + sy
        elif kind == "xz":
            source = sent.at[sz, pl.ds(Z_ROWS + sx * 56, 8)]
            place = sx * 2 + sz
        elif kind == "yz":
            source, place = yz_pack.at[sy, sz], sy * 2 + sz
        else:
            source = sent.at[sz, pl.ds(Z_ROWS + sx * 56 + sy * 7, 1)]
            place = sx * 4 + sy * 2 + sz
        if kind == "xyz":
            target = r_xyz.at[slot, pl.ds(place, 1)]
        else:
            target = received[kind].at[slot, place]
        k = KINDS.index(kind)
        return pltpu.make_async_remote_copy(
            src_ref=source,
            dst_ref=target,
            send_sem=send_sem.at[k],
            recv_sem=recv_sem.at[slot, k],
            device_id=neighbour(d),
            device_id_type=MESH,
        )

    def send(directions, slot):
        for d in directions:
            message(d, slot).start()

    def every(kind, directions, slot):
        count = sum(kind_of(d) == kind for d in directions)
        whole = received[kind].at[slot, pl.ds(0, count)]
        k = KINDS.index(kind)
        return pltpu.make_async_remote_copy(
            src_ref=whole,
            dst_ref=whole,
            send_sem=send_sem.at[k],
            recv_sem=recv_sem.at[slot, k],
            device_id=neighbour((1, 0, 0)),
            device_id_type=MESH,
        )

    def wait_sent(directions, slot):
        for kind in KINDS:
            every(kind, directions, slot).wait_send()

    def collect(total, directions, slot, scale):
        for kind in KINDS:
            every(kind, directions, slot).wait_recv()
            for dx, dy, dz in directions:
                if "".join(n for n, s in zip("xyz", (dx, dy, dz)) if s) != kind:
                    continue
                sx, sy, sz = side(dx), side(dy), side(dz)
                ix, iy = 7 * (1 - sx), 7 * (1 - sy)
                c, iz = (0, 0) if dz > 0 else (1, 7)
                if kind == "x":
                    total[:, ix * 64 : ix * 64 + 64, :] += scale * r_x[slot, sx]
                elif kind == "y":
                    for x in range(NPE):
                        row = (x * NPE + iy) * NPE
                        total[:, row : row + 8, :] += (
                            scale * r_y[slot, sy, :, x * 8 : x * 8 + 8, :]
                        )
                elif kind == "xy":
                    row = (ix * NPE + iy) * NPE
                    total[:, row : row + 8, :] += scale * r_xy[slot, sx * 2 + sy]
                elif kind == "z":
                    total[c, pl.ds(iz, 64, stride=8), :] += scale * r_z[slot, sz]
                elif kind == "xz":
                    rows = pl.ds(ix * 64 + iz, 8, stride=8)
                    total[c, rows, :] += scale * r_xz[slot, sx * 2 + sz]
                elif kind == "yz":
                    rows = pl.ds(iy * 8 + iz, 8, stride=64)
                    total[c, rows, :] += scale * r_yz[slot, sy * 2 + sz]
                else:
                    row = (ix * NPE + iy) * NPE + iz
                    place = sx * 4 + sy * 2 + sz
                    total[c, row : row + 1, :] += scale * r_xyz[slot, place : place + 1, :]

    SIGNED = [d for d in itertools.product((-1, 0, 1), repeat=3) if any(d)]

    def pack_yz():
        for s in range(2):
            for t in range(2):
                yz_pack[t, s] = sent[s, pl.ds(Z_ROWS + 7 * t, 8, stride=8), :]

    loads[0].wait()
    field[0] = jnp.zeros((2, CDOF, STATES), F32)
    for x in range(NPE - 1):
        for y in range(NPE - 1):
            row = (x * NPE + y) * NPE
            field[0, 0, row : row + 8, :] = wave_ref[x, y, 0:8, :]
            field[0, 1, row : row + 7, :] = wave_ref[x, y, 7:14, :]
    sent[0, Z_ROWS : Z_ROWS + 64, :] = field[0, 0, pl.ds(0, 64, stride=8), :]
    for c in range(2):
        sent[c, X_ROWS : X_ROWS + 64, :] = field[0, c, 0:64, :]
        for x in range(NPE):
            sent[c, Y_ROWS + x * 8 : Y_ROWS + x * 8 + 8, :] = field[0, c, x * 64 : x * 64 + 8, :]
    yz_pack[0, 0] = sent[0, pl.ds(Z_ROWS, 8, stride=8), :]
    pl.semaphore_wait(barrier, len(UP + DOWN))
    send(DOWN, 0)

    loads[1].wait()
    row_of = lax.broadcasted_iota(jnp.int32, (CDOF, CDOF), 0)
    n = lax.broadcasted_iota(jnp.int32, (64, CDOF), 0)
    for c in range(2):
        order = order_ref[c : c + 1, :]

        def chosen(rows):
            return (rows == order).astype(F32).astype(BF16)

        block = (n // 8) * 64 + lax.rem(n, 8)
        sent_rows = jnp.concatenate([n * 8 + 7 * c, block, block + 56, n, n + 448], axis=0)
        inner_rows = jnp.concatenate(
            [row_of[x * 64 + 8 : x * 64 + 56] for x in range(1, NPE - 1)], axis=0
        )
        pick = chosen(jnp.concatenate([sent_rows, inner_rows], axis=0))
        columns = chosen(row_of)
        loads[2 + c].wait()
        for part, value in enumerate(split(ham_raw[c])):
            half = jnp.dot(pick, value, preferred_element_type=F32).astype(BF16)
            whole = lax.dot_general(
                half, columns, (((1,), (1,)), ((), ())), preferred_element_type=F32
            ).astype(BF16)
            ham_sent[c, part * SENT : (part + 1) * SENT, :] = whole[:SENT]
            ham_inner[c, part * INNER : (part + 1) * INNER, :] = whole[SENT:]

    collect(field.at[0], DOWN, 0, 1.0)
    wait_sent(DOWN, 0)

    def four(matrix, value):
        rows = matrix.shape[0] // 2
        all_four = jnp.dot(matrix, value, preferred_element_type=F32)
        return (
            all_four[:rows, :STATES]
            + (all_four[:rows, STATES:] + all_four[rows:, :STATES])
            + all_four[rows:, STATES:]
        )

    def join(ref, first, count):
        upper, lower = pl.ds(first + 7, count, stride=8), pl.ds(first, count, stride=8)
        middle = ref[0, upper, :] + ref[1, lower, :]
        ref[0, upper, :] = middle
        ref[1, lower, :] = middle

    def apply(now, later, slot, directions, signed, factor, keep):
        gain, shift = factor / HALF_WIDTH, -factor * CENTER / HALF_WIDTH
        values = [jnp.concatenate(split(field[now, c]), axis=1) for c in range(2)]
        for c in range(2):
            sent[c] = four(ham_sent[c], values[c])
        join(sent, Y_ROWS, 32)
        pack_yz()
        send(directions, slot)
        for c in range(2):
            inner[c] = four(ham_inner[c], values[c])
        join(inner, 0, 36)

        def advance(c, row, count, products):
            rows = slice(row, row + count)
            fresh = gain * products + shift * field[now, c, rows, :]
            if keep:
                fresh = fresh - field[later, c, rows, :]
            field[later, c, rows, :] = fresh

        for c in range(2):
            for x in range(NPE):
                if x in (0, NPE - 1):
                    first = X_ROWS + 64 * (x // 7)
                    advance(c, x * 64, 64, sent[c, first : first + 64, :])
                    continue
                for t in range(2):
                    first = Y_ROWS + 64 * t + x * 8
                    advance(c, x * 64 + 56 * t, 8, sent[c, first : first + 8, :])
                first = (x - 1) * 48
                advance(c, x * 64 + 8, 48, inner[c, first : first + 48, :])
        collect(field.at[later], signed, slot, gain)
        wait_sent(signed, slot)

    apply(0, 1, 1, every_way, SIGNED, 1.0, False)

    def step(k, carry):
        now = lax.rem(k, 2)
        apply(now, 1 - now, 1 - now, every_way, SIGNED, 2.0, True)
        return carry

    lax.fori_loop(1, DEGREE - 1, step, 0)
    last = DEGREE % 2
    apply(1 - last, last, last, UP, UP, 2.0, True)

    owned_z = lax.broadcasted_iota(jnp.int32, (7 * 8, STATES), 0) % 8 < 7
    blocks = []
    for c in range(2):
        for x in range(NPE - 1):
            block = field[last, c, x * 64 : x * 64 + 56, :]
            blocks.append(jnp.where(owned_z, block, 0.0))
    columns = jnp.concatenate(blocks, axis=0)
    high, low = split(columns)
    both = lax.dot_general(
        high,
        jnp.concatenate([high, low], axis=1),
        (((0,), (0,)), ((), ())),
        preferred_element_type=F32,
    )
    cross = both[:, STATES:]
    gram[...] = both[:, :STATES] + (cross + cross.T)

    piece = STATES // nz
    mine = pl.ds(pl.multiple_of(me[2] * piece, piece), piece)
    index = me[0] * ny + me[1]

    def scatter(j):
        rows = pl.ds(pl.multiple_of(lax.rem(me[2] + j, nz) * piece, piece), piece)
        return pltpu.make_async_remote_copy(
            src_ref=gram.at[rows],
            dst_ref=r_scatter.at[j - 1],
            send_sem=sum_send.at[0],
            recv_sem=sum_recv.at[0],
            device_id=along_z(j),
            device_id_type=MESH,
        )

    def reduce(j):
        return pltpu.make_async_remote_copy(
            src_ref=r_reduce.at[index],
            dst_ref=r_reduce.at[index],
            send_sem=sum_send.at[1],
            recv_sem=sum_recv.at[1],
            device_id=in_plane(j),
            device_id_type=MESH,
        )

    def gather(j):
        return pltpu.make_async_remote_copy(
            src_ref=r_gather.at[mine],
            dst_ref=r_gather.at[mine],
            send_sem=sum_send.at[2],
            recv_sem=sum_recv.at[2],
            device_id=along_z(j),
            device_id_type=MESH,
        )

    def waiter(ref, k):
        return pltpu.make_async_remote_copy(
            src_ref=ref,
            dst_ref=ref,
            send_sem=sum_send.at[k],
            recv_sem=sum_recv.at[k],
            device_id=along_z(1),
            device_id_type=MESH,
        )

    for j in range(1, nz):
        scatter(j).start()
    waiter(r_scatter, 0).wait_recv()
    r_reduce[index] = gram[mine, :] + jnp.sum(r_scatter[...], axis=0)
    for j in range(1, plane):
        reduce(j).start()
    waiter(r_scatter, 0).wait_send()
    waiter(r_reduce.at[pl.ds(0, plane - 1)], 1).wait_recv()
    nodes = 686 * nx * ny * nz
    r_gather[mine, :] = jnp.sum(r_reduce[...], axis=0) * (1.0 / nodes)
    for j in range(1, nz):
        gather(j).start()
    waiter(r_reduce.at[pl.ds(0, plane - 1)], 1).wait_send()
    rest = r_gather.at[pl.ds(0, piece * (nz - 1))]
    waiter(rest, 2).wait_recv()

    total = r_gather[...]
    diagonal = lax.broadcasted_iota(jnp.int32, (STATES, STATES), 0) == (
        lax.broadcasted_iota(jnp.int32, (STATES, STATES), 1)
    )
    trace = jnp.sum(jnp.where(diagonal, total, 0.0), keepdims=True)
    three = jnp.where(diagonal, 3.0, 0.0)

    def newton(k, pair):
        root, inverse = pair
        middle = three - product(inverse, root)
        return 0.5 * product(root, middle), 0.5 * product(middle, inverse)

    _, inverse = lax.fori_loop(
        0, NS_STEPS, newton, (total / trace, jnp.where(diagonal, 1.0, 0.0))
    )
    rotation = inverse / jnp.sqrt(trace)
    for c in range(2):
        for x in range(NPE - 1):
            turned = product(field[last, c, x * 64 : x * 64 + 56, :], rotation)
            for y in range(NPE - 1):
                out_ref[x, y, c * 7 : c * 7 + 7, :] = turned[y * 8 : y * 8 + 7, :]
    waiter(rest, 2).wait_send()


def shards(wavefunctions, hamiltonians, cell_order):
    sizes = tuple(lax.axis_size(a) for a in AXES)
    plane = sizes[0] * sizes[1]
    piece = STATES // sizes[2]
    matrices = hamiltonians.reshape((2, CDOF, CDOF))
    orders = cell_order.reshape((2, CDOF))
    kinds = len(KINDS)
    return pl.pallas_call(
        functools.partial(kernel, sizes),
        out_shape=jax.ShapeDtypeStruct(wavefunctions.shape, F32),
        in_specs=[pl.BlockSpec(memory_space=pltpu.HBM)] * 3,
        out_specs=pl.BlockSpec(memory_space=pltpu.VMEM),
        scratch_shapes=[
            pltpu.VMEM(wavefunctions.shape, F32),
            pltpu.VMEM((2, CDOF, CDOF), F32),
            pltpu.VMEM((2, CDOF), jnp.int32),
            pltpu.VMEM((2, 2 * SENT, CDOF), BF16),
            pltpu.VMEM((2, 2 * INNER, CDOF), BF16),
            pltpu.VMEM((2, 2, CDOF, STATES), F32),
            pltpu.VMEM((2, SENT, STATES), F32),
            pltpu.VMEM((2, INNER, STATES), F32),
            pltpu.VMEM((2, 2, 8, STATES), F32),
            pltpu.VMEM((2, 2, 2, 64, STATES), F32),
            pltpu.VMEM((2, 2, 2, 64, STATES), F32),
            pltpu.VMEM((2, 2, 64, STATES), F32),
            pltpu.VMEM((2, 4, 2, 8, STATES), F32),
            pltpu.VMEM((2, 4, 8, STATES), F32),
            pltpu.VMEM((2, 4, 8, STATES), F32),
            pltpu.VMEM((2, 8, STATES), F32),
            pltpu.VMEM((STATES, STATES), F32),
            pltpu.VMEM((sizes[2] - 1, piece, STATES), F32),
            pltpu.VMEM((plane, piece, STATES), F32),
            pltpu.VMEM((STATES, STATES), F32),
            pltpu.SemaphoreType.DMA((4,)),
            pltpu.SemaphoreType.DMA((kinds,)),
            pltpu.SemaphoreType.DMA((2, kinds)),
            pltpu.SemaphoreType.DMA((3,)),
            pltpu.SemaphoreType.DMA((3,)),
        ],
        compiler_params=pltpu.CompilerParams(
            collective_id=0, has_side_effects=True, vmem_limit_bytes=56 << 20
        ),
    )(wavefunctions, matrices, orders)


def solution(mesh):
    in_specs = (
        P("gx", "gy", "gz", None),
        P("gx", "gy", "gz", None, None),
        P("gx", "gy", "gz", None),
    )
    out_specs = P("gx", "gy", "gz", None)
    return jax.shard_map(
        shards, mesh=mesh, in_specs=in_specs, out_specs=out_specs, check_vma=False
    )
```

```python
import functools
import itertools

import jax
import jax.numpy as jnp
from jax import lax
from jax.experimental import pallas as pl
from jax.experimental.pallas import tpu as pltpu
from jax.sharding import PartitionSpec as P

NPE = 8
CDOF = 512
STATES = 128
DEGREE = 6
NS_STEPS = 12
CENTER = 0.4
HALF_WIDTH = 0.7
AXES = ("gx", "gy", "gz")
MESH = pl.DeviceIdType.MESH
F32 = jnp.float32
BF16 = jnp.bfloat16

ALL = sorted(
    (d for d in itertools.product((-1, 0, 1), repeat=3) if any(d)),
    key=lambda d: -sum(map(abs, d)),
)
DOWN = [d for d in itertools.product((-1, 0), repeat=3) if any(d)]
UP = [d for d in itertools.product((1, 0), repeat=3) if any(d)]

KINDS = ("x", "z", "xz", "y", "xy", "yz", "xyz")
Z_ROWS, E_ROWS, Y_ROWS, X_ROWS = 0, 64, 0, 128
FIRST, SECOND = 96, 256
INNER = 36 * 8


def split(value):
    high = value.astype(BF16)
    low = (value - high.astype(F32)).astype(BF16)
    return high, low


def product(left, right):
    columns = right.shape[1]
    high, low = split(right)
    upper = jnp.concatenate([high, low], axis=1)
    lower = jnp.concatenate([high, jnp.zeros_like(low)], axis=1)
    sums = jnp.dot(
        jnp.concatenate(split(left), axis=1),
        jnp.concatenate([upper, lower], axis=0),
        preferred_element_type=F32,
    )
    return sums[:, :columns] + sums[:, columns:]


def side(step):
    return (step + 1) // 2


def kind_of(d):
    return "".join(name for name, step in zip("xyz", d) if step)


def kernel(
    sizes,
    wave_hbm,
    ham_hbm,
    order_hbm,
    out_ref,
    wave_ref,
    ham_raw,
    order_ref,
    ham_second,
    ham_inner,
    field,
    rims,
    faces,
    inner,
    yz_pack,
    r_x,
    r_y,
    r_z,
    r_xy,
    r_xz,
    r_yz,
    r_xyz,
    gram,
    r_scatter,
    r_reduce,
    r_gather,
    load_sem,
    send_sem,
    recv_sem,
    sum_send,
    sum_recv,
):
    me = tuple(lax.axis_index(a) for a in AXES)
    nx, ny, nz = sizes
    received = dict(x=r_x, y=r_y, z=r_z, xy=r_xy, xz=r_xz, yz=r_yz, xyz=r_xyz)

    shifted = [
        {s: lax.rem(m + (s + n), n) for s in (-1, 0, 1)} for m, n in zip(me, sizes)
    ]
    neighbours = {
        d: tuple(table[s] for table, s in zip(shifted, d)) for d in ALL
    }

    def neighbour(d):
        return neighbours[d]

    ring_place = me[0] * 2 + lax.rem(me[1], 2)
    other_place = (me[1] // 2) * nz + me[2]
    ring, others = nx * 2, (ny // 2) * nz

    def in_ring(j):
        place = lax.rem(ring_place + j, ring)
        return (place // 2, (me[1] // 2) * 2 + lax.rem(place, 2), me[2])

    def across(j):
        place = lax.rem(other_place + j, others)
        return (me[0], (place // nz) * 2 + lax.rem(me[1], 2), lax.rem(place, nz))

    barrier = pltpu.get_barrier_semaphore()
    for d in UP + DOWN:
        pl.semaphore_signal(barrier, inc=1, device_id=neighbour(d), device_id_type=MESH)

    loads = [
        pltpu.make_async_copy(wave_hbm, wave_ref, load_sem.at[0]),
        pltpu.make_async_copy(order_hbm, order_ref, load_sem.at[1]),
        pltpu.make_async_copy(ham_hbm.at[0], ham_raw.at[0], load_sem.at[2]),
        pltpu.make_async_copy(ham_hbm.at[1], ham_raw.at[1], load_sem.at[3]),
    ]
    for load in loads:
        load.start()

    def message(d, slot):
        dx, dy, dz = d
        kind = kind_of(d)
        sx, sy, sz = side(dx), side(dy), side(dz)
        if kind == "x":
            source, place = faces.at[:, pl.ds(X_ROWS + sx * 64, 64)], sx
        elif kind == "y":
            source, place = faces.at[:, pl.ds(Y_ROWS + sy * 64, 64)], sy
        elif kind == "z":
            source, place = rims.at[sz, pl.ds(Z_ROWS, 64)], sz
        elif kind == "xy":
            place = sx * 2 + sy
            source = rims.at[:, pl.ds(E_ROWS + place * 8, 8)]
        elif kind == "xz":
            source = rims.at[sz, pl.ds(Z_ROWS + sx * 56, 8)]
            place = sx * 2 + sz
        elif kind == "yz":
            source, place = yz_pack.at[sy, sz], sy * 2 + sz
        else:
            source = rims.at[sz, pl.ds(Z_ROWS + sx * 56 + sy * 7, 1)]
            place = sx * 4 + sy * 2 + sz
        if kind == "xyz":
            target = r_xyz.at[slot, pl.ds(place, 1)]
        else:
            target = received[kind].at[slot, place]
        k = KINDS.index(kind)
        return pltpu.make_async_remote_copy(
            src_ref=source,
            dst_ref=target,
            send_sem=send_sem.at[k],
            recv_sem=recv_sem.at[slot, k],
            device_id=neighbour(d),
            device_id_type=MESH,
        )

    def send(directions, slot):
        for d in directions:
            message(d, slot).start()

    def every(kind, directions, slot):
        count = sum(kind_of(d) == kind for d in directions)
        whole = received[kind].at[slot, pl.ds(0, count)]
        k = KINDS.index(kind)
        return pltpu.make_async_remote_copy(
            src_ref=whole,
            dst_ref=whole,
            send_sem=send_sem.at[k],
            recv_sem=recv_sem.at[slot, k],
            device_id=neighbour((1, 0, 0)),
            device_id_type=MESH,
        )

    def wait_sent(directions, slot):
        for kind in KINDS:
            every(kind, directions, slot).wait_send()

    def collect(total, directions, slot, scale):
        for kind in KINDS:
            every(kind, directions, slot).wait_recv()
            for dx, dy, dz in directions:
                if kind_of((dx, dy, dz)) != kind:
                    continue
                sx, sy, sz = side(dx), side(dy), side(dz)
                ix, iy = 7 * (1 - sx), 7 * (1 - sy)
                c, iz = (0, 0) if dz > 0 else (1, 7)
                if kind == "x":
                    total[:, ix * 64 : ix * 64 + 64, :] += scale * r_x[slot, sx]
                elif kind == "y":
                    for x in range(NPE):
                        row = (x * NPE + iy) * NPE
                        total[:, row : row + 8, :] += (
                            scale * r_y[slot, sy, :, x * 8 : x * 8 + 8, :]
                        )
                elif kind == "xy":
                    row = (ix * NPE + iy) * NPE
                    total[:, row : row + 8, :] += scale * r_xy[slot, sx * 2 + sy]
                elif kind == "z":
                    total[c, pl.ds(iz, 64, stride=8), :] += scale * r_z[slot, sz]
                elif kind == "xz":
                    rows = pl.ds(ix * 64 + iz, 8, stride=8)
                    total[c, rows, :] += scale * r_xz[slot, sx * 2 + sz]
                elif kind == "yz":
                    rows = pl.ds(iy * 8 + iz, 8, stride=64)
                    total[c, rows, :] += scale * r_yz[slot, sy * 2 + sz]
                else:
                    row = (ix * NPE + iy) * NPE + iz
                    place = sx * 4 + sy * 2 + sz
                    total[c, row : row + 1, :] += scale * r_xyz[slot, place : place + 1, :]

    def pack_yz():
        for s in range(2):
            for t in range(2):
                yz_pack[t, s] = rims[s, pl.ds(Z_ROWS + 7 * t, 8, stride=8), :]

    loads[0].wait()
    field[0] = jnp.zeros((2, CDOF, STATES), F32)
    for x in range(NPE - 1):
        for y in range(NPE - 1):
            row = (x * NPE + y) * NPE
            field[0, 0, row : row + 8, :] = wave_ref[x, y, 0:8, :]
            field[0, 1, row : row + 7, :] = wave_ref[x, y, 7:14, :]
    rims[0, Z_ROWS : Z_ROWS + 64, :] = field[0, 0, pl.ds(0, 64, stride=8), :]
    for c in range(2):
        rims[c, E_ROWS : E_ROWS + 8, :] = field[0, c, 0:8, :]
        faces[c, X_ROWS : X_ROWS + 64, :] = field[0, c, 0:64, :]
        for x in range(NPE):
            faces[c, Y_ROWS + x * 8 : Y_ROWS + x * 8 + 8, :] = field[0, c, x * 64 : x * 64 + 8, :]
    yz_pack[0, 0] = rims[0, pl.ds(Z_ROWS, 8, stride=8), :]
    pl.semaphore_wait(barrier, len(UP + DOWN))
    send(DOWN, 0)

    loads[1].wait()
    row_of = lax.broadcasted_iota(jnp.int32, (CDOF, CDOF), 0)
    n = lax.broadcasted_iota(jnp.int32, (64, CDOF), 0)
    for c in range(2):
        order = order_ref[c : c + 1, :]

        def chosen(rows):
            return (rows == order).astype(F32).astype(BF16)

        block = (n // 8) * 64 + lax.rem(n, 8)
        edges = [row_of[first : first + 8] for first in (0, 56, 448, 504)]
        rows = [n * 8 + 7 * c] + edges + [block, block + 56, n, n + 448]
        rows += [row_of[x * 64 + 8 : x * 64 + 56] for x in range(1, NPE - 1)]
        pick = chosen(jnp.concatenate(rows, axis=0))
        columns = chosen(row_of)
        loads[2 + c].wait()
        for part, value in enumerate(split(ham_raw[c])):
            half = jnp.dot(pick, value, preferred_element_type=F32).astype(BF16)
            whole = lax.dot_general(
                half, columns, (((1,), (1,)), ((), ())), preferred_element_type=F32
            ).astype(BF16)
            first = 0
            for ref, count in ((ham_second, FIRST + SECOND), (ham_inner, INNER)):
                ref[c, part * count : (part + 1) * count, :] = whole[first : first + count]
                first += count

    collect(field.at[0], DOWN, 0, 1.0)
    wait_sent(DOWN, 0)

    def four(matrix, value):
        rows = matrix.shape[0] // 2
        all_four = jnp.dot(matrix, value, preferred_element_type=F32)
        return (
            all_four[:rows, :STATES]
            + (all_four[:rows, STATES:] + all_four[rows:, :STATES])
            + all_four[rows:, STATES:]
        )

    def join(ref, first, count):
        upper, lower = pl.ds(first + 7, count, stride=8), pl.ds(first, count, stride=8)
        middle = ref[0, upper, :] + ref[1, lower, :]
        ref[0, upper, :] = middle
        ref[1, lower, :] = middle

    def apply(now, directions, factor, keep):
        later = slot = 1 - now
        gain, shift = factor / HALF_WIDTH, -factor * CENTER / HALF_WIDTH
        values = [jnp.concatenate(split(field[now, c]), axis=1) for c in range(2)]
        small = [d for d in directions if kind_of(d) not in ("x", "y")]
        large = [d for d in directions if kind_of(d) in ("x", "y")]
        for c in range(2):
            products = four(ham_second[c], values[c])
            rims[c, :FIRST, :] = products[:FIRST]
            faces[c] = products[FIRST:]
        join(rims, E_ROWS, 4)
        pack_yz()
        join(faces, 0, 32)
        send(small + large, slot)
        for c in range(2):
            inner[c, :INNER, :] = four(ham_inner[c], values[c])
        join(inner, 0, 36)

        def advance(c, row, count, products):
            rows = slice(row, row + count)
            fresh = gain * products + shift * field[now, c, rows, :]
            if keep:
                fresh = fresh - field[later, c, rows, :]
            field[later, c, rows, :] = fresh

        for c in range(2):
            for x in range(NPE):
                if x in (0, NPE - 1):
                    first = X_ROWS + 64 * (x // 7)
                    advance(c, x * 64, 64, faces[c, first : first + 64, :])
                    continue
                for t in range(2):
                    first = Y_ROWS + 64 * t + x * 8
                    advance(c, x * 64 + 56 * t, 8, faces[c, first : first + 8, :])
                first = (x - 1) * 48
                advance(c, x * 64 + 8, 48, inner[c, first : first + 48, :])
        collect(field.at[later], directions, slot, gain)
        wait_sent(directions, slot)

    apply(0, ALL, 1.0, False)

    def two_steps(k, carry):
        apply(1, ALL, 2.0, True)
        apply(0, ALL, 2.0, True)
        return carry

    lax.fori_loop(0, (DEGREE - 2) // 2, two_steps, 0)
    apply(1, UP, 2.0, True)
    last = 0

    owned_z = lax.broadcasted_iota(jnp.int32, (7 * 8, STATES), 0) % 8 < 7
    blocks = []
    for c in range(2):
        for x in range(NPE - 1):
            block = field[last, c, x * 64 : x * 64 + 56, :]
            blocks.append(jnp.where(owned_z, block, 0.0))
    columns = jnp.concatenate(blocks, axis=0)
    high, low = split(columns)
    both = lax.dot_general(
        high,
        jnp.concatenate([high, low], axis=1),
        (((0,), (0,)), ((), ())),
        preferred_element_type=F32,
    )
    cross = both[:, STATES:]
    gram[...] = both[:, :STATES] + (cross + cross.T)

    piece = STATES // ring
    mine = pl.ds(pl.multiple_of(ring_place * piece, piece), piece)

    def scatter(j):
        rows = pl.ds(pl.multiple_of(lax.rem(ring_place + j, ring) * piece, piece), piece)
        return pltpu.make_async_remote_copy(
            src_ref=gram.at[rows],
            dst_ref=r_scatter.at[j - 1],
            send_sem=sum_send.at[0],
            recv_sem=sum_recv.at[0],
            device_id=in_ring(j),
            device_id_type=MESH,
        )

    def reduce(j):
        return pltpu.make_async_remote_copy(
            src_ref=r_reduce.at[other_place],
            dst_ref=r_reduce.at[other_place],
            send_sem=sum_send.at[1],
            recv_sem=sum_recv.at[1],
            device_id=across(j),
            device_id_type=MESH,
        )

    def gather(j):
        return pltpu.make_async_remote_copy(
            src_ref=r_gather.at[mine],
            dst_ref=r_gather.at[mine],
            send_sem=sum_send.at[2],
            recv_sem=sum_recv.at[2],
            device_id=in_ring(j),
            device_id_type=MESH,
        )

    def waiter(ref, k):
        return pltpu.make_async_remote_copy(
            src_ref=ref,
            dst_ref=ref,
            send_sem=sum_send.at[k],
            recv_sem=sum_recv.at[k],
            device_id=in_ring(1),
            device_id_type=MESH,
        )

    for j in range(1, ring):
        scatter(j).start()
    waiter(r_scatter, 0).wait_recv()
    r_reduce[other_place] = gram[mine, :] + jnp.sum(r_scatter[...], axis=0)
    for j in range(1, others):
        reduce(j).start()
    waiter(r_scatter, 0).wait_send()
    waiter(r_reduce.at[pl.ds(0, others - 1)], 1).wait_recv()
    nodes = 686 * nx * ny * nz
    r_gather[mine, :] = jnp.sum(r_reduce[...], axis=0) * (1.0 / nodes)
    for j in range(1, ring):
        gather(j).start()
    waiter(r_reduce.at[pl.ds(0, others - 1)], 1).wait_send()
    rest = r_gather.at[pl.ds(0, piece * (ring - 1))]
    waiter(rest, 2).wait_recv()

    total = r_gather[...]
    diagonal = lax.broadcasted_iota(jnp.int32, (STATES, STATES), 0) == (
        lax.broadcasted_iota(jnp.int32, (STATES, STATES), 1)
    )
    trace = jnp.sum(jnp.where(diagonal, total, 0.0), keepdims=True)
    three = jnp.where(diagonal, 3.0, 0.0)

    def newton(k, pair):
        root, inverse = pair
        middle = three - product(inverse, root)
        return 0.5 * product(root, middle), 0.5 * product(middle, inverse)

    _, inverse = lax.fori_loop(
        0, NS_STEPS, newton, (total / trace, jnp.where(diagonal, 1.0, 0.0))
    )
    rotation = inverse / jnp.sqrt(trace)
    for c in range(2):
        for x in range(NPE - 1):
            turned = product(field[last, c, x * 64 : x * 64 + 56, :], rotation)
            for y in range(NPE - 1):
                out_ref[x, y, c * 7 : c * 7 + 7, :] = turned[y * 8 : y * 8 + 7, :]
    waiter(rest, 2).wait_send()


def shards(wavefunctions, hamiltonians, cell_order):
    sizes = tuple(lax.axis_size(a) for a in AXES)
    ring, others = sizes[0] * 2, sizes[1] // 2 * sizes[2]
    piece = STATES // ring
    matrices = hamiltonians.reshape((2, CDOF, CDOF))
    orders = cell_order.reshape((2, CDOF))
    kinds = len(KINDS)
    return pl.pallas_call(
        functools.partial(kernel, sizes),
        out_shape=pltpu.VMEM(wavefunctions.shape, F32),
        in_specs=[pl.BlockSpec(memory_space=pltpu.HBM)] * 3,
        out_specs=pl.BlockSpec(memory_space=pltpu.VMEM),
        scratch_shapes=[
            pltpu.VMEM(wavefunctions.shape, F32),
            pltpu.VMEM((2, CDOF, CDOF), F32),
            pltpu.VMEM((2, CDOF), jnp.int32),
            pltpu.VMEM((2, 2 * (FIRST + SECOND), CDOF), BF16),
            pltpu.VMEM((2, 2 * INNER, CDOF), BF16),
            pltpu.VMEM((2, 2, CDOF, STATES), F32),
            pltpu.VMEM((2, FIRST + 40, STATES), F32),
            pltpu.VMEM((2, SECOND, STATES), F32),
            pltpu.VMEM((2, INNER + 32, STATES), F32),
            pltpu.VMEM((2, 2, 8, STATES), F32),
            pltpu.VMEM((2, 2, 2, 64, STATES), F32),
            pltpu.VMEM((2, 2, 2, 64, STATES), F32),
            pltpu.VMEM((2, 2, 64, STATES), F32),
            pltpu.VMEM((2, 4, 2, 8, STATES), F32),
            pltpu.VMEM((2, 4, 8, STATES), F32),
            pltpu.VMEM((2, 4, 8, STATES), F32),
            pltpu.VMEM((2, 8, STATES), F32),
            pltpu.VMEM((STATES, STATES), F32),
            pltpu.VMEM((ring - 1, piece, STATES), F32),
            pltpu.VMEM((others, piece, STATES), F32),
            pltpu.VMEM((STATES, STATES), F32),
            pltpu.SemaphoreType.DMA((4,)),
            pltpu.SemaphoreType.DMA((kinds,)),
            pltpu.SemaphoreType.DMA((2, kinds)),
            pltpu.SemaphoreType.DMA((3,)),
            pltpu.SemaphoreType.DMA((3,)),
        ],
        compiler_params=pltpu.CompilerParams(
            collective_id=0, has_side_effects=True, vmem_limit_bytes=56 << 20
        ),
    )(wavefunctions, matrices, orders)


def solution(mesh):
    in_specs = (
        P("gx", "gy", "gz", None),
        P("gx", "gy", "gz", None, None),
        P("gx", "gy", "gz", None),
    )
    out_specs = P("gx", "gy", "gz", None)
    return jax.shard_map(
        shards, mesh=mesh, in_specs=in_specs, out_specs=out_specs, check_vma=False
    )
```

```python
import functools
import itertools

import jax
import jax.numpy as jnp
from jax import lax
from jax.experimental import pallas as pl
from jax.experimental.pallas import tpu as pltpu
from jax.sharding import PartitionSpec as P

NPE = 8
CDOF = 512
STATES = 128
DEGREE = 6
NS_STEPS = 12
CENTER = 0.4
HALF_WIDTH = 0.7
AXES = ("gx", "gy", "gz")
MESH = pl.DeviceIdType.MESH
F32 = jnp.float32
BF16 = jnp.bfloat16

ALL = sorted(
    (d for d in itertools.product((-1, 0, 1), repeat=3) if any(d)),
    key=lambda d: -sum(map(abs, d)),
)
DOWN = [d for d in itertools.product((-1, 0), repeat=3) if any(d)]
UP = [d for d in itertools.product((1, 0), repeat=3) if any(d)]

KINDS = ("x", "z", "xz", "y", "xy", "yz", "xyz")
Z_ROWS, E_ROWS, Y_ROWS, X_ROWS = 0, 64, 0, 128
FIRST, SECOND = 96, 256
INNER = 36 * 8
SENT = FIRST + SECOND
ROWS = SENT + INNER
EARLY, LATE = 384, 256


def split(value):
    high = value.astype(BF16)
    low = (value - high.astype(F32)).astype(BF16)
    return high, low


def product(left, right):
    columns = right.shape[1]
    high, low = split(right)
    upper = jnp.concatenate([high, low], axis=1)
    lower = jnp.concatenate([high, jnp.zeros_like(low)], axis=1)
    sums = jnp.dot(
        jnp.concatenate(split(left), axis=1),
        jnp.concatenate([upper, lower], axis=0),
        preferred_element_type=F32,
    )
    return sums[:, :columns] + sums[:, columns:]


def side(step):
    return (step + 1) // 2


def kind_of(d):
    return "".join(name for name, step in zip("xyz", d) if step)


def kernel(
    sizes,
    wave_hbm,
    ham_hbm,
    order_hbm,
    out_ref,
    wave_ref,
    ham_raw,
    order_ref,
    ham_early,
    ham_sent,
    ham_inner,
    early,
    field,
    rims,
    faces,
    inner,
    yz_pack,
    r_x,
    r_y,
    r_z,
    r_xy,
    r_xz,
    r_yz,
    r_xyz,
    gram,
    r_scatter,
    r_reduce,
    r_gather,
    load_sem,
    send_sem,
    recv_sem,
    sum_send,
    sum_recv,
):
    me = tuple(lax.axis_index(a) for a in AXES)
    nx, ny, nz = sizes
    received = dict(x=r_x, y=r_y, z=r_z, xy=r_xy, xz=r_xz, yz=r_yz, xyz=r_xyz)

    shifted = [
        {s: lax.rem(m + (s + n), n) for s in (-1, 0, 1)} for m, n in zip(me, sizes)
    ]
    neighbours = {
        d: tuple(table[s] for table, s in zip(shifted, d)) for d in ALL
    }

    def neighbour(d):
        return neighbours[d]

    ring_place = me[0] * 2 + lax.rem(me[1], 2)
    other_place = (me[1] // 2) * nz + me[2]
    ring, others = nx * 2, (ny // 2) * nz

    def in_ring(j):
        place = lax.rem(ring_place + j, ring)
        return (place // 2, (me[1] // 2) * 2 + lax.rem(place, 2), me[2])

    def across(j):
        place = lax.rem(other_place + j, others)
        return (me[0], (place // nz) * 2 + lax.rem(me[1], 2), lax.rem(place, nz))

    barrier = pltpu.get_barrier_semaphore()
    for d in UP + DOWN:
        pl.semaphore_signal(barrier, inc=1, device_id=neighbour(d), device_id_type=MESH)

    loads = [
        pltpu.make_async_copy(wave_hbm, wave_ref, load_sem.at[0]),
        pltpu.make_async_copy(order_hbm, order_ref, load_sem.at[1]),
        pltpu.make_async_copy(ham_hbm.at[0], ham_raw.at[0], load_sem.at[2]),
        pltpu.make_async_copy(ham_hbm.at[1], ham_raw.at[1], load_sem.at[3]),
    ]
    for load in loads:
        load.start()

    def message(d, slot):
        dx, dy, dz = d
        kind = kind_of(d)
        sx, sy, sz = side(dx), side(dy), side(dz)
        if kind == "x":
            source, place = faces.at[:, pl.ds(X_ROWS + sx * 64, 64)], sx
        elif kind == "y":
            source, place = faces.at[:, pl.ds(Y_ROWS + sy * 64, 64)], sy
        elif kind == "z":
            source, place = rims.at[sz, pl.ds(Z_ROWS, 64)], sz
        elif kind == "xy":
            place = sx * 2 + sy
            source = rims.at[:, pl.ds(E_ROWS + place * 8, 8)]
        elif kind == "xz":
            source = rims.at[sz, pl.ds(Z_ROWS + sx * 56, 8)]
            place = sx * 2 + sz
        elif kind == "yz":
            source, place = yz_pack.at[sy, sz], sy * 2 + sz
        else:
            source = rims.at[sz, pl.ds(Z_ROWS + sx * 56 + sy * 7, 1)]
            place = sx * 4 + sy * 2 + sz
        if kind == "xyz":
            target = r_xyz.at[slot, pl.ds(place, 1)]
        else:
            target = received[kind].at[slot, place]
        k = KINDS.index(kind)
        return pltpu.make_async_remote_copy(
            src_ref=source,
            dst_ref=target,
            send_sem=send_sem.at[k],
            recv_sem=recv_sem.at[slot, place if kind == "y" else 2 + k],
            device_id=neighbour(d),
            device_id_type=MESH,
        )

    def send(directions, slot):
        for d in directions:
            message(d, slot).start()

    def every(kind, directions, slot):
        count = sum(kind_of(d) == kind for d in directions)
        whole = received[kind].at[slot, pl.ds(0, count)]
        k = KINDS.index(kind)
        return pltpu.make_async_remote_copy(
            src_ref=whole,
            dst_ref=whole,
            send_sem=send_sem.at[k],
            recv_sem=recv_sem.at[slot, 2 + k],
            device_id=neighbour((1, 0, 0)),
            device_id_type=MESH,
        )

    def wait_sent(directions, slot):
        for kind in KINDS:
            every(kind, directions, slot).wait_send()

    def collect_y(total, slot, place, scale):
        pltpu.make_async_remote_copy(
            src_ref=r_y.at[slot, place],
            dst_ref=r_y.at[slot, place],
            send_sem=send_sem.at[KINDS.index("y")],
            recv_sem=recv_sem.at[slot, place],
            device_id=neighbour((1, 0, 0)),
            device_id_type=MESH,
        ).wait_recv()
        for x in range(NPE):
            rows = pl.ds(pl.multiple_of(x * 64 + 56 * (1 - place), 8), 8)
            total[:, rows, :] += scale * r_y[slot, place, :, x * 8 : x * 8 + 8, :]

    def collect(total, directions, slot, scale):
        for kind in KINDS:
            if kind == "y":
                for d in directions:
                    if kind_of(d) == "y":
                        collect_y(total, slot, side(d[1]), scale)
                continue
            every(kind, directions, slot).wait_recv()
            for dx, dy, dz in directions:
                if kind_of((dx, dy, dz)) != kind:
                    continue
                sx, sy, sz = side(dx), side(dy), side(dz)
                ix, iy = 7 * (1 - sx), 7 * (1 - sy)
                c, iz = (0, 0) if dz > 0 else (1, 7)
                if kind == "x":
                    total[:, ix * 64 : ix * 64 + 64, :] += scale * r_x[slot, sx]
                elif kind == "xy":
                    row = (ix * NPE + iy) * NPE
                    total[:, row : row + 8, :] += scale * r_xy[slot, sx * 2 + sy]
                elif kind == "z":
                    total[c, pl.ds(iz, 64, stride=8), :] += scale * r_z[slot, sz]
                elif kind == "xz":
                    rows = pl.ds(ix * 64 + iz, 8, stride=8)
                    total[c, rows, :] += scale * r_xz[slot, sx * 2 + sz]
                elif kind == "yz":
                    rows = pl.ds(iy * 8 + iz, 8, stride=64)
                    total[c, rows, :] += scale * r_yz[slot, sy * 2 + sz]
                else:
                    row = (ix * NPE + iy) * NPE + iz
                    place = sx * 4 + sy * 2 + sz
                    total[c, row : row + 1, :] += scale * r_xyz[slot, place : place + 1, :]

    def pack_yz():
        for s in range(2):
            for t in range(2):
                yz_pack[t, s] = rims[s, pl.ds(Z_ROWS + 7 * t, 8, stride=8), :]

    loads[0].wait()
    field[0] = jnp.zeros((2, CDOF, STATES), F32)
    for x in range(NPE - 1):
        for y in range(NPE - 1):
            row = (x * NPE + y) * NPE
            field[0, 0, row : row + 8, :] = wave_ref[x, y, 0:8, :]
            field[0, 1, row : row + 7, :] = wave_ref[x, y, 7:14, :]
    rims[0, Z_ROWS : Z_ROWS + 64, :] = field[0, 0, pl.ds(0, 64, stride=8), :]
    for c in range(2):
        rims[c, E_ROWS : E_ROWS + 8, :] = field[0, c, 0:8, :]
        faces[c, X_ROWS : X_ROWS + 64, :] = field[0, c, 0:64, :]
        for x in range(NPE):
            faces[c, Y_ROWS + x * 8 : Y_ROWS + x * 8 + 8, :] = field[0, c, x * 64 : x * 64 + 8, :]
    yz_pack[0, 0] = rims[0, pl.ds(Z_ROWS, 8, stride=8), :]
    pl.semaphore_wait(barrier, len(UP + DOWN))
    send(DOWN, 0)

    loads[1].wait()
    near_place = lax.rem(me[1], 2)
    near_y = 7 * (1 - near_place)
    row_of = lax.broadcasted_iota(jnp.int32, (CDOF, CDOF), 0)
    n = lax.broadcasted_iota(jnp.int32, (64, CDOF), 0)
    for c in range(2):
        order = order_ref[c : c + 1, :]

        def chosen(rows):
            return (rows == order).astype(F32).astype(BF16)

        block = (n // 8) * 64 + lax.rem(n, 8)
        edges = [row_of[first : first + 8] for first in (0, 56, 448, 504)]
        rows = [n * 8 + 7 * c] + edges + [block, block + 56, n, n + 448]
        rows += [row_of[x * 64 + 8 : x * 64 + 56] for x in range(1, NPE - 1)]
        pick = chosen(jnp.concatenate(rows, axis=0))
        k = lax.broadcasted_iota(jnp.int32, (48, CDOF), 0)
        none = jnp.full((48, CDOF), -1, jnp.int32)
        near_rows = (k // 8 + 1) * 64 + near_y * 8 + lax.rem(k, 8)
        early_rows = [row_of[x * 64 + 8 : x * 64 + 56] for x in range(1, NPE - 1)]
        early_rows = [
            jnp.where(lax.rem(k, 8) == 7 * c, -1, rows) for rows in early_rows + [near_rows]
        ] + [none]
        rim_rows = (k // 8 + 1) * 64 + lax.rem(k, 8) * 8 + 7 * c
        late_rows = [
            n,
            n + 448,
            (k // 8 + 1) * 64 + (7 - near_y) * 8 + lax.rem(k, 8),
            jnp.where(lax.rem(k, 8) == 7 - near_y, -1, rim_rows),
            none[:32],
        ]
        early_columns = chosen(jnp.concatenate(early_rows, axis=0))
        late_columns = chosen(jnp.concatenate(late_rows, axis=0))
        loads[2 + c].wait()
        for part, value in enumerate(split(ham_raw[c])):
            half = jnp.dot(pick, value, preferred_element_type=F32).astype(BF16)
            whole = lax.dot_general(
                half, early_columns, (((1,), (1,)), ((), ())), preferred_element_type=F32
            ).astype(BF16)
            ham_early[c, part * ROWS : (part + 1) * ROWS, :] = whole
            whole = lax.dot_general(
                half, late_columns, (((1,), (1,)), ((), ())), preferred_element_type=F32
            ).astype(BF16)
            ham_sent[c, part * SENT : (part + 1) * SENT, :] = whole[:SENT]
            ham_inner[c, part * INNER : (part + 1) * INNER, :] = whole[SENT:]

    collect(field.at[0], DOWN, 0, 1.0)
    wait_sent(DOWN, 0)

    def four(matrix, value):
        rows = matrix.shape[0] // 2
        all_four = jnp.dot(matrix, value, preferred_element_type=F32)
        return (
            all_four[:rows, :STATES]
            + (all_four[:rows, STATES:] + all_four[rows:, :STATES])
            + all_four[rows:, STATES:]
        )

    def join(ref, first, count):
        upper, lower = pl.ds(first + 7, count, stride=8), pl.ds(first, count, stride=8)
        middle = ref[0, upper, :] + ref[1, lower, :]
        ref[0, upper, :] = middle
        ref[1, lower, :] = middle

    def pair(parts):
        return jnp.concatenate(split(jnp.concatenate(parts, axis=0)), axis=1)

    def y_rows(now, c, y):
        return [
            field[now, c, pl.ds(pl.multiple_of(x * 64 + y * 8, 8), 8), :]
            for x in range(1, NPE - 1)
        ]

    def multiply_early(now):
        for c in range(2):
            parts = [field[now, c, x * 64 + 8 : x * 64 + 56, :] for x in range(1, NPE - 1)]
            parts += y_rows(now, c, near_y) + [jnp.zeros((48, STATES), F32)]
            early[c] = four(ham_early[c], pair(parts))

    def late_values(now, c):
        parts = [field[now, c, 0:64, :], field[now, c, 448:512, :]]
        parts += y_rows(now, c, 7 - near_y)
        parts += [field[now, c, pl.ds(64 + 7 * c, 48, stride=8), :]]
        return pair(parts + [jnp.zeros((32, STATES), F32)])

    def apply(now, directions, factor, keep):
        later = slot = 1 - now
        gain, shift = factor / HALF_WIDTH, -factor * CENTER / HALF_WIDTH
        values = [late_values(now, c) for c in range(2)]
        for c in range(2):
            products = early[c, :SENT, :] + four(ham_sent[c], values[c])
            rims[c, :FIRST, :] = products[:FIRST]
            faces[c] = products[FIRST:]
        join(rims, E_ROWS, 4)
        pack_yz()
        join(faces, 0, 32)
        send(directions, slot)
        for c in range(2):
            inner[c, :INNER, :] = early[c, SENT:, :] + four(ham_inner[c], values[c])
        join(inner, 0, 36)

        def advance(c, row, count, products):
            rows = slice(row, row + count)
            fresh = gain * products + shift * field[now, c, rows, :]
            if keep:
                fresh = fresh - field[later, c, rows, :]
            field[later, c, rows, :] = fresh

        for c in range(2):
            for x in range(NPE):
                if x in (0, NPE - 1):
                    first = X_ROWS + 64 * (x // 7)
                    advance(c, x * 64, 64, faces[c, first : first + 64, :])
                    continue
                for t in range(2):
                    first = Y_ROWS + 64 * t + x * 8
                    advance(c, x * 64 + 56 * t, 8, faces[c, first : first + 8, :])
                first = (x - 1) * 48
                advance(c, x * 64 + 8, 48, inner[c, first : first + 48, :])
        total = field.at[later]
        if directions is ALL:
            collect_y(total, slot, near_place, gain)
            multiply_early(later)
            collect(total, [d for d in ALL if kind_of(d) != "y"], slot, gain)
            collect_y(total, slot, 1 - near_place, gain)
        else:
            collect(total, directions, slot, gain)
        wait_sent(directions, slot)

    multiply_early(0)
    apply(0, ALL, 1.0, False)

    def two_steps(k, carry):
        apply(1, ALL, 2.0, True)
        apply(0, ALL, 2.0, True)
        return carry

    lax.fori_loop(0, (DEGREE - 2) // 2, two_steps, 0)
    apply(1, UP, 2.0, True)
    last = 0

    owned_z = lax.broadcasted_iota(jnp.int32, (7 * 8, STATES), 0) % 8 < 7
    blocks = []
    for c in range(2):
        for x in range(NPE - 1):
            block = field[last, c, x * 64 : x * 64 + 56, :]
            blocks.append(jnp.where(owned_z, block, 0.0))
    columns = jnp.concatenate(blocks, axis=0)
    high, low = split(columns)
    both = lax.dot_general(
        high,
        jnp.concatenate([high, low], axis=1),
        (((0,), (0,)), ((), ())),
        preferred_element_type=F32,
    )
    cross = both[:, STATES:]
    gram[...] = both[:, :STATES] + (cross + cross.T)

    piece = STATES // ring
    mine = pl.ds(pl.multiple_of(ring_place * piece, piece), piece)

    def scatter(j):
        rows = pl.ds(pl.multiple_of(lax.rem(ring_place + j, ring) * piece, piece), piece)
        return pltpu.make_async_remote_copy(
            src_ref=gram.at[rows],
            dst_ref=r_scatter.at[j - 1],
            send_sem=sum_send.at[0],
            recv_sem=sum_recv.at[0],
            device_id=in_ring(j),
            device_id_type=MESH,
        )

    def reduce(j):
        return pltpu.make_async_remote_copy(
            src_ref=r_reduce.at[other_place],
            dst_ref=r_reduce.at[other_place],
            send_sem=sum_send.at[1],
            recv_sem=sum_recv.at[1],
            device_id=across(j),
            device_id_type=MESH,
        )

    def gather(j):
        return pltpu.make_async_remote_copy(
            src_ref=r_gather.at[mine],
            dst_ref=r_gather.at[mine],
            send_sem=sum_send.at[2],
            recv_sem=sum_recv.at[2],
            device_id=in_ring(j),
            device_id_type=MESH,
        )

    def waiter(ref, k):
        return pltpu.make_async_remote_copy(
            src_ref=ref,
            dst_ref=ref,
            send_sem=sum_send.at[k],
            recv_sem=sum_recv.at[k],
            device_id=in_ring(1),
            device_id_type=MESH,
        )

    for j in range(1, ring):
        scatter(j).start()
    waiter(r_scatter, 0).wait_recv()
    r_reduce[other_place] = gram[mine, :] + jnp.sum(r_scatter[...], axis=0)
    for j in range(1, others):
        reduce(j).start()
    waiter(r_scatter, 0).wait_send()
    waiter(r_reduce.at[pl.ds(0, others - 1)], 1).wait_recv()
    nodes = 686 * nx * ny * nz
    r_gather[mine, :] = jnp.sum(r_reduce[...], axis=0) * (1.0 / nodes)
    for j in range(1, ring):
        gather(j).start()
    waiter(r_reduce.at[pl.ds(0, others - 1)], 1).wait_send()
    rest = r_gather.at[pl.ds(0, piece * (ring - 1))]
    waiter(rest, 2).wait_recv()

    total = r_gather[...]
    diagonal = lax.broadcasted_iota(jnp.int32, (STATES, STATES), 0) == (
        lax.broadcasted_iota(jnp.int32, (STATES, STATES), 1)
    )
    trace = jnp.sum(jnp.where(diagonal, total, 0.0), keepdims=True)
    three = jnp.where(diagonal, 3.0, 0.0)

    def newton(k, pair):
        root, inverse = pair
        middle = three - product(inverse, root)
        return 0.5 * product(root, middle), 0.5 * product(middle, inverse)

    scaled = total / trace
    middle = three - scaled
    root, inverse = lax.fori_loop(
        0, NS_STEPS - 2, newton, (0.5 * product(scaled, middle), 0.5 * middle)
    )
    inverse = 0.5 * product(three - product(inverse, root), inverse)
    rotation = inverse / jnp.sqrt(trace)
    for c in range(2):
        for x in range(NPE - 1):
            turned = product(field[last, c, x * 64 : x * 64 + 56, :], rotation)
            for y in range(NPE - 1):
                out_ref[x, y, c * 7 : c * 7 + 7, :] = turned[y * 8 : y * 8 + 7, :]
    waiter(rest, 2).wait_send()


def shards(wavefunctions, hamiltonians, cell_order):
    sizes = tuple(lax.axis_size(a) for a in AXES)
    ring, others = sizes[0] * 2, sizes[1] // 2 * sizes[2]
    piece = STATES // ring
    matrices = hamiltonians.reshape((2, CDOF, CDOF))
    orders = cell_order.reshape((2, CDOF))
    kinds = len(KINDS)
    return pl.pallas_call(
        functools.partial(kernel, sizes),
        out_shape=pltpu.VMEM(wavefunctions.shape, F32),
        in_specs=[pl.BlockSpec(memory_space=pltpu.HBM)] * 3,
        out_specs=pl.BlockSpec(memory_space=pltpu.VMEM),
        scratch_shapes=[
            pltpu.VMEM(wavefunctions.shape, F32),
            pltpu.VMEM((2, CDOF, CDOF), F32),
            pltpu.VMEM((2, CDOF), jnp.int32),
            pltpu.VMEM((2, 2 * ROWS, EARLY), BF16),
            pltpu.VMEM((2, 2 * SENT, LATE), BF16),
            pltpu.VMEM((2, 2 * INNER, LATE), BF16),
            pltpu.VMEM((2, ROWS, STATES), F32),
            pltpu.VMEM((2, 2, CDOF, STATES), F32),
            pltpu.VMEM((2, FIRST + 40, STATES), F32),
            pltpu.VMEM((2, SECOND, STATES), F32),
            pltpu.VMEM((2, INNER + 32, STATES), F32),
            pltpu.VMEM((2, 2, 8, STATES), F32),
            pltpu.VMEM((2, 2, 2, 64, STATES), F32),
            pltpu.VMEM((2, 2, 2, 64, STATES), F32),
            pltpu.VMEM((2, 2, 64, STATES), F32),
            pltpu.VMEM((2, 4, 2, 8, STATES), F32),
            pltpu.VMEM((2, 4, 8, STATES), F32),
            pltpu.VMEM((2, 4, 8, STATES), F32),
            pltpu.VMEM((2, 8, STATES), F32),
            pltpu.VMEM((STATES, STATES), F32),
            pltpu.VMEM((ring - 1, piece, STATES), F32),
            pltpu.VMEM((others, piece, STATES), F32),
            pltpu.VMEM((STATES, STATES), F32),
            pltpu.SemaphoreType.DMA((4,)),
            pltpu.SemaphoreType.DMA((kinds,)),
            pltpu.SemaphoreType.DMA((2, 2 + kinds)),
            pltpu.SemaphoreType.DMA((3,)),
            pltpu.SemaphoreType.DMA((3,)),
        ],
        compiler_params=pltpu.CompilerParams(
            collective_id=0, has_side_effects=True, vmem_limit_bytes=56 << 20
        ),
    )(wavefunctions, matrices, orders)


def solution(mesh):
    in_specs = (
        P("gx", "gy", "gz", None),
        P("gx", "gy", "gz", None, None),
        P("gx", "gy", "gz", None),
    )
    out_specs = P("gx", "gy", "gz", None)
    return jax.shard_map(
        shards, mesh=mesh, in_specs=in_specs, out_specs=out_specs, check_vma=False
    )
```

```python
import functools
import itertools

import jax
import jax.numpy as jnp
from jax import lax
from jax.experimental import pallas as pl
from jax.experimental.pallas import tpu as pltpu
from jax.sharding import PartitionSpec as P

NPE = 8
CDOF = 512
STATES = 128
DEGREE = 6
NS_STEPS = 12
CENTER = 0.4
HALF_WIDTH = 0.7
AXES = ("gx", "gy", "gz")
MESH = pl.DeviceIdType.MESH
F32 = jnp.float32
BF16 = jnp.bfloat16

ALL = sorted(
    (d for d in itertools.product((-1, 0, 1), repeat=3) if any(d)),
    key=lambda d: -sum(map(abs, d)),
)
DOWN = [d for d in itertools.product((-1, 0), repeat=3) if any(d)]
UP = [d for d in itertools.product((1, 0), repeat=3) if any(d)]

KINDS = ("x", "z", "xz", "y", "xy", "yz", "xyz")
Z_ROWS, E_ROWS, Y_ROWS, X_ROWS = 0, 64, 0, 128
FIRST, SECOND = 96, 256
INNER = 36 * 8
SENT = FIRST + SECOND
ROWS = SENT + INNER
EARLY, LATE = 384, 256


def split(value):
    high = value.astype(BF16)
    low = (value - high.astype(F32)).astype(BF16)
    return high, low


def product(left, right):
    columns = right.shape[1]
    high, low = split(right)
    upper = jnp.concatenate([high, low], axis=1)
    lower = jnp.concatenate([high, jnp.zeros_like(low)], axis=1)
    sums = jnp.dot(
        jnp.concatenate(split(left), axis=1),
        jnp.concatenate([upper, lower], axis=0),
        preferred_element_type=F32,
    )
    return sums[:, :columns] + sums[:, columns:]


def side(step):
    return (step + 1) // 2


def kind_of(d):
    return "".join(name for name, step in zip("xyz", d) if step)


def kernel(
    sizes,
    wave_hbm,
    ham_hbm,
    order_hbm,
    out_ref,
    wave_ref,
    ham_raw,
    order_ref,
    ham_early,
    ham_sent,
    ham_inner,
    early,
    field,
    rims,
    faces,
    inner,
    yz_pack,
    r_x,
    r_y,
    r_z,
    r_xy,
    r_xz,
    r_yz,
    r_xyz,
    gram,
    r_scatter,
    r_reduce,
    r_gather,
    load_sem,
    send_sem,
    recv_sem,
    sum_send,
    sum_recv,
):
    me = tuple(lax.axis_index(a) for a in AXES)
    nx, ny, nz = sizes
    received = dict(x=r_x, y=r_y, z=r_z, xy=r_xy, xz=r_xz, yz=r_yz, xyz=r_xyz)

    shifted = [
        {s: lax.rem(m + (s + n), n) for s in (-1, 0, 1)} for m, n in zip(me, sizes)
    ]
    neighbours = {
        d: tuple(table[s] for table, s in zip(shifted, d)) for d in ALL
    }

    def neighbour(d):
        return neighbours[d]

    ring_place = me[0] * 2 + lax.rem(me[1], 2)
    other_place = (me[1] // 2) * nz + me[2]
    ring, others = nx * 2, (ny // 2) * nz

    def in_ring(j):
        place = lax.rem(ring_place + j, ring)
        return (place // 2, (me[1] // 2) * 2 + lax.rem(place, 2), me[2])

    def across(j):
        place = lax.rem(other_place + j, others)
        return (me[0], (place // nz) * 2 + lax.rem(me[1], 2), lax.rem(place, nz))

    barrier = pltpu.get_barrier_semaphore()
    for d in UP + DOWN:
        pl.semaphore_signal(barrier, inc=1, device_id=neighbour(d), device_id_type=MESH)

    loads = [
        pltpu.make_async_copy(wave_hbm, wave_ref, load_sem.at[0]),
        pltpu.make_async_copy(order_hbm, order_ref, load_sem.at[1]),
        pltpu.make_async_copy(ham_hbm.at[0], ham_raw.at[0], load_sem.at[2]),
        pltpu.make_async_copy(ham_hbm.at[1], ham_raw.at[1], load_sem.at[3]),
    ]
    for load in loads:
        load.start()

    def message(d, slot):
        dx, dy, dz = d
        kind = kind_of(d)
        sx, sy, sz = side(dx), side(dy), side(dz)
        if kind == "x":
            source, place = faces.at[:, pl.ds(X_ROWS + sx * 64, 64)], sx
        elif kind == "y":
            source, place = faces.at[:, pl.ds(Y_ROWS + sy * 64, 64)], sy
        elif kind == "z":
            source, place = rims.at[sz, pl.ds(Z_ROWS, 64)], sz
        elif kind == "xy":
            place = sx * 2 + sy
            source = rims.at[:, pl.ds(E_ROWS + place * 8, 8)]
        elif kind == "xz":
            source = rims.at[sz, pl.ds(Z_ROWS + sx * 56, 8)]
            place = sx * 2 + sz
        elif kind == "yz":
            source, place = yz_pack.at[sy, sz], sy * 2 + sz
        else:
            source = rims.at[sz, pl.ds(Z_ROWS + sx * 56 + sy * 7, 1)]
            place = sx * 4 + sy * 2 + sz
        if kind == "xyz":
            target = r_xyz.at[slot, pl.ds(place, 1)]
        else:
            target = received[kind].at[slot, place]
        k = KINDS.index(kind)
        return pltpu.make_async_remote_copy(
            src_ref=source,
            dst_ref=target,
            send_sem=send_sem.at[k],
            recv_sem=recv_sem.at[slot, place if kind == "y" else 2 + k],
            device_id=neighbour(d),
            device_id_type=MESH,
        )

    def send(directions, slot):
        for d in directions:
            message(d, slot).start()

    def every(kind, directions, slot):
        count = sum(kind_of(d) == kind for d in directions)
        whole = received[kind].at[slot, pl.ds(0, count)]
        k = KINDS.index(kind)
        return pltpu.make_async_remote_copy(
            src_ref=whole,
            dst_ref=whole,
            send_sem=send_sem.at[k],
            recv_sem=recv_sem.at[slot, 2 + k],
            device_id=neighbour((1, 0, 0)),
            device_id_type=MESH,
        )

    def wait_sent(directions, slot):
        for kind in KINDS:
            every(kind, directions, slot).wait_send()

    def collect_y(total, slot, place, scale):
        pltpu.make_async_remote_copy(
            src_ref=r_y.at[slot, place],
            dst_ref=r_y.at[slot, place],
            send_sem=send_sem.at[KINDS.index("y")],
            recv_sem=recv_sem.at[slot, place],
            device_id=neighbour((1, 0, 0)),
            device_id_type=MESH,
        ).wait_recv()
        for x in range(NPE):
            rows = pl.ds(pl.multiple_of(x * 64 + 56 * (1 - place), 8), 8)
            total[:, rows, :] += scale * r_y[slot, place, :, x * 8 : x * 8 + 8, :]

    def collect(total, directions, slot, scale):
        for kind in KINDS:
            if kind == "y":
                for d in directions:
                    if kind_of(d) == "y":
                        collect_y(total, slot, side(d[1]), scale)
                continue
            every(kind, directions, slot).wait_recv()
            for dx, dy, dz in directions:
                if kind_of((dx, dy, dz)) != kind:
                    continue
                sx, sy, sz = side(dx), side(dy), side(dz)
                ix, iy = 7 * (1 - sx), 7 * (1 - sy)
                c, iz = (0, 0) if dz > 0 else (1, 7)
                if kind == "x":
                    total[:, ix * 64 : ix * 64 + 64, :] += scale * r_x[slot, sx]
                elif kind == "xy":
                    row = (ix * NPE + iy) * NPE
                    total[:, row : row + 8, :] += scale * r_xy[slot, sx * 2 + sy]
                elif kind == "z":
                    total[c, pl.ds(iz, 64, stride=8), :] += scale * r_z[slot, sz]
                elif kind == "xz":
                    rows = pl.ds(ix * 64 + iz, 8, stride=8)
                    total[c, rows, :] += scale * r_xz[slot, sx * 2 + sz]
                elif kind == "yz":
                    rows = pl.ds(iy * 8 + iz, 8, stride=64)
                    total[c, rows, :] += scale * r_yz[slot, sy * 2 + sz]
                else:
                    row = (ix * NPE + iy) * NPE + iz
                    place = sx * 4 + sy * 2 + sz
                    total[c, row : row + 1, :] += scale * r_xyz[slot, place : place + 1, :]

    def pack_yz():
        for s in range(2):
            for t in range(2):
                yz_pack[t, s] = rims[s, pl.ds(Z_ROWS + 7 * t, 8, stride=8), :]

    loads[0].wait()
    field[0] = jnp.zeros((2, CDOF, STATES), F32)
    for x in range(NPE - 1):
        for y in range(NPE - 1):
            row = (x * NPE + y) * NPE
            field[0, 0, row : row + 8, :] = wave_ref[x, y, 0:8, :]
            field[0, 1, row : row + 7, :] = wave_ref[x, y, 7:14, :]
    rims[0, Z_ROWS : Z_ROWS + 64, :] = field[0, 0, pl.ds(0, 64, stride=8), :]
    for c in range(2):
        rims[c, E_ROWS : E_ROWS + 8, :] = field[0, c, 0:8, :]
        faces[c, X_ROWS : X_ROWS + 64, :] = field[0, c, 0:64, :]
        for x in range(NPE):
            faces[c, Y_ROWS + x * 8 : Y_ROWS + x * 8 + 8, :] = field[0, c, x * 64 : x * 64 + 8, :]
    yz_pack[0, 0] = rims[0, pl.ds(Z_ROWS, 8, stride=8), :]
    pl.semaphore_wait(barrier, len(UP + DOWN))
    send(DOWN, 0)

    loads[1].wait()
    near_place = lax.rem(me[1], 2)
    near_y = 7 * (1 - near_place)
    row_of = lax.broadcasted_iota(jnp.int32, (CDOF, CDOF), 0)
    n = lax.broadcasted_iota(jnp.int32, (64, CDOF), 0)
    for c in range(2):
        order = order_ref[c : c + 1, :]

        def chosen(rows):
            return (rows == order).astype(F32).astype(BF16)

        block = (n // 8) * 64 + lax.rem(n, 8)
        edges = [row_of[first : first + 8] for first in (0, 56, 448, 504)]
        rows = [n * 8 + 7 * c] + edges + [block, block + 56, n, n + 448]
        rows += [row_of[x * 64 + 8 : x * 64 + 56] for x in range(1, NPE - 1)]
        pick = chosen(jnp.concatenate(rows, axis=0))
        k = lax.broadcasted_iota(jnp.int32, (48, CDOF), 0)
        none = jnp.full((48, CDOF), -1, jnp.int32)
        near_rows = (k // 8 + 1) * 64 + near_y * 8 + lax.rem(k, 8)
        early_rows = [row_of[x * 64 + 8 : x * 64 + 56] for x in range(1, NPE - 1)]
        early_rows = [
            jnp.where(lax.rem(k, 8) == 7 * c, -1, rows) for rows in early_rows + [near_rows]
        ] + [none]
        rim_rows = (k // 8 + 1) * 64 + lax.rem(k, 8) * 8 + 7 * c
        late_rows = [
            n,
            n + 448,
            (k // 8 + 1) * 64 + (7 - near_y) * 8 + lax.rem(k, 8),
            jnp.where(lax.rem(k, 8) == 7 - near_y, -1, rim_rows),
            none[:32],
        ]
        early_columns = chosen(jnp.concatenate(early_rows, axis=0))
        late_columns = chosen(jnp.concatenate(late_rows, axis=0))
        loads[2 + c].wait()
        for part, value in enumerate(split(ham_raw[c])):
            half = jnp.dot(pick, value, preferred_element_type=F32).astype(BF16)
            whole = lax.dot_general(
                half, early_columns, (((1,), (1,)), ((), ())), preferred_element_type=F32
            ).astype(BF16)
            ham_early[c, part * ROWS : (part + 1) * ROWS, :] = whole
            whole = lax.dot_general(
                half, late_columns, (((1,), (1,)), ((), ())), preferred_element_type=F32
            ).astype(BF16)
            ham_sent[c, part * SENT : (part + 1) * SENT, :] = whole[:SENT]
            ham_inner[c, part * INNER : (part + 1) * INNER, :] = whole[SENT:]


    def four(matrix, value):
        rows = matrix.shape[0] // 2
        all_four = jnp.dot(matrix, value, preferred_element_type=F32)
        return (
            all_four[:rows, :STATES]
            + (all_four[:rows, STATES:] + all_four[rows:, :STATES])
            + all_four[rows:, STATES:]
        )

    def join(ref, first, count):
        upper, lower = pl.ds(first + 7, count, stride=8), pl.ds(first, count, stride=8)
        middle = ref[0, upper, :] + ref[1, lower, :]
        ref[0, upper, :] = middle
        ref[1, lower, :] = middle

    def pair(parts):
        return jnp.concatenate(split(jnp.concatenate(parts, axis=0)), axis=1)

    def y_rows(now, c, y):
        return [
            field[now, c, pl.ds(pl.multiple_of(x * 64 + y * 8, 8), 8), :]
            for x in range(1, NPE - 1)
        ]

    def multiply_early(now):
        for c in range(2):
            parts = [field[now, c, x * 64 + 8 : x * 64 + 56, :] for x in range(1, NPE - 1)]
            parts += y_rows(now, c, near_y) + [jnp.zeros((48, STATES), F32)]
            early[c] = four(ham_early[c], pair(parts))

    def late_values(now, c):
        parts = [field[now, c, 0:64, :], field[now, c, 448:512, :]]
        parts += y_rows(now, c, 7 - near_y)
        parts += [field[now, c, pl.ds(64 + 7 * c, 48, stride=8), :]]
        return pair(parts + [jnp.zeros((32, STATES), F32)])

    def apply(now, directions, factor, keep):
        later = slot = 1 - now
        gain, shift = factor / HALF_WIDTH, -factor * CENTER / HALF_WIDTH
        values = [late_values(now, c) for c in range(2)]
        for c in range(2):
            products = early[c, :SENT, :] + four(ham_sent[c], values[c])
            rims[c, :FIRST, :] = products[:FIRST]
            faces[c] = products[FIRST:]
        join(rims, E_ROWS, 4)
        pack_yz()
        join(faces, 0, 32)
        send(directions, slot)
        for c in range(2):
            inner[c, :INNER, :] = early[c, SENT:, :] + four(ham_inner[c], values[c])
        join(inner, 0, 36)

        def advance(c, row, count, products):
            rows = slice(row, row + count)
            fresh = gain * products + shift * field[now, c, rows, :]
            if keep:
                fresh = fresh - field[later, c, rows, :]
            field[later, c, rows, :] = fresh

        for c in range(2):
            for x in range(NPE):
                if x in (0, NPE - 1):
                    first = X_ROWS + 64 * (x // 7)
                    advance(c, x * 64, 64, faces[c, first : first + 64, :])
                    continue
                for t in range(2):
                    first = Y_ROWS + 64 * t + x * 8
                    advance(c, x * 64 + 56 * t, 8, faces[c, first : first + 8, :])
                first = (x - 1) * 48
                advance(c, x * 64 + 8, 48, inner[c, first : first + 48, :])
        total = field.at[later]
        if directions is ALL:
            collect_y(total, slot, near_place, gain)
            multiply_early(later)
            collect(total, [d for d in ALL if kind_of(d) != "y"], slot, gain)
            collect_y(total, slot, 1 - near_place, gain)
        else:
            collect(total, directions, slot, gain)
        wait_sent(directions, slot)

    @pl.when(near_place == 0)
    def _():
        collect_y(field.at[0], 0, 0, 1.0)

    multiply_early(0)
    collect(field.at[0], [d for d in DOWN if kind_of(d) != "y"], 0, 1.0)

    @pl.when(near_place == 1)
    def _():
        collect_y(field.at[0], 0, 0, 1.0)

    wait_sent(DOWN, 0)
    apply(0, ALL, 1.0, False)

    def two_steps(k, carry):
        apply(1, ALL, 2.0, True)
        apply(0, ALL, 2.0, True)
        return carry

    lax.fori_loop(0, (DEGREE - 2) // 2, two_steps, 0)
    apply(1, UP, 2.0, True)
    last = 0

    owned_z = lax.broadcasted_iota(jnp.int32, (7 * 8, STATES), 0) % 8 < 7
    blocks = []
    for c in range(2):
        for x in range(NPE - 1):
            block = field[last, c, x * 64 : x * 64 + 56, :]
            blocks.append(jnp.where(owned_z, block, 0.0))
    columns = jnp.concatenate(blocks, axis=0)
    high, low = split(columns)
    both = lax.dot_general(
        high,
        jnp.concatenate([high, low], axis=1),
        (((0,), (0,)), ((), ())),
        preferred_element_type=F32,
    )
    cross = both[:, STATES:]
    gram[...] = both[:, :STATES] + (cross + cross.T)

    piece = STATES // ring
    mine = pl.ds(pl.multiple_of(ring_place * piece, piece), piece)

    def scatter(j):
        rows = pl.ds(pl.multiple_of(lax.rem(ring_place + j, ring) * piece, piece), piece)
        return pltpu.make_async_remote_copy(
            src_ref=gram.at[rows],
            dst_ref=r_scatter.at[j - 1],
            send_sem=sum_send.at[0],
            recv_sem=sum_recv.at[0],
            device_id=in_ring(j),
            device_id_type=MESH,
        )

    def reduce(j):
        return pltpu.make_async_remote_copy(
            src_ref=r_reduce.at[other_place],
            dst_ref=r_reduce.at[other_place],
            send_sem=sum_send.at[1],
            recv_sem=sum_recv.at[1],
            device_id=across(j),
            device_id_type=MESH,
        )

    def gather(j):
        return pltpu.make_async_remote_copy(
            src_ref=r_gather.at[mine],
            dst_ref=r_gather.at[mine],
            send_sem=sum_send.at[2],
            recv_sem=sum_recv.at[2],
            device_id=in_ring(j),
            device_id_type=MESH,
        )

    def waiter(ref, k):
        return pltpu.make_async_remote_copy(
            src_ref=ref,
            dst_ref=ref,
            send_sem=sum_send.at[k],
            recv_sem=sum_recv.at[k],
            device_id=in_ring(1),
            device_id_type=MESH,
        )

    for j in range(1, ring):
        scatter(j).start()
    waiter(r_scatter, 0).wait_recv()
    r_reduce[other_place] = gram[mine, :] + jnp.sum(r_scatter[...], axis=0)
    for j in range(1, others):
        reduce(j).start()
    waiter(r_scatter, 0).wait_send()
    waiter(r_reduce.at[pl.ds(0, others - 1)], 1).wait_recv()
    nodes = 686 * nx * ny * nz
    r_gather[mine, :] = jnp.sum(r_reduce[...], axis=0) * (1.0 / nodes)
    for j in range(1, ring):
        gather(j).start()
    waiter(r_reduce.at[pl.ds(0, others - 1)], 1).wait_send()
    rest = r_gather.at[pl.ds(0, piece * (ring - 1))]
    waiter(rest, 2).wait_recv()

    total = r_gather[...]
    diagonal = lax.broadcasted_iota(jnp.int32, (STATES, STATES), 0) == (
        lax.broadcasted_iota(jnp.int32, (STATES, STATES), 1)
    )
    trace = jnp.sum(jnp.where(diagonal, total, 0.0), keepdims=True)
    three = jnp.where(diagonal, 3.0, 0.0)

    def newton(k, pair):
        root, inverse = pair
        middle = three - product(inverse, root)
        return 0.5 * product(root, middle), 0.5 * product(middle, inverse)

    scaled = total / trace
    middle = three - scaled
    root, inverse = lax.fori_loop(
        0, NS_STEPS - 2, newton, (0.5 * product(scaled, middle), 0.5 * middle)
    )
    inverse = 0.5 * product(three - product(inverse, root), inverse)
    rotation = inverse / jnp.sqrt(trace)
    for c in range(2):
        for x in range(NPE - 1):
            turned = product(field[last, c, x * 64 : x * 64 + 56, :], rotation)
            for y in range(NPE - 1):
                out_ref[x, y, c * 7 : c * 7 + 7, :] = turned[y * 8 : y * 8 + 7, :]
    waiter(rest, 2).wait_send()


def shards(wavefunctions, hamiltonians, cell_order):
    sizes = tuple(lax.axis_size(a) for a in AXES)
    ring, others = sizes[0] * 2, sizes[1] // 2 * sizes[2]
    piece = STATES // ring
    matrices = hamiltonians.reshape((2, CDOF, CDOF))
    orders = cell_order.reshape((2, CDOF))
    kinds = len(KINDS)
    return pl.pallas_call(
        functools.partial(kernel, sizes),
        out_shape=pltpu.VMEM(wavefunctions.shape, F32),
        in_specs=[pl.BlockSpec(memory_space=pltpu.HBM)] * 3,
        out_specs=pl.BlockSpec(memory_space=pltpu.VMEM),
        scratch_shapes=[
            pltpu.VMEM(wavefunctions.shape, F32),
            pltpu.VMEM((2, CDOF, CDOF), F32),
            pltpu.VMEM((2, CDOF), jnp.int32),
            pltpu.VMEM((2, 2 * ROWS, EARLY), BF16),
            pltpu.VMEM((2, 2 * SENT, LATE), BF16),
            pltpu.VMEM((2, 2 * INNER, LATE), BF16),
            pltpu.VMEM((2, ROWS, STATES), F32),
            pltpu.VMEM((2, 2, CDOF, STATES), F32),
            pltpu.VMEM((2, FIRST + 40, STATES), F32),
            pltpu.VMEM((2, SECOND, STATES), F32),
            pltpu.VMEM((2, INNER + 32, STATES), F32),
            pltpu.VMEM((2, 2, 8, STATES), F32),
            pltpu.VMEM((2, 2, 2, 64, STATES), F32),
            pltpu.VMEM((2, 2, 2, 64, STATES), F32),
            pltpu.VMEM((2, 2, 64, STATES), F32),
            pltpu.VMEM((2, 4, 2, 8, STATES), F32),
            pltpu.VMEM((2, 4, 8, STATES), F32),
            pltpu.VMEM((2, 4, 8, STATES), F32),
            pltpu.VMEM((2, 8, STATES), F32),
            pltpu.VMEM((STATES, STATES), F32),
            pltpu.VMEM((ring - 1, piece, STATES), F32),
            pltpu.VMEM((others, piece, STATES), F32),
            pltpu.VMEM((STATES, STATES), F32),
            pltpu.SemaphoreType.DMA((4,)),
            pltpu.SemaphoreType.DMA((kinds,)),
            pltpu.SemaphoreType.DMA((2, 2 + kinds)),
            pltpu.SemaphoreType.DMA((3,)),
            pltpu.SemaphoreType.DMA((3,)),
        ],
        compiler_params=pltpu.CompilerParams(
            collective_id=0, has_side_effects=True, vmem_limit_bytes=56 << 20
        ),
    )(wavefunctions, matrices, orders)


def solution(mesh):
    in_specs = (
        P("gx", "gy", "gz", None),
        P("gx", "gy", "gz", None, None),
        P("gx", "gy", "gz", None),
    )
    out_specs = P("gx", "gy", "gz", None)
    return jax.shard_map(
        shards, mesh=mesh, in_specs=in_specs, out_specs=out_specs, check_vma=False
    )
```

```python
import functools
import itertools

import jax
import jax.numpy as jnp
from jax import lax
from jax.experimental import pallas as pl
from jax.experimental.pallas import tpu as pltpu
from jax.sharding import PartitionSpec as P

NPE = 8
CDOF = 512
STATES = 128
DEGREE = 6
NS_STEPS = 12
CENTER = 0.4
HALF_WIDTH = 0.7
AXES = ("gx", "gy", "gz")
MESH = pl.DeviceIdType.MESH
F32 = jnp.float32
BF16 = jnp.bfloat16

ALL = sorted(
    (d for d in itertools.product((-1, 0, 1), repeat=3) if any(d)),
    key=lambda d: -sum(map(abs, d)),
)
DOWN = [d for d in itertools.product((-1, 0), repeat=3) if any(d)]
UP = [d for d in itertools.product((1, 0), repeat=3) if any(d)]

KINDS = ("x", "z", "xz", "y", "xy", "yz", "xyz")
Y_ROWS, X_ROWS = 0, 128
INNER = 36 * 8
SENT = 64 + 128 + 96
ROWS = SENT + INNER
EARLY, LATE = 384, 256


def split(value):
    high = value.astype(BF16)
    low = (value - high.astype(F32)).astype(BF16)
    return high, low


def product(left, right):
    columns = right.shape[1]
    high, low = split(right)
    upper = jnp.concatenate([high, low], axis=1)
    lower = jnp.concatenate([high, jnp.zeros_like(low)], axis=1)
    sums = jnp.dot(
        jnp.concatenate(split(left), axis=1),
        jnp.concatenate([upper, lower], axis=0),
        preferred_element_type=F32,
    )
    return sums[:, :columns] + sums[:, columns:]


def side(step):
    return (step + 1) // 2


def kind_of(d):
    return "".join(name for name, step in zip("xyz", d) if step)


def kernel(
    sizes,
    wave_hbm,
    ham_hbm,
    order_hbm,
    out_ref,
    wave_ref,
    ham_raw,
    pick,
    early_columns,
    late_columns,
    order_ref,
    ham_early,
    ham_sent,
    ham_inner,
    early,
    field,
    rims,
    faces,
    inner,
    yz_pack,
    r_x,
    r_y,
    r_z,
    r_xy,
    r_xz,
    r_yz,
    r_xyz,
    gram,
    r_scatter,
    r_reduce,
    r_gather,
    load_sem,
    send_sem,
    recv_sem,
    sum_send,
    sum_recv,
):
    me = tuple(lax.axis_index(a) for a in AXES)
    nx, ny, nz = sizes
    received = dict(x=r_x, y=r_y, z=r_z, xy=r_xy, xz=r_xz, yz=r_yz, xyz=r_xyz)

    shifted = [
        {s: lax.rem(m + (s + n), n) for s in (-1, 0, 1)} for m, n in zip(me, sizes)
    ]
    neighbours = {
        d: tuple(table[s] for table, s in zip(shifted, d)) for d in ALL
    }

    def neighbour(d):
        return neighbours[d]

    ring_place = me[0] * 2 + lax.rem(me[1], 2)
    other_place = (me[1] // 2) * nz + me[2]
    ring, others = nx * 2, (ny // 2) * nz

    def in_ring(j):
        place = lax.rem(ring_place + j, ring)
        return (place // 2, (me[1] // 2) * 2 + lax.rem(place, 2), me[2])

    def across(j):
        place = lax.rem(other_place + j, others)
        return (me[0], (place // nz) * 2 + lax.rem(me[1], 2), lax.rem(place, nz))

    barrier = pltpu.get_barrier_semaphore()
    for d in UP + DOWN:
        pl.semaphore_signal(barrier, inc=1, device_id=neighbour(d), device_id_type=MESH)

    loads = [
        pltpu.make_async_copy(wave_hbm, wave_ref, load_sem.at[0]),
        pltpu.make_async_copy(order_hbm, order_ref, load_sem.at[1]),
        pltpu.make_async_copy(ham_hbm.at[0], ham_raw.at[0], load_sem.at[2]),
        pltpu.make_async_copy(ham_hbm.at[1], ham_raw.at[1], load_sem.at[3]),
    ]
    for load in loads:
        load.start()

    def message(d, slot):
        dx, dy, dz = d
        kind = kind_of(d)
        sx, sy, sz = side(dx), side(dy), side(dz)
        if kind == "x":
            source, place = faces.at[:, pl.ds(X_ROWS + sx * 64, 64)], sx
        elif kind == "y":
            source, place = faces.at[:, pl.ds(Y_ROWS + sy * 64, 64)], sy
        elif kind == "z":
            source, place = rims.at[sz, pl.ds(0, 64)], sz
        elif kind == "xy":
            source = faces.at[:, pl.ds(X_ROWS + sx * 64 + sy * 56, 8)]
            place = sx * 2 + sy
        elif kind == "xz":
            source = rims.at[sz, pl.ds(sx * 56, 8)]
            place = sx * 2 + sz
        elif kind == "yz":
            source, place = yz_pack.at[sy, sz], sy * 2 + sz
        else:
            source = rims.at[sz, pl.ds(sx * 56 + sy * 7, 1)]
            place = sx * 4 + sy * 2 + sz
        if kind == "xyz":
            target = r_xyz.at[slot, pl.ds(place, 1)]
        else:
            target = received[kind].at[slot, place]
        k = KINDS.index(kind)
        return pltpu.make_async_remote_copy(
            src_ref=source,
            dst_ref=target,
            send_sem=send_sem.at[k],
            recv_sem=recv_sem.at[slot, place if kind == "y" else 2 + k],
            device_id=neighbour(d),
            device_id_type=MESH,
        )

    def send(directions, slot):
        for d in directions:
            message(d, slot).start()

    def every(kind, directions, slot):
        count = sum(kind_of(d) == kind for d in directions)
        whole = received[kind].at[slot, pl.ds(0, count)]
        k = KINDS.index(kind)
        return pltpu.make_async_remote_copy(
            src_ref=whole,
            dst_ref=whole,
            send_sem=send_sem.at[k],
            recv_sem=recv_sem.at[slot, 2 + k],
            device_id=neighbour((1, 0, 0)),
            device_id_type=MESH,
        )

    def wait_sent(directions, slot):
        for kind in KINDS:
            every(kind, directions, slot).wait_send()

    def collect_y(total, slot, place, scale):
        pltpu.make_async_remote_copy(
            src_ref=r_y.at[slot, place],
            dst_ref=r_y.at[slot, place],
            send_sem=send_sem.at[KINDS.index("y")],
            recv_sem=recv_sem.at[slot, place],
            device_id=neighbour((1, 0, 0)),
            device_id_type=MESH,
        ).wait_recv()
        for x in range(NPE):
            rows = pl.ds(pl.multiple_of(x * 64 + 56 * (1 - place), 8), 8)
            total[:, rows, :] += scale * r_y[slot, place, :, x * 8 : x * 8 + 8, :]

    def collect(total, directions, slot, scale):
        for kind in KINDS:
            if kind == "y":
                for d in directions:
                    if kind_of(d) == "y":
                        collect_y(total, slot, side(d[1]), scale)
                continue
            every(kind, directions, slot).wait_recv()
            for dx, dy, dz in directions:
                if kind_of((dx, dy, dz)) != kind:
                    continue
                sx, sy, sz = side(dx), side(dy), side(dz)
                ix, iy = 7 * (1 - sx), 7 * (1 - sy)
                c, iz = (0, 0) if dz > 0 else (1, 7)
                if kind == "x":
                    total[:, ix * 64 : ix * 64 + 64, :] += scale * r_x[slot, sx]
                elif kind == "xy":
                    row = (ix * NPE + iy) * NPE
                    total[:, row : row + 8, :] += scale * r_xy[slot, sx * 2 + sy]
                elif kind == "z":
                    total[c, pl.ds(iz, 64, stride=8), :] += scale * r_z[slot, sz]
                elif kind == "xz":
                    rows = pl.ds(ix * 64 + iz, 8, stride=8)
                    total[c, rows, :] += scale * r_xz[slot, sx * 2 + sz]
                elif kind == "yz":
                    rows = pl.ds(iy * 8 + iz, 8, stride=64)
                    total[c, rows, :] += scale * r_yz[slot, sy * 2 + sz]
                else:
                    row = (ix * NPE + iy) * NPE + iz
                    place = sx * 4 + sy * 2 + sz
                    total[c, row : row + 1, :] += scale * r_xyz[slot, place : place + 1, :]

    def pack_yz():
        for s in range(2):
            for t in range(2):
                yz_pack[t, s] = rims[s, pl.ds(7 * t, 8, stride=8), :]

    loads[0].wait()
    field[0] = jnp.zeros((2, CDOF, STATES), F32)
    for x in range(NPE - 1):
        for y in range(NPE - 1):
            row = (x * NPE + y) * NPE
            field[0, 0, row : row + 8, :] = wave_ref[x, y, 0:8, :]
            field[0, 1, row : row + 7, :] = wave_ref[x, y, 7:14, :]
    rims[0] = field[0, 0, pl.ds(0, 64, stride=8), :]
    for c in range(2):
        faces[c, X_ROWS : X_ROWS + 64, :] = field[0, c, 0:64, :]
        for x in range(NPE):
            faces[c, Y_ROWS + x * 8 : Y_ROWS + x * 8 + 8, :] = field[0, c, x * 64 : x * 64 + 8, :]
    yz_pack[0, 0] = rims[0, pl.ds(0, 8, stride=8), :]
    loads[1].wait()
    near_place = lax.rem(me[1], 2)
    near_y = 7 * (1 - near_place)
    row_of = lax.broadcasted_iota(jnp.int32, (CDOF, CDOF), 0)
    n = lax.broadcasted_iota(jnp.int32, (64, CDOF), 0)
    for c in range(2):
        order = order_ref[c : c + 1, :]

        def chosen(rows):
            return (rows == order).astype(F32).astype(BF16)

        block = (n // 8) * 64 + lax.rem(n, 8)
        rows = [n * 8 + 7 * c, block, block + 56, n[8:56], n[8:56] + 448]
        rows += [row_of[x * 64 + 8 : x * 64 + 56] for x in range(1, NPE - 1)]
        pick[c] = chosen(jnp.concatenate(rows, axis=0))
        k = lax.broadcasted_iota(jnp.int32, (48, CDOF), 0)
        none = jnp.full((48, CDOF), -1, jnp.int32)
        near_rows = (k // 8 + 1) * 64 + near_y * 8 + lax.rem(k, 8)
        early_rows = [row_of[x * 64 + 8 : x * 64 + 56] for x in range(1, NPE - 1)]
        early_rows = [
            jnp.where(lax.rem(k, 8) == 7 * c, -1, rows) for rows in early_rows + [near_rows]
        ] + [none]
        rim_rows = (k // 8 + 1) * 64 + lax.rem(k, 8) * 8 + 7 * c
        late_rows = [
            n,
            n + 448,
            (k // 8 + 1) * 64 + (7 - near_y) * 8 + lax.rem(k, 8),
            jnp.where(lax.rem(k, 8) == 7 - near_y, -1, rim_rows),
            none[:32],
        ]
        early_columns[c] = chosen(jnp.concatenate(early_rows, axis=0))
        late_columns[c] = chosen(jnp.concatenate(late_rows, axis=0))

    pl.semaphore_wait(barrier, len(UP + DOWN))
    send(DOWN, 0)

    for c in range(2):
        loads[2 + c].wait()
        for part, value in enumerate(split(ham_raw[c])):
            half = jnp.dot(pick[c], value, preferred_element_type=F32).astype(BF16)
            whole = lax.dot_general(
                half, early_columns[c], (((1,), (1,)), ((), ())), preferred_element_type=F32
            ).astype(BF16)
            ham_early[c, part * ROWS : (part + 1) * ROWS, :] = whole
            whole = lax.dot_general(
                half, late_columns[c], (((1,), (1,)), ((), ())), preferred_element_type=F32
            ).astype(BF16)
            ham_sent[c, part * SENT : (part + 1) * SENT, :] = whole[:SENT]
            ham_inner[c, part * INNER : (part + 1) * INNER, :] = whole[SENT:]


    def four(matrix, value):
        rows = matrix.shape[0] // 2
        all_four = jnp.dot(matrix, value, preferred_element_type=F32)
        return (
            all_four[:rows, :STATES]
            + (all_four[:rows, STATES:] + all_four[rows:, :STATES])
            + all_four[rows:, STATES:]
        )

    def join(ref, first, count):
        upper, lower = pl.ds(first + 7, count, stride=8), pl.ds(first, count, stride=8)
        middle = ref[0, upper, :] + ref[1, lower, :]
        ref[0, upper, :] = middle
        ref[1, lower, :] = middle

    def pair(parts):
        return jnp.concatenate(split(jnp.concatenate(parts, axis=0)), axis=1)

    def y_rows(now, c, y):
        return [
            field[now, c, pl.ds(pl.multiple_of(x * 64 + y * 8, 8), 8), :]
            for x in range(1, NPE - 1)
        ]

    def multiply_early(now):
        for c in range(2):
            parts = [field[now, c, x * 64 + 8 : x * 64 + 56, :] for x in range(1, NPE - 1)]
            parts += y_rows(now, c, near_y) + [jnp.zeros((48, STATES), F32)]
            early[c] = four(ham_early[c], pair(parts))

    def late_values(now, c):
        parts = [field[now, c, 0:64, :], field[now, c, 448:512, :]]
        parts += y_rows(now, c, 7 - near_y)
        parts += [field[now, c, pl.ds(64 + 7 * c, 48, stride=8), :]]
        return pair(parts + [jnp.zeros((32, STATES), F32)])

    def apply(now, directions, factor, keep):
        later = slot = 1 - now
        gain, shift = factor / HALF_WIDTH, -factor * CENTER / HALF_WIDTH
        values = [late_values(now, c) for c in range(2)]
        for c in range(2):
            products = early[c, :SENT, :] + four(ham_sent[c], values[c])
            rims[c] = products[:64]
            faces[c, Y_ROWS : Y_ROWS + 128, :] = products[64:192]
            for t in range(2):
                row = X_ROWS + t * 64
                faces[c, row + 8 : row + 56, :] = products[192 + t * 48 : 240 + t * 48]
                for u in range(2):
                    edge = products[64 + u * 64 + t * 56 : 72 + u * 64 + t * 56]
                    faces[c, row + u * 56 : row + u * 56 + 8, :] = edge
        pack_yz()
        join(faces, 0, 32)
        send(directions, slot)
        for c in range(2):
            inner[c, :INNER, :] = early[c, SENT:, :] + four(ham_inner[c], values[c])
        join(inner, 0, 36)

        def advance(c, row, count, products):
            rows = slice(row, row + count)
            fresh = gain * products + shift * field[now, c, rows, :]
            if keep:
                fresh = fresh - field[later, c, rows, :]
            field[later, c, rows, :] = fresh

        for c in range(2):
            for x in range(NPE):
                if x in (0, NPE - 1):
                    first = X_ROWS + 64 * (x // 7)
                    advance(c, x * 64, 64, faces[c, first : first + 64, :])
                    continue
                for t in range(2):
                    first = Y_ROWS + 64 * t + x * 8
                    advance(c, x * 64 + 56 * t, 8, faces[c, first : first + 8, :])
                first = (x - 1) * 48
                advance(c, x * 64 + 8, 48, inner[c, first : first + 48, :])
        total = field.at[later]
        if directions is ALL:
            collect_y(total, slot, near_place, gain)
            multiply_early(later)
            collect(total, [d for d in ALL if kind_of(d) != "y"], slot, gain)
            collect_y(total, slot, 1 - near_place, gain)
        else:
            collect(total, directions, slot, gain)
        wait_sent(directions, slot)

    @pl.when(near_place == 0)
    def _():
        collect_y(field.at[0], 0, 0, 1.0)

    multiply_early(0)
    collect(field.at[0], [d for d in DOWN if kind_of(d) != "y"], 0, 1.0)

    @pl.when(near_place == 1)
    def _():
        collect_y(field.at[0], 0, 0, 1.0)

    wait_sent(DOWN, 0)
    apply(0, ALL, 1.0, False)

    def two_steps(k, carry):
        apply(1, ALL, 2.0, True)
        apply(0, ALL, 2.0, True)
        return carry

    lax.fori_loop(0, (DEGREE - 2) // 2, two_steps, 0)
    apply(1, UP, 2.0, True)
    last = 0

    owned_z = lax.broadcasted_iota(jnp.int32, (7 * 8, STATES), 0) % 8 < 7
    blocks = []
    for c in range(2):
        for x in range(NPE - 1):
            block = field[last, c, x * 64 : x * 64 + 56, :]
            blocks.append(jnp.where(owned_z, block, 0.0))
    columns = jnp.concatenate(blocks, axis=0)
    high, low = split(columns)
    both = lax.dot_general(
        high,
        jnp.concatenate([high, low], axis=1),
        (((0,), (0,)), ((), ())),
        preferred_element_type=F32,
    )
    cross = both[:, STATES:]
    gram[...] = both[:, :STATES] + (cross + cross.T)

    piece = STATES // ring
    mine = pl.ds(pl.multiple_of(ring_place * piece, piece), piece)

    def scatter(j):
        rows = pl.ds(pl.multiple_of(lax.rem(ring_place + j, ring) * piece, piece), piece)
        return pltpu.make_async_remote_copy(
            src_ref=gram.at[rows],
            dst_ref=r_scatter.at[j - 1],
            send_sem=sum_send.at[0],
            recv_sem=sum_recv.at[0],
            device_id=in_ring(j),
            device_id_type=MESH,
        )

    def reduce(j):
        return pltpu.make_async_remote_copy(
            src_ref=r_reduce.at[other_place],
            dst_ref=r_reduce.at[other_place],
            send_sem=sum_send.at[1],
            recv_sem=sum_recv.at[1],
            device_id=across(j),
            device_id_type=MESH,
        )

    def gather(j):
        return pltpu.make_async_remote_copy(
            src_ref=r_gather.at[mine],
            dst_ref=r_gather.at[mine],
            send_sem=sum_send.at[2],
            recv_sem=sum_recv.at[2],
            device_id=in_ring(j),
            device_id_type=MESH,
        )

    def waiter(ref, k):
        return pltpu.make_async_remote_copy(
            src_ref=ref,
            dst_ref=ref,
            send_sem=sum_send.at[k],
            recv_sem=sum_recv.at[k],
            device_id=in_ring(1),
            device_id_type=MESH,
        )

    for j in range(1, ring):
        scatter(j).start()
    waiter(r_scatter, 0).wait_recv()
    r_reduce[other_place] = gram[mine, :] + jnp.sum(r_scatter[...], axis=0)
    for j in range(1, others):
        reduce(j).start()
    waiter(r_scatter, 0).wait_send()
    waiter(r_reduce.at[pl.ds(0, others - 1)], 1).wait_recv()
    nodes = 686 * nx * ny * nz
    r_gather[mine, :] = jnp.sum(r_reduce[...], axis=0) * (1.0 / nodes)
    for j in range(1, ring):
        gather(j).start()
    waiter(r_reduce.at[pl.ds(0, others - 1)], 1).wait_send()
    rest = r_gather.at[pl.ds(0, piece * (ring - 1))]
    waiter(rest, 2).wait_recv()

    total = r_gather[...]
    diagonal = lax.broadcasted_iota(jnp.int32, (STATES, STATES), 0) == (
        lax.broadcasted_iota(jnp.int32, (STATES, STATES), 1)
    )
    trace = jnp.sum(jnp.where(diagonal, total, 0.0), keepdims=True)
    three = jnp.where(diagonal, 3.0, 0.0)

    def newton(k, pair):
        root, inverse = pair
        middle = three - product(inverse, root)
        return 0.5 * product(root, middle), 0.5 * product(middle, inverse)

    scaled = total / trace
    middle = three - scaled
    root, inverse = lax.fori_loop(
        0, NS_STEPS - 2, newton, (0.5 * product(scaled, middle), 0.5 * middle)
    )
    inverse = 0.5 * product(three - product(inverse, root), inverse)
    rotation = inverse / jnp.sqrt(trace)
    for c in range(2):
        for x in range(NPE - 1):
            turned = product(field[last, c, x * 64 : x * 64 + 56, :], rotation)
            for y in range(NPE - 1):
                out_ref[x, y, c * 7 : c * 7 + 7, :] = turned[y * 8 : y * 8 + 7, :]
    waiter(rest, 2).wait_send()


def shards(wavefunctions, hamiltonians, cell_order):
    sizes = tuple(lax.axis_size(a) for a in AXES)
    ring, others = sizes[0] * 2, sizes[1] // 2 * sizes[2]
    piece = STATES // ring
    matrices = hamiltonians.reshape((2, CDOF, CDOF))
    orders = cell_order.reshape((2, CDOF))
    kinds = len(KINDS)
    return pl.pallas_call(
        functools.partial(kernel, sizes),
        out_shape=pltpu.VMEM(wavefunctions.shape, F32),
        in_specs=[pl.BlockSpec(memory_space=pltpu.HBM)] * 3,
        out_specs=pl.BlockSpec(memory_space=pltpu.VMEM),
        scratch_shapes=[
            pltpu.VMEM(wavefunctions.shape, F32),
            pltpu.VMEM((2, CDOF, CDOF), F32),
            pltpu.VMEM((2, ROWS, CDOF), BF16),
            pltpu.VMEM((2, EARLY, CDOF), BF16),
            pltpu.VMEM((2, LATE, CDOF), BF16),
            pltpu.VMEM((2, CDOF), jnp.int32),
            pltpu.VMEM((2, 2 * ROWS, EARLY), BF16),
            pltpu.VMEM((2, 2 * SENT, LATE), BF16),
            pltpu.VMEM((2, 2 * INNER, LATE), BF16),
            pltpu.VMEM((2, ROWS, STATES), F32),
            pltpu.VMEM((2, 2, CDOF, STATES), F32),
            pltpu.VMEM((2, 64, STATES), F32),
            pltpu.VMEM((2, 256, STATES), F32),
            pltpu.VMEM((2, INNER + 32, STATES), F32),
            pltpu.VMEM((2, 2, 8, STATES), F32),
            pltpu.VMEM((2, 2, 2, 64, STATES), F32),
            pltpu.VMEM((2, 2, 2, 64, STATES), F32),
            pltpu.VMEM((2, 2, 64, STATES), F32),
            pltpu.VMEM((2, 4, 2, 8, STATES), F32),
            pltpu.VMEM((2, 4, 8, STATES), F32),
            pltpu.VMEM((2, 4, 8, STATES), F32),
            pltpu.VMEM((2, 8, STATES), F32),
            pltpu.VMEM((STATES, STATES), F32),
            pltpu.VMEM((ring - 1, piece, STATES), F32),
            pltpu.VMEM((others, piece, STATES), F32),
            pltpu.VMEM((STATES, STATES), F32),
            pltpu.SemaphoreType.DMA((4,)),
            pltpu.SemaphoreType.DMA((kinds,)),
            pltpu.SemaphoreType.DMA((2, 2 + kinds)),
            pltpu.SemaphoreType.DMA((3,)),
            pltpu.SemaphoreType.DMA((3,)),
        ],
        compiler_params=pltpu.CompilerParams(
            collective_id=0, has_side_effects=True, vmem_limit_bytes=56 << 20
        ),
    )(wavefunctions, matrices, orders)


def solution(mesh):
    in_specs = (
        P("gx", "gy", "gz", None),
        P("gx", "gy", "gz", None, None),
        P("gx", "gy", "gz", None),
    )
    out_specs = P("gx", "gy", "gz", None)
    return jax.shard_map(
        shards, mesh=mesh, in_specs=in_specs, out_specs=out_specs, check_vma=False
    )
```

```python
import functools
import itertools

import jax
import jax.numpy as jnp
from jax import lax
from jax.experimental import pallas as pl
from jax.experimental.pallas import tpu as pltpu
from jax.sharding import PartitionSpec as P

NPE = 8
CDOF = 512
STATES = 128
DEGREE = 6
NS_STEPS = 12
CENTER = 0.4
HALF_WIDTH = 0.7
AXES = ("gx", "gy", "gz")
MESH = pl.DeviceIdType.MESH
F32 = jnp.float32
BF16 = jnp.bfloat16

ALL = sorted(
    (d for d in itertools.product((-1, 0, 1), repeat=3) if any(d)),
    key=lambda d: -sum(map(abs, d)),
)
DOWN = [d for d in ALL if max(d) <= 0]
UP = [d for d in ALL if min(d) >= 0]

KINDS = ("x", "z", "xz", "y", "xy", "yz", "xyz")
Y_ROWS, X_ROWS = 0, 128
INNER = 36 * 8
SENT = 64 + 128 + 96
ROWS = SENT + INNER
EARLY, LATE = 384, 256


def split(value):
    high = value.astype(BF16)
    low = (value - high.astype(F32)).astype(BF16)
    return high, low


def product(left, right):
    columns = right.shape[1]
    high, low = split(right)
    upper = jnp.concatenate([high, low], axis=1)
    lower = jnp.concatenate([high, jnp.zeros_like(low)], axis=1)
    sums = jnp.dot(
        jnp.concatenate(split(left), axis=1),
        jnp.concatenate([upper, lower], axis=0),
        preferred_element_type=F32,
    )
    return sums[:, :columns] + sums[:, columns:]


def side(step):
    return (step + 1) // 2


def kind_of(d):
    return "".join(name for name, step in zip("xyz", d) if step)


def kernel(
    sizes,
    wave_hbm,
    ham_hbm,
    order_hbm,
    out_ref,
    wave_ref,
    ham_raw,
    pick,
    early_columns,
    late_columns,
    order_ref,
    ham_early,
    ham_sent,
    ham_inner,
    early,
    field,
    rims,
    faces,
    inner,
    yz_pack,
    r_x,
    r_y,
    r_z,
    r_xy,
    r_xz,
    r_yz,
    r_xyz,
    gram,
    r_scatter,
    r_reduce,
    r_gather,
    load_sem,
    send_sem,
    recv_sem,
    sum_send,
    sum_recv,
):
    me = tuple(lax.axis_index(a) for a in AXES)
    nx, ny, nz = sizes
    received = dict(x=r_x, y=r_y, z=r_z, xy=r_xy, xz=r_xz, yz=r_yz, xyz=r_xyz)

    shifted = [
        {s: lax.rem(m + (s + n), n) for s in (-1, 0, 1)} for m, n in zip(me, sizes)
    ]
    neighbours = {
        d: tuple(table[s] for table, s in zip(shifted, d)) for d in ALL
    }

    def neighbour(d):
        return neighbours[d]

    ring_place = me[0] * 2 + lax.rem(me[1], 2)
    other_place = (me[1] // 2) * nz + me[2]
    ring, others = nx * 2, (ny // 2) * nz

    def turns(*lengths):
        shifts = [j for j in itertools.product(*map(range, lengths)) if any(j)]
        return sorted(shifts, key=lambda j: -sum(min(i, n - i) for i, n in zip(j, lengths)))

    def in_ring(j):
        x = lax.rem(me[0] + j[0], nx)
        core = lax.rem(me[1] + j[1], 2)
        return (x, (me[1] // 2) * 2 + core, me[2]), x * 2 + core

    def across(j):
        y = lax.rem((me[1] // 2) * 2 + me[2] // 4 + j[0], 4)
        z = lax.rem(y, 2) * 4 + lax.rem(me[2] + j[1], 4)
        return (me[0], (y // 2) * 2 + lax.rem(me[1], 2), z)

    barrier = pltpu.get_barrier_semaphore()
    for d in UP + DOWN:
        pl.semaphore_signal(barrier, inc=1, device_id=neighbour(d), device_id_type=MESH)

    loads = [
        pltpu.make_async_copy(wave_hbm, wave_ref, load_sem.at[0]),
        pltpu.make_async_copy(order_hbm, order_ref, load_sem.at[1]),
        pltpu.make_async_copy(ham_hbm.at[0], ham_raw.at[0], load_sem.at[2]),
        pltpu.make_async_copy(ham_hbm.at[1], ham_raw.at[1], load_sem.at[3]),
    ]
    for load in loads:
        load.start()

    def message(d, slot):
        dx, dy, dz = d
        kind = kind_of(d)
        sx, sy, sz = side(dx), side(dy), side(dz)
        if kind == "x":
            source, place = faces.at[:, pl.ds(X_ROWS + sx * 64, 64)], sx
        elif kind == "y":
            source, place = faces.at[:, pl.ds(Y_ROWS + sy * 64, 64)], sy
        elif kind == "z":
            source, place = rims.at[sz, pl.ds(0, 64)], sz
        elif kind == "xy":
            source = faces.at[:, pl.ds(X_ROWS + sx * 64 + sy * 56, 8)]
            place = sx * 2 + sy
        elif kind == "xz":
            source = rims.at[sz, pl.ds(sx * 56, 8)]
            place = sx * 2 + sz
        elif kind == "yz":
            source, place = yz_pack.at[sy, sz], sy * 2 + sz
        else:
            source = rims.at[sz, pl.ds(sx * 56 + sy * 7, 1)]
            place = sx * 4 + sy * 2 + sz
        if kind == "xyz":
            target = r_xyz.at[slot, pl.ds(place, 1)]
        else:
            target = received[kind].at[slot, place]
        k = KINDS.index(kind)
        return pltpu.make_async_remote_copy(
            src_ref=source,
            dst_ref=target,
            send_sem=send_sem.at[k],
            recv_sem=recv_sem.at[slot, place if kind == "y" else 2 + k],
            device_id=neighbour(d),
            device_id_type=MESH,
        )

    def send(directions, slot):
        for d in directions:
            message(d, slot).start()

    def every(kind, directions, slot):
        count = sum(kind_of(d) == kind for d in directions)
        whole = received[kind].at[slot, pl.ds(0, count)]
        k = KINDS.index(kind)
        return pltpu.make_async_remote_copy(
            src_ref=whole,
            dst_ref=whole,
            send_sem=send_sem.at[k],
            recv_sem=recv_sem.at[slot, 2 + k],
            device_id=neighbour((1, 0, 0)),
            device_id_type=MESH,
        )

    def wait_sent(directions, slot):
        for kind in KINDS:
            every(kind, directions, slot).wait_send()

    def collect_y(total, slot, place, scale):
        pltpu.make_async_remote_copy(
            src_ref=r_y.at[slot, place],
            dst_ref=r_y.at[slot, place],
            send_sem=send_sem.at[KINDS.index("y")],
            recv_sem=recv_sem.at[slot, place],
            device_id=neighbour((1, 0, 0)),
            device_id_type=MESH,
        ).wait_recv()
        for x in range(NPE):
            rows = pl.ds(pl.multiple_of(x * 64 + 56 * (1 - place), 8), 8)
            total[:, rows, :] += scale * r_y[slot, place, :, x * 8 : x * 8 + 8, :]

    def collect(total, directions, slot, scale):
        for kind in KINDS:
            if kind == "y":
                for d in directions:
                    if kind_of(d) == "y":
                        collect_y(total, slot, side(d[1]), scale)
                continue
            every(kind, directions, slot).wait_recv()
            for dx, dy, dz in directions:
                if kind_of((dx, dy, dz)) != kind:
                    continue
                sx, sy, sz = side(dx), side(dy), side(dz)
                ix, iy = 7 * (1 - sx), 7 * (1 - sy)
                c, iz = (0, 0) if dz > 0 else (1, 7)
                if kind == "x":
                    total[:, ix * 64 : ix * 64 + 64, :] += scale * r_x[slot, sx]
                elif kind == "xy":
                    row = (ix * NPE + iy) * NPE
                    total[:, row : row + 8, :] += scale * r_xy[slot, sx * 2 + sy]
                elif kind == "z":
                    total[c, pl.ds(iz, 64, stride=8), :] += scale * r_z[slot, sz]
                elif kind == "xz":
                    rows = pl.ds(ix * 64 + iz, 8, stride=8)
                    total[c, rows, :] += scale * r_xz[slot, sx * 2 + sz]
                elif kind == "yz":
                    rows = pl.ds(iy * 8 + iz, 8, stride=64)
                    total[c, rows, :] += scale * r_yz[slot, sy * 2 + sz]
                else:
                    row = (ix * NPE + iy) * NPE + iz
                    place = sx * 4 + sy * 2 + sz
                    total[c, row : row + 1, :] += scale * r_xyz[slot, place : place + 1, :]

    def pack_yz():
        for s in range(2):
            for t in range(2):
                yz_pack[t, s] = rims[s, pl.ds(7 * t, 8, stride=8), :]

    loads[0].wait()
    field[0] = jnp.zeros((2, CDOF, STATES), F32)
    for x in range(NPE - 1):
        for y in range(NPE - 1):
            row = (x * NPE + y) * NPE
            field[0, 0, row : row + 8, :] = wave_ref[x, y, 0:8, :]
            field[0, 1, row : row + 7, :] = wave_ref[x, y, 7:14, :]
    rims[0] = field[0, 0, pl.ds(0, 64, stride=8), :]
    for c in range(2):
        faces[c, X_ROWS : X_ROWS + 64, :] = field[0, c, 0:64, :]
        for x in range(NPE):
            faces[c, Y_ROWS + x * 8 : Y_ROWS + x * 8 + 8, :] = field[0, c, x * 64 : x * 64 + 8, :]
    yz_pack[0, 0] = rims[0, pl.ds(0, 8, stride=8), :]
    loads[1].wait()
    near_place = lax.rem(me[1], 2)
    near_y = 7 * (1 - near_place)
    row_of = lax.broadcasted_iota(jnp.int32, (CDOF, CDOF), 0)
    n = lax.broadcasted_iota(jnp.int32, (64, CDOF), 0)
    for c in range(2):
        order = order_ref[c : c + 1, :]

        def chosen(rows):
            return (rows == order).astype(F32).astype(BF16)

        block = (n // 8) * 64 + lax.rem(n, 8)
        rows = [n * 8 + 7 * c, block, block + 56, n[8:56], n[8:56] + 448]
        rows += [row_of[x * 64 + 8 : x * 64 + 56] for x in range(1, NPE - 1)]
        pick[c] = chosen(jnp.concatenate(rows, axis=0))
        k = lax.broadcasted_iota(jnp.int32, (48, CDOF), 0)
        none = jnp.full((48, CDOF), -1, jnp.int32)
        near_rows = (k // 8 + 1) * 64 + near_y * 8 + lax.rem(k, 8)
        early_rows = [row_of[x * 64 + 8 : x * 64 + 56] for x in range(1, NPE - 1)]
        early_rows = [
            jnp.where(lax.rem(k, 8) == 7 * c, -1, rows) for rows in early_rows + [near_rows]
        ] + [none]
        rim_rows = (k // 8 + 1) * 64 + lax.rem(k, 8) * 8 + 7 * c
        late_rows = [
            n,
            n + 448,
            (k // 8 + 1) * 64 + (7 - near_y) * 8 + lax.rem(k, 8),
            jnp.where(lax.rem(k, 8) == 7 - near_y, -1, rim_rows),
            none[:32],
        ]
        early_columns[c] = chosen(jnp.concatenate(early_rows, axis=0))
        late_columns[c] = chosen(jnp.concatenate(late_rows, axis=0))

    pl.semaphore_wait(barrier, len(UP + DOWN))
    send(DOWN, 0)

    for c in range(2):
        loads[2 + c].wait()
        for part, value in enumerate(split(ham_raw[c])):
            half = jnp.dot(pick[c], value, preferred_element_type=F32).astype(BF16)
            whole = lax.dot_general(
                half, early_columns[c], (((1,), (1,)), ((), ())), preferred_element_type=F32
            ).astype(BF16)
            ham_early[c, part * ROWS : (part + 1) * ROWS, :] = whole
            whole = lax.dot_general(
                half, late_columns[c], (((1,), (1,)), ((), ())), preferred_element_type=F32
            ).astype(BF16)
            ham_sent[c, part * SENT : (part + 1) * SENT, :] = whole[:SENT]
            ham_inner[c, part * INNER : (part + 1) * INNER, :] = whole[SENT:]


    def four(matrix, value):
        rows = matrix.shape[0] // 2
        all_four = jnp.dot(matrix, value, preferred_element_type=F32)
        return (
            all_four[:rows, :STATES]
            + (all_four[:rows, STATES:] + all_four[rows:, :STATES])
            + all_four[rows:, STATES:]
        )

    def join(ref, first, count):
        upper, lower = pl.ds(first + 7, count, stride=8), pl.ds(first, count, stride=8)
        middle = ref[0, upper, :] + ref[1, lower, :]
        ref[0, upper, :] = middle
        ref[1, lower, :] = middle

    def pair(parts):
        return jnp.concatenate(split(jnp.concatenate(parts, axis=0)), axis=1)

    def y_rows(now, c, y):
        return [
            field[now, c, pl.ds(pl.multiple_of(x * 64 + y * 8, 8), 8), :]
            for x in range(1, NPE - 1)
        ]

    def multiply_early(now):
        for c in range(2):
            parts = [field[now, c, x * 64 + 8 : x * 64 + 56, :] for x in range(1, NPE - 1)]
            parts += y_rows(now, c, near_y) + [jnp.zeros((48, STATES), F32)]
            early[c] = four(ham_early[c], pair(parts))

    def late_values(now, c):
        parts = [field[now, c, 0:64, :], field[now, c, 448:512, :]]
        parts += y_rows(now, c, 7 - near_y)
        parts += [field[now, c, pl.ds(64 + 7 * c, 48, stride=8), :]]
        return pair(parts + [jnp.zeros((32, STATES), F32)])

    def apply(now, directions, factor, keep):
        later = slot = 1 - now
        gain, shift = factor / HALF_WIDTH, -factor * CENTER / HALF_WIDTH
        values = [late_values(now, c) for c in range(2)]
        products = []
        for c in range(2):
            products.append(early[c, :SENT, :] + four(ham_sent[c], values[c]))
            rims[c] = products[c][:64]
        pack_yz()
        first = [d for d in directions if kind_of(d) in ("xz", "yz", "xyz")]
        send(first, slot)
        for c in range(2):
            faces[c, Y_ROWS : Y_ROWS + 128, :] = products[c][64:192]
            for t in range(2):
                row = X_ROWS + t * 64
                faces[c, row + 8 : row + 56, :] = products[c][192 + t * 48 : 240 + t * 48]
                for u in range(2):
                    edge = products[c][64 + u * 64 + t * 56 : 72 + u * 64 + t * 56]
                    faces[c, row + u * 56 : row + u * 56 + 8, :] = edge
        join(faces, 0, 32)
        send([d for d in directions if d not in first], slot)
        for c in range(2):
            inner[c, :INNER, :] = early[c, SENT:, :] + four(ham_inner[c], values[c])
        join(inner, 0, 36)

        def advance(c, row, count, products):
            rows = slice(row, row + count)
            fresh = gain * products + shift * field[now, c, rows, :]
            if keep:
                fresh = fresh - field[later, c, rows, :]
            field[later, c, rows, :] = fresh

        for c in range(2):
            for x in range(NPE):
                if x in (0, NPE - 1):
                    first = X_ROWS + 64 * (x // 7)
                    advance(c, x * 64, 64, faces[c, first : first + 64, :])
                    continue
                for t in range(2):
                    first = Y_ROWS + 64 * t + x * 8
                    advance(c, x * 64 + 56 * t, 8, faces[c, first : first + 8, :])
                first = (x - 1) * 48
                advance(c, x * 64 + 8, 48, inner[c, first : first + 48, :])
        total = field.at[later]
        if directions is ALL:
            collect_y(total, slot, near_place, gain)
            multiply_early(later)
            wait_sent(directions, slot)
            collect(total, [d for d in ALL if kind_of(d) != "y"], slot, gain)
            collect_y(total, slot, 1 - near_place, gain)
        else:
            wait_sent(directions, slot)
            collect(total, directions, slot, gain)

    @pl.when(near_place == 0)
    def _():
        collect_y(field.at[0], 0, 0, 1.0)

    multiply_early(0)
    wait_sent(DOWN, 0)
    collect(field.at[0], [d for d in DOWN if kind_of(d) != "y"], 0, 1.0)

    @pl.when(near_place == 1)
    def _():
        collect_y(field.at[0], 0, 0, 1.0)

    apply(0, ALL, 1.0, False)

    def two_steps(k, carry):
        apply(1, ALL, 2.0, True)
        apply(0, ALL, 2.0, True)
        return carry

    lax.fori_loop(0, (DEGREE - 2) // 2, two_steps, 0)
    apply(1, UP, 2.0, True)
    last = 0

    owned_z = lax.broadcasted_iota(jnp.int32, (7 * 8, STATES), 0) % 8 < 7
    blocks = []
    for c in range(2):
        for x in range(NPE - 1):
            block = field[last, c, x * 64 : x * 64 + 56, :]
            blocks.append(jnp.where(owned_z, block, 0.0))
    columns = jnp.concatenate(blocks, axis=0)
    high, low = split(columns)
    both = lax.dot_general(
        high,
        jnp.concatenate([high, low], axis=1),
        (((0,), (0,)), ((), ())),
        preferred_element_type=F32,
    )
    cross = both[:, STATES:]
    gram[...] = both[:, :STATES] + (cross + cross.T)

    piece = STATES // ring
    mine = pl.ds(pl.multiple_of(ring_place * piece, piece), piece)

    def scatter(k, j):
        device, place = in_ring(j)
        rows = pl.ds(pl.multiple_of(place * piece, piece), piece)
        return pltpu.make_async_remote_copy(
            src_ref=gram.at[rows],
            dst_ref=r_scatter.at[k],
            send_sem=sum_send.at[0],
            recv_sem=sum_recv.at[0],
            device_id=device,
            device_id_type=MESH,
        )

    def reduce(j):
        return pltpu.make_async_remote_copy(
            src_ref=r_reduce.at[other_place],
            dst_ref=r_reduce.at[other_place],
            send_sem=sum_send.at[1],
            recv_sem=sum_recv.at[1],
            device_id=across(j),
            device_id_type=MESH,
        )

    def gather(j):
        return pltpu.make_async_remote_copy(
            src_ref=r_gather.at[mine],
            dst_ref=r_gather.at[mine],
            send_sem=sum_send.at[2],
            recv_sem=sum_recv.at[2],
            device_id=in_ring(j)[0],
            device_id_type=MESH,
        )

    def waiter(ref, k):
        return pltpu.make_async_remote_copy(
            src_ref=ref,
            dst_ref=ref,
            send_sem=sum_send.at[k],
            recv_sem=sum_recv.at[k],
            device_id=neighbour((1, 0, 0)),
            device_id_type=MESH,
        )

    for k, j in enumerate(turns(nx, 2)):
        scatter(k, j).start()
    waiter(r_scatter, 0).wait_recv()
    r_reduce[other_place] = gram[mine, :] + jnp.sum(r_scatter[...], axis=0)
    for j in turns(4, 4):
        reduce(j).start()
    waiter(r_scatter, 0).wait_send()
    waiter(r_reduce.at[pl.ds(0, others - 1)], 1).wait_recv()
    nodes = 686 * nx * ny * nz
    r_gather[mine, :] = jnp.sum(r_reduce[...], axis=0) * (1.0 / nodes)
    for j in turns(nx, 2):
        gather(j).start()
    waiter(r_reduce.at[pl.ds(0, others - 1)], 1).wait_send()
    rest = r_gather.at[pl.ds(0, piece * (ring - 1))]
    waiter(rest, 2).wait_recv()

    total = r_gather[...]
    diagonal = lax.broadcasted_iota(jnp.int32, (STATES, STATES), 0) == (
        lax.broadcasted_iota(jnp.int32, (STATES, STATES), 1)
    )
    trace = jnp.sum(jnp.where(diagonal, total, 0.0), keepdims=True)
    three = jnp.where(diagonal, 3.0, 0.0)

    def newton(k, pair):
        root, inverse = pair
        middle = three - product(inverse, root)
        return 0.5 * product(root, middle), 0.5 * product(middle, inverse)

    scaled = total / trace
    middle = three - scaled
    root, inverse = lax.fori_loop(
        0, NS_STEPS - 2, newton, (0.5 * product(scaled, middle), 0.5 * middle)
    )
    inverse = 0.5 * product(three - product(inverse, root), inverse)
    rotation = inverse / jnp.sqrt(trace)
    for c in range(2):
        for x in range(NPE - 1):
            turned = product(field[last, c, x * 64 : x * 64 + 56, :], rotation)
            for y in range(NPE - 1):
                out_ref[x, y, c * 7 : c * 7 + 7, :] = turned[y * 8 : y * 8 + 7, :]
    waiter(rest, 2).wait_send()


def shards(wavefunctions, hamiltonians, cell_order):
    sizes = tuple(lax.axis_size(a) for a in AXES)
    ring, others = sizes[0] * 2, sizes[1] // 2 * sizes[2]
    piece = STATES // ring
    matrices = hamiltonians.reshape((2, CDOF, CDOF))
    orders = cell_order.reshape((2, CDOF))
    kinds = len(KINDS)
    return pl.pallas_call(
        functools.partial(kernel, sizes),
        out_shape=pltpu.VMEM(wavefunctions.shape, F32),
        in_specs=[pl.BlockSpec(memory_space=pltpu.HBM)] * 3,
        out_specs=pl.BlockSpec(memory_space=pltpu.VMEM),
        scratch_shapes=[
            pltpu.VMEM(wavefunctions.shape, F32),
            pltpu.VMEM((2, CDOF, CDOF), F32),
            pltpu.VMEM((2, ROWS, CDOF), BF16),
            pltpu.VMEM((2, EARLY, CDOF), BF16),
            pltpu.VMEM((2, LATE, CDOF), BF16),
            pltpu.VMEM((2, CDOF), jnp.int32),
            pltpu.VMEM((2, 2 * ROWS, EARLY), BF16),
            pltpu.VMEM((2, 2 * SENT, LATE), BF16),
            pltpu.VMEM((2, 2 * INNER, LATE), BF16),
            pltpu.VMEM((2, ROWS, STATES), F32),
            pltpu.VMEM((2, 2, CDOF, STATES), F32),
            pltpu.VMEM((2, 64, STATES), F32),
            pltpu.VMEM((2, 256, STATES), F32),
            pltpu.VMEM((2, INNER + 32, STATES), F32),
            pltpu.VMEM((2, 2, 8, STATES), F32),
            pltpu.VMEM((2, 2, 2, 64, STATES), F32),
            pltpu.VMEM((2, 2, 2, 64, STATES), F32),
            pltpu.VMEM((2, 2, 64, STATES), F32),
            pltpu.VMEM((2, 4, 2, 8, STATES), F32),
            pltpu.VMEM((2, 4, 8, STATES), F32),
            pltpu.VMEM((2, 4, 8, STATES), F32),
            pltpu.VMEM((2, 8, STATES), F32),
            pltpu.VMEM((STATES, STATES), F32),
            pltpu.VMEM((ring - 1, piece, STATES), F32),
            pltpu.VMEM((others, piece, STATES), F32),
            pltpu.VMEM((STATES, STATES), F32),
            pltpu.SemaphoreType.DMA((4,)),
            pltpu.SemaphoreType.DMA((kinds,)),
            pltpu.SemaphoreType.DMA((2, 2 + kinds)),
            pltpu.SemaphoreType.DMA((3,)),
            pltpu.SemaphoreType.DMA((3,)),
        ],
        compiler_params=pltpu.CompilerParams(
            collective_id=0, has_side_effects=True, vmem_limit_bytes=56 << 20
        ),
    )(wavefunctions, matrices, orders)


def solution(mesh):
    in_specs = (
        P("gx", "gy", "gz", None),
        P("gx", "gy", "gz", None, None),
        P("gx", "gy", "gz", None),
    )
    out_specs = P("gx", "gy", "gz", None)
    return jax.shard_map(
        shards, mesh=mesh, in_specs=in_specs, out_specs=out_specs, check_vma=False
    )
```

```python
import functools
import itertools

import jax
import jax.numpy as jnp
from jax import lax
from jax.experimental import pallas as pl
from jax.experimental.pallas import tpu as pltpu
from jax.sharding import PartitionSpec as P

NPE = 8
CDOF = 512
STATES = 128
DEGREE = 6
NS_STEPS = 12
CENTER = 0.4
HALF_WIDTH = 0.7
AXES = ("gx", "gy", "gz")
MESH = pl.DeviceIdType.MESH
F32 = jnp.float32
BF16 = jnp.bfloat16

ALL = sorted(
    (d for d in itertools.product((-1, 0, 1), repeat=3) if any(d)),
    key=lambda d: -sum(map(abs, d)),
)
NEAR, FAR = 1, 2
CODED = sorted(
    (d for d in itertools.product((-1, 0, 1), (0, NEAR, FAR), (-1, 0, 1)) if any(d)),
    key=lambda d: (-sum(map(bool, d)), (1, 2, 0)[d[1]]),
)
DOWN = [d for d in ALL if max(d) <= 0]
UP = [d for d in ALL if min(d) >= 0]

KINDS = ("x", "z", "xz", "y", "xy", "yz", "xyz")
Y_ROWS, X_ROWS = 0, 128
INNER = 36 * 8
SENT = 64 + 128 + 96
ROWS = SENT + INNER
EARLY, LATE = 384, 256


def split(value):
    high = value.astype(BF16)
    low = (value - high.astype(F32)).astype(BF16)
    return high, low


def product(left, right):
    columns = right.shape[1]
    high, low = split(right)
    upper = jnp.concatenate([high, low], axis=1)
    lower = jnp.concatenate([high, jnp.zeros_like(low)], axis=1)
    sums = jnp.dot(
        jnp.concatenate(split(left), axis=1),
        jnp.concatenate([upper, lower], axis=0),
        preferred_element_type=F32,
    )
    return sums[:, :columns] + sums[:, columns:]


def side(step):
    return (step + 1) // 2


def kind_of(d):
    return "".join(name for name, step in zip("xyz", d) if step)


def kernel(
    sizes,
    wave_hbm,
    ham_hbm,
    order_hbm,
    out_ref,
    wave_ref,
    ham_raw,
    pick,
    early_columns,
    late_columns,
    order_ref,
    ham_early,
    ham_sent,
    ham_inner,
    early,
    field,
    rims,
    faces,
    inner,
    yz_pack,
    r_x,
    r_y,
    r_z,
    r_xy,
    r_xz,
    r_yz,
    r_xyz,
    parts,
    gram,
    r_scatter,
    r_reduce,
    r_gather,
    load_sem,
    send_sem,
    recv_sem,
    sum_send,
    sum_recv,
):
    me = tuple(lax.axis_index(a) for a in AXES)
    nx, ny, nz = sizes
    received = dict(x=r_x, y=r_y, z=r_z, xy=r_xy, xz=r_xz, yz=r_yz, xyz=r_xyz)

    shifted = [
        {s: lax.rem(m + (s + n), n) for s in (-1, 0, 1)} for m, n in zip(me, sizes)
    ]
    neighbours = {
        d: tuple(table[s] for table, s in zip(shifted, d)) for d in ALL
    }

    core = lax.rem(me[1], 2)
    coded_y = {0: me[1], NEAR: me[1] + 1 - 2 * core, FAR: lax.rem(me[1] + 2 * core + 3, 4)}

    def neighbour(d):
        return neighbours[d]

    ring_place = me[0] * 2 + lax.rem(me[1], 2)
    other_place = (me[1] // 2) * nz + me[2]
    ring, others = nx * 2, (ny // 2) * nz

    def turns(*lengths):
        shifts = [j for j in itertools.product(*map(range, lengths)) if any(j)]
        return sorted(shifts, key=lambda j: -sum(min(i, n - i) for i, n in zip(j, lengths)))

    def in_ring(j):
        x = lax.rem(me[0] + j[0], nx)
        core = lax.rem(me[1] + j[1], 2)
        return (x, (me[1] // 2) * 2 + core, me[2]), x * 2 + core

    def across(j):
        y = lax.rem((me[1] // 2) * 2 + me[2] // 4 + j[0], 4)
        z = lax.rem(y, 2) * 4 + lax.rem(me[2] + j[1], 4)
        return (me[0], (y // 2) * 2 + lax.rem(me[1], 2), z)

    barrier = pltpu.get_barrier_semaphore()
    for d in UP + DOWN:
        pl.semaphore_signal(barrier, inc=1, device_id=neighbour(d), device_id_type=MESH)

    loads = [
        pltpu.make_async_copy(wave_hbm, wave_ref, load_sem.at[0]),
        pltpu.make_async_copy(order_hbm, order_ref, load_sem.at[1]),
        pltpu.make_async_copy(ham_hbm.at[0], ham_raw.at[0], load_sem.at[2]),
        pltpu.make_async_copy(ham_hbm.at[1], ham_raw.at[1], load_sem.at[3]),
    ]
    for load in loads:
        load.start()

    def message(d, slot, coded):
        dx, dy, dz = d
        kind = kind_of(d)
        sx, sy, sz = side(dx), side(dy), side(dz)
        device = neighbours[d] if not coded else (shifted[0][dx], coded_y[dy], shifted[2][dz])
        if coded and dy:
            sy = core if dy == FAR else 1 - core
        if kind == "x":
            source, place = faces.at[:, pl.ds(X_ROWS + sx * 64, 64)], sx
        elif kind == "y":
            source, place = faces.at[:, pl.ds(Y_ROWS + sy * 64, 64)], sy
        elif kind == "z":
            source, place = rims.at[sz, pl.ds(0, 64)], sz
        elif kind == "xy":
            source = faces.at[:, pl.ds(X_ROWS + sx * 64 + sy * 56, 8)]
            place = sx * 2 + sy
        elif kind == "xz":
            source = rims.at[sz, pl.ds(sx * 56, 8)]
            place = sx * 2 + sz
        elif kind == "yz":
            source, place = yz_pack.at[sy, sz], sy * 2 + sz
        else:
            source = rims.at[sz, pl.ds(sx * 56 + sy * 7, 1)]
            place = sx * 4 + sy * 2 + sz
        if kind == "xyz":
            target = r_xyz.at[slot, pl.ds(place, 1)]
        else:
            target = received[kind].at[slot, place]
        k = KINDS.index(kind)
        return pltpu.make_async_remote_copy(
            src_ref=source,
            dst_ref=target,
            send_sem=send_sem.at[k],
            recv_sem=recv_sem.at[slot, place if kind == "y" else 2 + k],
            device_id=device,
            device_id_type=MESH,
        )

    def send(directions, slot, coded=False):
        for d in directions:
            message(d, slot, coded).start()

    def every(kind, directions, slot):
        count = sum(kind_of(d) == kind for d in directions)
        whole = received[kind].at[slot, pl.ds(0, count)]
        k = KINDS.index(kind)
        return pltpu.make_async_remote_copy(
            src_ref=whole,
            dst_ref=whole,
            send_sem=send_sem.at[k],
            recv_sem=recv_sem.at[slot, 2 + k],
            device_id=neighbour((1, 0, 0)),
            device_id_type=MESH,
        )

    def wait_sent(directions, slot):
        for kind in KINDS:
            every(kind, directions, slot).wait_send()

    def collect_y(total, slot, place, scale):
        pltpu.make_async_remote_copy(
            src_ref=r_y.at[slot, place],
            dst_ref=r_y.at[slot, place],
            send_sem=send_sem.at[KINDS.index("y")],
            recv_sem=recv_sem.at[slot, place],
            device_id=neighbour((1, 0, 0)),
            device_id_type=MESH,
        ).wait_recv()
        for x in range(NPE):
            rows = pl.ds(pl.multiple_of(x * 64 + 56 * (1 - place), 8), 8)
            total[:, rows, :] += scale * r_y[slot, place, :, x * 8 : x * 8 + 8, :]

    def collect(total, directions, slot, scale):
        for kind in KINDS:
            if kind == "y":
                for d in directions:
                    if kind_of(d) == "y":
                        collect_y(total, slot, side(d[1]), scale)
                continue
            every(kind, directions, slot).wait_recv()
            for dx, dy, dz in directions:
                if kind_of((dx, dy, dz)) != kind:
                    continue
                sx, sy, sz = side(dx), side(dy), side(dz)
                ix, iy = 7 * (1 - sx), 7 * (1 - sy)
                c, iz = (0, 0) if dz > 0 else (1, 7)
                if kind == "x":
                    total[:, ix * 64 : ix * 64 + 64, :] += scale * r_x[slot, sx]
                elif kind == "xy":
                    row = (ix * NPE + iy) * NPE
                    total[:, row : row + 8, :] += scale * r_xy[slot, sx * 2 + sy]
                elif kind == "z":
                    total[c, pl.ds(iz, 64, stride=8), :] += scale * r_z[slot, sz]
                elif kind == "xz":
                    rows = pl.ds(ix * 64 + iz, 8, stride=8)
                    total[c, rows, :] += scale * r_xz[slot, sx * 2 + sz]
                elif kind == "yz":
                    rows = pl.ds(iy * 8 + iz, 8, stride=64)
                    total[c, rows, :] += scale * r_yz[slot, sy * 2 + sz]
                else:
                    row = (ix * NPE + iy) * NPE + iz
                    place = sx * 4 + sy * 2 + sz
                    total[c, row : row + 1, :] += scale * r_xyz[slot, place : place + 1, :]

    def pack_yz():
        for s in range(2):
            for t in range(2):
                yz_pack[t, s] = rims[s, pl.ds(7 * t, 8, stride=8), :]

    loads[0].wait()
    field[0] = jnp.zeros((2, CDOF, STATES), F32)
    for x in range(NPE - 1):
        for y in range(NPE - 1):
            row = (x * NPE + y) * NPE
            field[0, 0, row : row + 8, :] = wave_ref[x, y, 0:8, :]
            field[0, 1, row : row + 7, :] = wave_ref[x, y, 7:14, :]
    rims[0] = field[0, 0, pl.ds(0, 64, stride=8), :]
    for c in range(2):
        faces[c, X_ROWS : X_ROWS + 64, :] = field[0, c, 0:64, :]
        for x in range(NPE):
            faces[c, Y_ROWS + x * 8 : Y_ROWS + x * 8 + 8, :] = field[0, c, x * 64 : x * 64 + 8, :]
    yz_pack[0, 0] = rims[0, pl.ds(0, 8, stride=8), :]
    loads[1].wait()
    near_place = lax.rem(me[1], 2)
    near_y = 7 * (1 - near_place)
    lanes = 128
    row_of = lax.broadcasted_iota(jnp.int32, (CDOF, lanes), 0)
    n, k = row_of[:64], row_of[:48]
    none = jnp.full((48, lanes), -1, jnp.int32)
    for c in range(2):
        order = order_ref[c : c + 1, :]

        def chosen(rows):
            return jnp.concatenate(
                [
                    (rows == order[:, first : first + lanes]).astype(F32).astype(BF16)
                    for first in range(0, CDOF, lanes)
                ],
                axis=1,
            )

        block = (n >> 3) * 64 + (n & 7)
        rows = [n * 8 + 7 * c, block, block + 56, n[8:56], n[8:56] + 448]
        rows += [row_of[x * 64 + 8 : x * 64 + 56] for x in range(1, NPE - 1)]
        pick[c] = chosen(jnp.concatenate(rows, axis=0))
        near_rows = ((k >> 3) + 1) * 64 + near_y * 8 + (k & 7)
        early_rows = [row_of[x * 64 + 8 : x * 64 + 56] for x in range(1, NPE - 1)]
        early_rows = [
            jnp.where((k & 7) == 7 * c, -1, rows) for rows in early_rows + [near_rows]
        ] + [none]
        rim_rows = ((k >> 3) + 1) * 64 + (k & 7) * 8 + 7 * c
        late_rows = [
            n,
            n + 448,
            ((k >> 3) + 1) * 64 + (7 - near_y) * 8 + (k & 7),
            jnp.where((k & 7) == 7 - near_y, -1, rim_rows),
            none[:32],
        ]
        early_columns[c] = chosen(jnp.concatenate(early_rows, axis=0))
        late_columns[c] = chosen(jnp.concatenate(late_rows, axis=0))

    pl.semaphore_wait(barrier, len(UP + DOWN))
    send(DOWN, 0)

    for c in range(2):
        loads[2 + c].wait()
        for part, value in enumerate(split(ham_raw[c])):
            half = jnp.dot(pick[c], value, preferred_element_type=F32).astype(BF16)
            whole = lax.dot_general(
                half, early_columns[c], (((1,), (1,)), ((), ())), preferred_element_type=F32
            ).astype(BF16)
            ham_early[c, part * ROWS : (part + 1) * ROWS, :] = whole
            whole = lax.dot_general(
                half, late_columns[c], (((1,), (1,)), ((), ())), preferred_element_type=F32
            ).astype(BF16)
            ham_sent[c, part * SENT : (part + 1) * SENT, :] = whole[:SENT]
            ham_inner[c, part * INNER : (part + 1) * INNER, :] = whole[SENT:]


    def four(matrix, value):
        rows = matrix.shape[0] // 2
        all_four = jnp.dot(matrix, value, preferred_element_type=F32)
        return (
            all_four[:rows, :STATES]
            + (all_four[:rows, STATES:] + all_four[rows:, :STATES])
            + all_four[rows:, STATES:]
        )

    def join(ref, first, count):
        upper, lower = pl.ds(first + 7, count, stride=8), pl.ds(first, count, stride=8)
        middle = ref[0, upper, :] + ref[1, lower, :]
        ref[0, upper, :] = middle
        ref[1, lower, :] = middle

    def pair(parts):
        return jnp.concatenate(split(jnp.concatenate(parts, axis=0)), axis=1)

    def y_rows(now, c, y):
        return [
            field[now, c, pl.ds(pl.multiple_of(x * 64 + y * 8, 8), 8), :]
            for x in range(1, NPE - 1)
        ]

    def multiply_early(now):
        for c in range(2):
            parts = [field[now, c, x * 64 + 8 : x * 64 + 56, :] for x in range(1, NPE - 1)]
            parts += y_rows(now, c, near_y) + [jnp.zeros((48, STATES), F32)]
            early[c] = four(ham_early[c], pair(parts))

    def late_values(now, c):
        parts = [field[now, c, 0:64, :], field[now, c, 448:512, :]]
        parts += y_rows(now, c, 7 - near_y)
        parts += [field[now, c, pl.ds(64 + 7 * c, 48, stride=8), :]]
        return pair(parts + [jnp.zeros((32, STATES), F32)])

    def apply(now, directions, factor, keep):
        later = slot = 1 - now
        gain, shift = factor / HALF_WIDTH, -factor * CENTER / HALF_WIDTH
        values = [late_values(now, c) for c in range(2)]
        products = []
        for c in range(2):
            products.append(early[c, :SENT, :] + four(ham_sent[c], values[c]))
            rims[c] = products[c][:64]
        pack_yz()
        coded = directions is ALL
        order = CODED if coded else directions
        first = [d for d in order if kind_of(d) in ("xz", "yz", "xyz")]
        send(first, slot, coded)
        for c in range(2):
            faces[c, Y_ROWS : Y_ROWS + 128, :] = products[c][64:192]
            for t in range(2):
                row = X_ROWS + t * 64
                faces[c, row + 8 : row + 56, :] = products[c][192 + t * 48 : 240 + t * 48]
                for u in range(2):
                    edge = products[c][64 + u * 64 + t * 56 : 72 + u * 64 + t * 56]
                    faces[c, row + u * 56 : row + u * 56 + 8, :] = edge
        join(faces, 0, 32)
        send([d for d in order if d not in first], slot, coded)
        for c in range(2):
            inner[c, :INNER, :] = early[c, SENT:, :] + four(ham_inner[c], values[c])
        join(inner, 0, 36)

        def advance(c, row, count, products):
            rows = slice(row, row + count)
            fresh = gain * products + shift * field[now, c, rows, :]
            if keep:
                fresh = fresh - field[later, c, rows, :]
            field[later, c, rows, :] = fresh

        for c in range(2):
            for x in range(NPE):
                if x in (0, NPE - 1):
                    first = X_ROWS + 64 * (x // 7)
                    advance(c, x * 64, 64, faces[c, first : first + 64, :])
                    continue
                for t in range(2):
                    first = Y_ROWS + 64 * t + x * 8
                    advance(c, x * 64 + 56 * t, 8, faces[c, first : first + 8, :])
                first = (x - 1) * 48
                advance(c, x * 64 + 8, 48, inner[c, first : first + 48, :])
        total = field.at[later]
        if directions is ALL:
            collect_y(total, slot, near_place, gain)
            multiply_early(later)
            wait_sent(directions, slot)
            collect(total, [d for d in ALL if kind_of(d) != "y"], slot, gain)
            collect_y(total, slot, 1 - near_place, gain)
        else:
            wait_sent(directions, slot)
            collect(total, directions, slot, gain)

    @pl.when(near_place == 0)
    def _():
        collect_y(field.at[0], 0, 0, 1.0)

    multiply_early(0)
    wait_sent(DOWN, 0)
    collect(field.at[0], [d for d in DOWN if kind_of(d) != "y"], 0, 1.0)

    @pl.when(near_place == 1)
    def _():
        collect_y(field.at[0], 0, 0, 1.0)

    apply(0, ALL, 1.0, False)

    def two_steps(k, carry):
        apply(1, ALL, 2.0, True)
        apply(0, ALL, 2.0, True)
        return carry

    lax.fori_loop(0, (DEGREE - 2) // 2, two_steps, 0)
    apply(1, UP, 2.0, True)
    last = 0

    owned_z = lax.broadcasted_iota(jnp.int32, (7 * 8, STATES), 0) % 8 < 7
    blocks = []
    for c in range(2):
        for x in range(NPE - 1):
            block = field[last, c, x * 64 : x * 64 + 56, :]
            blocks.append(jnp.where(owned_z, block, 0.0))
    columns = jnp.concatenate(blocks, axis=0)
    high, low = split(columns)
    parts[...] = jnp.concatenate([high, low], axis=1)
    both = lax.dot_general(
        high,
        parts[...],
        (((0,), (0,)), ((), ())),
        preferred_element_type=F32,
    )
    cross = both[:, STATES:]
    gram[...] = both[:, :STATES] + (cross + cross.T)

    piece = STATES // ring
    mine = pl.ds(pl.multiple_of(ring_place * piece, piece), piece)

    def scatter(k, j):
        device, place = in_ring(j)
        rows = pl.ds(pl.multiple_of(place * piece, piece), piece)
        return pltpu.make_async_remote_copy(
            src_ref=gram.at[rows],
            dst_ref=r_scatter.at[k],
            send_sem=sum_send.at[0],
            recv_sem=sum_recv.at[0],
            device_id=device,
            device_id_type=MESH,
        )

    def reduce(j):
        return pltpu.make_async_remote_copy(
            src_ref=r_reduce.at[other_place],
            dst_ref=r_reduce.at[other_place],
            send_sem=sum_send.at[1],
            recv_sem=sum_recv.at[1],
            device_id=across(j),
            device_id_type=MESH,
        )

    def gather(j):
        return pltpu.make_async_remote_copy(
            src_ref=r_gather.at[mine],
            dst_ref=r_gather.at[mine],
            send_sem=sum_send.at[2],
            recv_sem=sum_recv.at[2],
            device_id=in_ring(j)[0],
            device_id_type=MESH,
        )

    def waiter(ref, k):
        return pltpu.make_async_remote_copy(
            src_ref=ref,
            dst_ref=ref,
            send_sem=sum_send.at[k],
            recv_sem=sum_recv.at[k],
            device_id=neighbour((1, 0, 0)),
            device_id_type=MESH,
        )

    for k, j in enumerate(turns(nx, 2)):
        scatter(k, j).start()
    waiter(r_scatter, 0).wait_recv()
    r_reduce[other_place] = gram[mine, :] + jnp.sum(r_scatter[...], axis=0)
    for j in turns(4, 4):
        reduce(j).start()
    waiter(r_scatter, 0).wait_send()
    waiter(r_reduce.at[pl.ds(0, others - 1)], 1).wait_recv()
    nodes = 686 * nx * ny * nz
    r_gather[mine, :] = jnp.sum(r_reduce[...], axis=0) * (1.0 / nodes)
    for j in turns(nx, 2):
        gather(j).start()
    waiter(r_reduce.at[pl.ds(0, others - 1)], 1).wait_send()
    rest = r_gather.at[pl.ds(0, piece * (ring - 1))]
    waiter(rest, 2).wait_recv()

    total = r_gather[...]
    diagonal = lax.broadcasted_iota(jnp.int32, (STATES, STATES), 0) == (
        lax.broadcasted_iota(jnp.int32, (STATES, STATES), 1)
    )
    trace = jnp.sum(jnp.where(diagonal, total, 0.0), keepdims=True)
    three = jnp.where(diagonal, 3.0, 0.0)

    def newton(k, pair):
        root, inverse = pair
        middle = three - product(inverse, root)
        return 0.5 * product(root, middle), 0.5 * product(middle, inverse)

    scaled = total / trace
    middle = three - scaled
    root, inverse = lax.fori_loop(
        0, NS_STEPS - 2, newton, (0.5 * product(scaled, middle), 0.5 * middle)
    )
    inverse = 0.5 * product(three - product(inverse, root), inverse)
    high, low = split(inverse / jnp.sqrt(trace))
    upper = jnp.concatenate([high, low], axis=1)
    lower = jnp.concatenate([high, jnp.zeros_like(low)], axis=1)
    both = jnp.dot(
        parts[...], jnp.concatenate([upper, lower], axis=0), preferred_element_type=F32
    )
    turned = both[:, :STATES] + both[:, STATES:]
    for c in range(2):
        for x in range(NPE - 1):
            for y in range(NPE - 1):
                row = ((c * 7 + x) * 7 + y) * 8
                out_ref[x, y, c * 7 : c * 7 + 7, :] = turned[row : row + 7]
    waiter(rest, 2).wait_send()


def shards(wavefunctions, hamiltonians, cell_order):
    sizes = tuple(lax.axis_size(a) for a in AXES)
    ring, others = sizes[0] * 2, sizes[1] // 2 * sizes[2]
    piece = STATES // ring
    matrices = hamiltonians.reshape((2, CDOF, CDOF))
    orders = cell_order.reshape((2, CDOF))
    kinds = len(KINDS)
    return pl.pallas_call(
        functools.partial(kernel, sizes),
        out_shape=pltpu.VMEM(wavefunctions.shape, F32),
        in_specs=[pl.BlockSpec(memory_space=pltpu.HBM)] * 3,
        out_specs=pl.BlockSpec(memory_space=pltpu.VMEM),
        scratch_shapes=[
            pltpu.VMEM(wavefunctions.shape, F32),
            pltpu.VMEM((2, CDOF, CDOF), F32),
            pltpu.VMEM((2, ROWS, CDOF), BF16),
            pltpu.VMEM((2, EARLY, CDOF), BF16),
            pltpu.VMEM((2, LATE, CDOF), BF16),
            pltpu.VMEM((2, CDOF), jnp.int32),
            pltpu.VMEM((2, 2 * ROWS, EARLY), BF16),
            pltpu.VMEM((2, 2 * SENT, LATE), BF16),
            pltpu.VMEM((2, 2 * INNER, LATE), BF16),
            pltpu.VMEM((2, ROWS, STATES), F32),
            pltpu.VMEM((2, 2, CDOF, STATES), F32),
            pltpu.VMEM((2, 64, STATES), F32),
            pltpu.VMEM((2, 256, STATES), F32),
            pltpu.VMEM((2, INNER + 32, STATES), F32),
            pltpu.VMEM((2, 2, 8, STATES), F32),
            pltpu.VMEM((2, 2, 2, 64, STATES), F32),
            pltpu.VMEM((2, 2, 2, 64, STATES), F32),
            pltpu.VMEM((2, 2, 64, STATES), F32),
            pltpu.VMEM((2, 4, 2, 8, STATES), F32),
            pltpu.VMEM((2, 4, 8, STATES), F32),
            pltpu.VMEM((2, 4, 8, STATES), F32),
            pltpu.VMEM((2, 8, STATES), F32),
            pltpu.VMEM((2 * 7 * 7 * 8, 2 * STATES), BF16),
            pltpu.VMEM((STATES, STATES), F32),
            pltpu.VMEM((ring - 1, piece, STATES), F32),
            pltpu.VMEM((others, piece, STATES), F32),
            pltpu.VMEM((STATES, STATES), F32),
            pltpu.SemaphoreType.DMA((4,)),
            pltpu.SemaphoreType.DMA((kinds,)),
            pltpu.SemaphoreType.DMA((2, 2 + kinds)),
            pltpu.SemaphoreType.DMA((3,)),
            pltpu.SemaphoreType.DMA((3,)),
        ],
        compiler_params=pltpu.CompilerParams(
            collective_id=0, has_side_effects=True, vmem_limit_bytes=56 << 20
        ),
    )(wavefunctions, matrices, orders)


def solution(mesh):
    in_specs = (
        P("gx", "gy", "gz", None),
        P("gx", "gy", "gz", None, None),
        P("gx", "gy", "gz", None),
    )
    out_specs = P("gx", "gy", "gz", None)
    return jax.shard_map(
        shards, mesh=mesh, in_specs=in_specs, out_specs=out_specs, check_vma=False
    )
```

```python
import functools
import itertools

import jax
import jax.numpy as jnp
from jax import lax
from jax.experimental import pallas as pl
from jax.experimental.pallas import tpu as pltpu
from jax.sharding import PartitionSpec as P

NPE = 8
CDOF = 512
STATES = 128
DEGREE = 6
NS_STEPS = 12
CENTER = 0.4
HALF_WIDTH = 0.7
AXES = ("gx", "gy", "gz")
MESH = pl.DeviceIdType.MESH
F32 = jnp.float32
BF16 = jnp.bfloat16

ALL = sorted(
    (d for d in itertools.product((-1, 0, 1), repeat=3) if any(d)),
    key=lambda d: -sum(map(abs, d)),
)
NEAR, FAR = 1, 2
CODED = sorted(
    (d for d in itertools.product((-1, 0, 1), (0, NEAR, FAR), (-1, 0, 1)) if any(d)),
    key=lambda d: (-sum(map(bool, d)), (1, 2, 0)[d[1]]),
)
DOWN = [d for d in ALL if max(d) <= 0]
UP = [d for d in ALL if min(d) >= 0]

KINDS = ("x", "z", "y", "xz", "xy", "yz", "xyz")
SOON, LATER = KINDS[:2], KINDS[3:]
Y_ROWS, X_ROWS = 0, 128
INNER = 36 * 8
SENT = 64 + 128 + 96
ROWS = SENT + INNER
EARLY, LATE = 384, 256


def split(value):
    high = value.astype(BF16)
    low = (value - high.astype(F32)).astype(BF16)
    return high, low


def product(left, right):
    columns = right.shape[1]
    high, low = split(right)
    upper = jnp.concatenate([high, low], axis=1)
    lower = jnp.concatenate([high, jnp.zeros_like(low)], axis=1)
    sums = jnp.dot(
        jnp.concatenate(split(left), axis=1),
        jnp.concatenate([upper, lower], axis=0),
        preferred_element_type=F32,
    )
    return sums[:, :columns] + sums[:, columns:]


def side(step):
    return (step + 1) // 2


def kind_of(d):
    return "".join(name for name, step in zip("xyz", d) if step)


def kernel(
    sizes,
    wave_hbm,
    ham_hbm,
    order_hbm,
    out_ref,
    wave_ref,
    ham_raw,
    pick,
    early_columns,
    late_columns,
    order_ref,
    ham_early,
    ham_sent,
    ham_inner,
    early,
    field,
    rims,
    faces,
    inner,
    yz_pack,
    r_x,
    r_y,
    r_z,
    r_xy,
    r_xz,
    r_yz,
    r_xyz,
    parts,
    gram,
    r_scatter,
    r_reduce,
    r_gather,
    load_sem,
    send_sem,
    recv_sem,
    sum_send,
    sum_recv,
):
    me = tuple(lax.axis_index(a) for a in AXES)
    nx, ny, nz = sizes
    received = dict(x=r_x, y=r_y, z=r_z, xy=r_xy, xz=r_xz, yz=r_yz, xyz=r_xyz)

    shifted = [
        {s: lax.rem(m + (s + n), n) for s in (-1, 0, 1)} for m, n in zip(me, sizes)
    ]
    neighbours = {
        d: tuple(table[s] for table, s in zip(shifted, d)) for d in ALL
    }

    core = lax.rem(me[1], 2)
    coded_y = {0: me[1], NEAR: me[1] + 1 - 2 * core, FAR: lax.rem(me[1] + 2 * core + 3, 4)}

    def neighbour(d):
        return neighbours[d]

    ring_place = me[0] * 2 + lax.rem(me[1], 2)
    other_place = (me[1] // 2) * nz + me[2]
    ring, others = nx * 2, (ny // 2) * nz

    def turns(*lengths):
        shifts = [j for j in itertools.product(*map(range, lengths)) if any(j)]
        return sorted(shifts, key=lambda j: -sum(min(i, n - i) for i, n in zip(j, lengths)))

    def in_ring(j):
        x = lax.rem(me[0] + j[0], nx)
        core = lax.rem(me[1] + j[1], 2)
        return (x, (me[1] // 2) * 2 + core, me[2]), x * 2 + core

    def across(j):
        y = lax.rem((me[1] // 2) * 2 + me[2] // 4 + j[0], 4)
        z = lax.rem(y, 2) * 4 + lax.rem(me[2] + j[1], 4)
        return (me[0], (y // 2) * 2 + lax.rem(me[1], 2), z)

    barrier = pltpu.get_barrier_semaphore()
    for d in UP + DOWN:
        pl.semaphore_signal(barrier, inc=1, device_id=neighbour(d), device_id_type=MESH)

    loads = [
        pltpu.make_async_copy(wave_hbm, wave_ref, load_sem.at[0]),
        pltpu.make_async_copy(order_hbm, order_ref, load_sem.at[1]),
        pltpu.make_async_copy(ham_hbm.at[0], ham_raw.at[0], load_sem.at[2]),
        pltpu.make_async_copy(ham_hbm.at[1], ham_raw.at[1], load_sem.at[3]),
    ]
    for load in loads:
        load.start()

    def message(d, slot, coded):
        dx, dy, dz = d
        kind = kind_of(d)
        sx, sy, sz = side(dx), side(dy), side(dz)
        device = neighbours[d] if not coded else (shifted[0][dx], coded_y[dy], shifted[2][dz])
        if coded and dy:
            sy = core if dy == FAR else 1 - core
        if kind == "x":
            source, place = faces.at[:, pl.ds(X_ROWS + sx * 64, 64)], sx
        elif kind == "y":
            source, place = faces.at[:, pl.ds(Y_ROWS + sy * 64, 64)], sy
        elif kind == "z":
            source, place = rims.at[sz, pl.ds(0, 64)], sz
        elif kind == "xy":
            source = faces.at[:, pl.ds(X_ROWS + sx * 64 + sy * 56, 8)]
            place = sx * 2 + sy
        elif kind == "xz":
            source = rims.at[sz, pl.ds(sx * 56, 8)]
            place = sx * 2 + sz
        elif kind == "yz":
            source, place = yz_pack.at[sy, sz], sy * 2 + sz
        else:
            source = rims.at[sz, pl.ds(sx * 56 + sy * 7, 1)]
            place = sx * 4 + sy * 2 + sz
        if kind == "xyz":
            target = r_xyz.at[slot, pl.ds(place, 1)]
        else:
            target = received[kind].at[slot, place]
        k = KINDS.index(kind)
        return pltpu.make_async_remote_copy(
            src_ref=source,
            dst_ref=target,
            send_sem=send_sem.at[k],
            recv_sem=recv_sem.at[slot, place if kind == "y" else 2 + k],
            device_id=device,
            device_id_type=MESH,
        )

    def send(directions, slot, coded=False):
        for d in directions:
            message(d, slot, coded).start()

    def every(kind, directions, slot):
        count = sum(kind_of(d) == kind for d in directions)
        whole = received[kind].at[slot, pl.ds(0, count)]
        k = KINDS.index(kind)
        return pltpu.make_async_remote_copy(
            src_ref=whole,
            dst_ref=whole,
            send_sem=send_sem.at[k],
            recv_sem=recv_sem.at[slot, 2 + k],
            device_id=neighbour((1, 0, 0)),
            device_id_type=MESH,
        )

    def wait_sent(directions, slot):
        for kind in KINDS:
            every(kind, directions, slot).wait_send()

    def collect_y(total, slot, place, scale):
        pltpu.make_async_remote_copy(
            src_ref=r_y.at[slot, place],
            dst_ref=r_y.at[slot, place],
            send_sem=send_sem.at[KINDS.index("y")],
            recv_sem=recv_sem.at[slot, place],
            device_id=neighbour((1, 0, 0)),
            device_id_type=MESH,
        ).wait_recv()
        for x in range(NPE):
            rows = pl.ds(pl.multiple_of(x * 64 + 56 * (1 - place), 8), 8)
            total[:, rows, :] += scale * r_y[slot, place, :, x * 8 : x * 8 + 8, :]

    def collect(total, directions, slot, scale, kinds=KINDS):
        for kind in kinds:
            if kind == "y":
                for d in directions:
                    if kind_of(d) == "y":
                        collect_y(total, slot, side(d[1]), scale)
                continue
            every(kind, directions, slot).wait_recv()
            for dx, dy, dz in directions:
                if kind_of((dx, dy, dz)) != kind:
                    continue
                sx, sy, sz = side(dx), side(dy), side(dz)
                ix, iy = 7 * (1 - sx), 7 * (1 - sy)
                c, iz = (0, 0) if dz > 0 else (1, 7)
                if kind == "x":
                    total[:, ix * 64 : ix * 64 + 64, :] += scale * r_x[slot, sx]
                elif kind == "xy":
                    row = (ix * NPE + iy) * NPE
                    total[:, row : row + 8, :] += scale * r_xy[slot, sx * 2 + sy]
                elif kind == "z":
                    total[c, pl.ds(iz, 64, stride=8), :] += scale * r_z[slot, sz]
                elif kind == "xz":
                    rows = pl.ds(ix * 64 + iz, 8, stride=8)
                    total[c, rows, :] += scale * r_xz[slot, sx * 2 + sz]
                elif kind == "yz":
                    rows = pl.ds(iy * 8 + iz, 8, stride=64)
                    total[c, rows, :] += scale * r_yz[slot, sy * 2 + sz]
                else:
                    row = (ix * NPE + iy) * NPE + iz
                    place = sx * 4 + sy * 2 + sz
                    total[c, row : row + 1, :] += scale * r_xyz[slot, place : place + 1, :]

    def pack_yz():
        for s in range(2):
            for t in range(2):
                yz_pack[t, s] = rims[s, pl.ds(7 * t, 8, stride=8), :]

    loads[0].wait()
    field[0] = jnp.zeros((2, CDOF, STATES), F32)
    for x in range(NPE - 1):
        for y in range(NPE - 1):
            row = (x * NPE + y) * NPE
            field[0, 0, row : row + 8, :] = wave_ref[x, y, 0:8, :]
            field[0, 1, row : row + 7, :] = wave_ref[x, y, 7:14, :]
    rims[0] = field[0, 0, pl.ds(0, 64, stride=8), :]
    for c in range(2):
        faces[c, X_ROWS : X_ROWS + 64, :] = field[0, c, 0:64, :]
        for x in range(NPE):
            faces[c, Y_ROWS + x * 8 : Y_ROWS + x * 8 + 8, :] = field[0, c, x * 64 : x * 64 + 8, :]
    yz_pack[0, 0] = rims[0, pl.ds(0, 8, stride=8), :]
    loads[1].wait()
    near_place = lax.rem(me[1], 2)
    near_y = 7 * (1 - near_place)
    lanes = 128
    row_of = lax.broadcasted_iota(jnp.int32, (CDOF, lanes), 0)
    n, k = row_of[:64], row_of[:48]
    none = jnp.full((48, lanes), -1, jnp.int32)
    for c in range(2):
        order = order_ref[c : c + 1, :]

        def chosen(rows):
            return jnp.concatenate(
                [
                    (rows == order[:, first : first + lanes]).astype(F32).astype(BF16)
                    for first in range(0, CDOF, lanes)
                ],
                axis=1,
            )

        block = (n >> 3) * 64 + (n & 7)
        rows = [n * 8 + 7 * c, block, block + 56, n[8:56], n[8:56] + 448]
        rows += [row_of[x * 64 + 8 : x * 64 + 56] for x in range(1, NPE - 1)]
        pick[c] = chosen(jnp.concatenate(rows, axis=0))
        near_rows = ((k >> 3) + 1) * 64 + near_y * 8 + (k & 7)
        early_rows = [row_of[x * 64 + 8 : x * 64 + 56] for x in range(1, NPE - 1)]
        early_rows = [
            jnp.where((k & 7) == 7 * c, -1, rows) for rows in early_rows + [near_rows]
        ] + [none]
        rim_rows = ((k >> 3) + 1) * 64 + (k & 7) * 8 + 7 * c
        late_rows = [
            n,
            n + 448,
            ((k >> 3) + 1) * 64 + (7 - near_y) * 8 + (k & 7),
            jnp.where((k & 7) == 7 - near_y, -1, rim_rows),
            none[:32],
        ]
        early_columns[c] = chosen(jnp.concatenate(early_rows, axis=0))
        late_columns[c] = chosen(jnp.concatenate(late_rows, axis=0))

    pl.semaphore_wait(barrier, len(UP + DOWN))
    send(DOWN, 0)

    for c in range(2):
        loads[2 + c].wait()
        for part, value in enumerate(split(ham_raw[c])):
            half = jnp.dot(pick[c], value, preferred_element_type=F32).astype(BF16)
            whole = lax.dot_general(
                half, early_columns[c], (((1,), (1,)), ((), ())), preferred_element_type=F32
            ).astype(BF16)
            ham_early[c, part * ROWS : (part + 1) * ROWS, :] = whole
            whole = lax.dot_general(
                half, late_columns[c], (((1,), (1,)), ((), ())), preferred_element_type=F32
            ).astype(BF16)
            ham_sent[c, part * SENT : (part + 1) * SENT, :] = whole[:SENT]
            ham_inner[c, part * INNER : (part + 1) * INNER, :] = whole[SENT:]


    def four(matrix, value):
        rows = matrix.shape[0] // 2
        all_four = jnp.dot(matrix, value, preferred_element_type=F32)
        return (
            all_four[:rows, :STATES]
            + (all_four[:rows, STATES:] + all_four[rows:, :STATES])
            + all_four[rows:, STATES:]
        )

    def join(ref, first, count):
        upper, lower = pl.ds(first + 7, count, stride=8), pl.ds(first, count, stride=8)
        middle = ref[0, upper, :] + ref[1, lower, :]
        ref[0, upper, :] = middle
        ref[1, lower, :] = middle

    def pair(parts):
        return jnp.concatenate(split(jnp.concatenate(parts, axis=0)), axis=1)

    def y_rows(now, c, y):
        return [
            field[now, c, pl.ds(pl.multiple_of(x * 64 + y * 8, 8), 8), :]
            for x in range(1, NPE - 1)
        ]

    def multiply_early(now):
        for c in range(2):
            parts = [field[now, c, x * 64 + 8 : x * 64 + 56, :] for x in range(1, NPE - 1)]
            parts += y_rows(now, c, near_y) + [jnp.zeros((48, STATES), F32)]
            early[c] = four(ham_early[c], pair(parts))

    def late_values(now, c):
        parts = [field[now, c, 0:64, :], field[now, c, 448:512, :]]
        parts += y_rows(now, c, 7 - near_y)
        parts += [field[now, c, pl.ds(64 + 7 * c, 48, stride=8), :]]
        return pair(parts + [jnp.zeros((32, STATES), F32)])

    def apply(now, directions, factor, keep):
        later = slot = 1 - now
        gain, shift = factor / HALF_WIDTH, -factor * CENTER / HALF_WIDTH
        values = [late_values(now, c) for c in range(2)]
        products = []
        for c in range(2):
            products.append(early[c, :SENT, :] + four(ham_sent[c], values[c]))
            rims[c] = products[c][:64]
        pack_yz()
        coded = directions is ALL
        order = CODED if coded else directions
        first = [d for d in order if kind_of(d) in ("xz", "yz", "xyz")]
        send(first, slot, coded)
        for c in range(2):
            faces[c, Y_ROWS : Y_ROWS + 128, :] = products[c][64:192]
            for t in range(2):
                row = X_ROWS + t * 64
                faces[c, row + 8 : row + 56, :] = products[c][192 + t * 48 : 240 + t * 48]
                for u in range(2):
                    edge = products[c][64 + u * 64 + t * 56 : 72 + u * 64 + t * 56]
                    faces[c, row + u * 56 : row + u * 56 + 8, :] = edge
        join(faces, 0, 32)
        send([d for d in order if d not in first], slot, coded)
        for c in range(2):
            inner[c, :INNER, :] = early[c, SENT:, :] + four(ham_inner[c], values[c])
        join(inner, 0, 36)

        def advance(c, row, count, products):
            rows = slice(row, row + count)
            fresh = gain * products + shift * field[now, c, rows, :]
            if keep:
                fresh = fresh - field[later, c, rows, :]
            field[later, c, rows, :] = fresh

        for c in range(2):
            for x in range(NPE):
                if x in (0, NPE - 1):
                    first = X_ROWS + 64 * (x // 7)
                    advance(c, x * 64, 64, faces[c, first : first + 64, :])
                    continue
                for t in range(2):
                    first = Y_ROWS + 64 * t + x * 8
                    advance(c, x * 64 + 56 * t, 8, faces[c, first : first + 8, :])
                first = (x - 1) * 48
                advance(c, x * 64 + 8, 48, inner[c, first : first + 48, :])
        total = field.at[later]
        if directions is ALL:
            collect_y(total, slot, near_place, gain)
            multiply_early(later)
            wait_sent(directions, slot)
            collect(total, directions, slot, gain, SOON)
            collect_y(total, slot, 1 - near_place, gain)
            collect(total, directions, slot, gain, LATER)
        else:
            wait_sent(directions, slot)
            collect(total, directions, slot, gain)

    @pl.when(near_place == 0)
    def _():
        collect_y(field.at[0], 0, 0, 1.0)

    multiply_early(0)
    wait_sent(DOWN, 0)
    collect(field.at[0], DOWN, 0, 1.0, SOON)

    @pl.when(near_place == 1)
    def _():
        collect_y(field.at[0], 0, 0, 1.0)

    collect(field.at[0], DOWN, 0, 1.0, LATER)

    apply(0, ALL, 1.0, False)

    def two_steps(k, carry):
        apply(1, ALL, 2.0, True)
        apply(0, ALL, 2.0, True)
        return carry

    lax.fori_loop(0, (DEGREE - 2) // 2, two_steps, 0)
    apply(1, UP, 2.0, True)
    last = 0

    owned_z = lax.broadcasted_iota(jnp.int32, (7 * 8, STATES), 0) % 8 < 7
    blocks = []
    for c in range(2):
        for x in range(NPE - 1):
            block = field[last, c, x * 64 : x * 64 + 56, :]
            blocks.append(jnp.where(owned_z, block, 0.0))
    columns = jnp.concatenate(blocks, axis=0)
    high, low = split(columns)
    parts[...] = jnp.concatenate([high, low], axis=1)
    both = lax.dot_general(
        high,
        parts[...],
        (((0,), (0,)), ((), ())),
        preferred_element_type=F32,
    )
    cross = both[:, STATES:]
    gram[...] = both[:, :STATES] + (cross + cross.T)

    piece = STATES // ring
    mine = pl.ds(pl.multiple_of(ring_place * piece, piece), piece)

    def scatter(k, j):
        device, place = in_ring(j)
        rows = pl.ds(pl.multiple_of(place * piece, piece), piece)
        return pltpu.make_async_remote_copy(
            src_ref=gram.at[rows],
            dst_ref=r_scatter.at[k],
            send_sem=sum_send.at[0],
            recv_sem=sum_recv.at[0],
            device_id=device,
            device_id_type=MESH,
        )

    def reduce(j):
        return pltpu.make_async_remote_copy(
            src_ref=r_reduce.at[other_place],
            dst_ref=r_reduce.at[other_place],
            send_sem=sum_send.at[1],
            recv_sem=sum_recv.at[1],
            device_id=across(j),
            device_id_type=MESH,
        )

    def gather(j):
        return pltpu.make_async_remote_copy(
            src_ref=r_gather.at[mine],
            dst_ref=r_gather.at[mine],
            send_sem=sum_send.at[2],
            recv_sem=sum_recv.at[2],
            device_id=in_ring(j)[0],
            device_id_type=MESH,
        )

    def waiter(ref, k):
        return pltpu.make_async_remote_copy(
            src_ref=ref,
            dst_ref=ref,
            send_sem=sum_send.at[k],
            recv_sem=sum_recv.at[k],
            device_id=neighbour((1, 0, 0)),
            device_id_type=MESH,
        )

    for k, j in enumerate(turns(nx, 2)):
        scatter(k, j).start()
    waiter(r_scatter, 0).wait_recv()
    r_reduce[other_place] = gram[mine, :] + jnp.sum(r_scatter[...], axis=0)
    for j in turns(4, 4):
        reduce(j).start()
    waiter(r_scatter, 0).wait_send()
    waiter(r_reduce.at[pl.ds(0, others - 1)], 1).wait_recv()
    nodes = 686 * nx * ny * nz
    r_gather[mine, :] = jnp.sum(r_reduce[...], axis=0) * (1.0 / nodes)
    for j in turns(nx, 2):
        gather(j).start()
    waiter(r_reduce.at[pl.ds(0, others - 1)], 1).wait_send()
    rest = r_gather.at[pl.ds(0, piece * (ring - 1))]
    waiter(rest, 2).wait_recv()

    total = r_gather[...]
    diagonal = lax.broadcasted_iota(jnp.int32, (STATES, STATES), 0) == (
        lax.broadcasted_iota(jnp.int32, (STATES, STATES), 1)
    )
    trace = jnp.sum(jnp.where(diagonal, total, 0.0), keepdims=True)
    three = jnp.where(diagonal, 3.0, 0.0)

    def newton(k, pair):
        root, inverse = pair
        middle = three - product(inverse, root)
        return 0.5 * product(root, middle), 0.5 * product(middle, inverse)

    scaled = total / trace
    middle = three - scaled
    root, inverse = lax.fori_loop(
        0,
        NS_STEPS - 2,
        newton,
        (0.5 * product(scaled, middle), 0.5 * middle),
        unroll=2,
    )
    inverse = 0.5 * product(three - product(inverse, root), inverse)
    high, low = split(inverse / jnp.sqrt(trace))
    upper = jnp.concatenate([high, low], axis=1)
    lower = jnp.concatenate([high, jnp.zeros_like(low)], axis=1)
    both = jnp.dot(
        parts[...], jnp.concatenate([upper, lower], axis=0), preferred_element_type=F32
    )
    turned = both[:, :STATES] + both[:, STATES:]
    for c in range(2):
        for x in range(NPE - 1):
            for y in range(NPE - 1):
                row = ((c * 7 + x) * 7 + y) * 8
                out_ref[x, y, c * 7 : c * 7 + 7, :] = turned[row : row + 7]
    waiter(rest, 2).wait_send()


def shards(wavefunctions, hamiltonians, cell_order):
    sizes = tuple(lax.axis_size(a) for a in AXES)
    ring, others = sizes[0] * 2, sizes[1] // 2 * sizes[2]
    piece = STATES // ring
    matrices = hamiltonians.reshape((2, CDOF, CDOF))
    orders = cell_order.reshape((2, CDOF))
    kinds = len(KINDS)
    return pl.pallas_call(
        functools.partial(kernel, sizes),
        out_shape=pltpu.VMEM(wavefunctions.shape, F32),
        in_specs=[pl.BlockSpec(memory_space=pltpu.HBM)] * 3,
        out_specs=pl.BlockSpec(memory_space=pltpu.VMEM),
        scratch_shapes=[
            pltpu.VMEM(wavefunctions.shape, F32),
            pltpu.VMEM((2, CDOF, CDOF), F32),
            pltpu.VMEM((2, ROWS, CDOF), BF16),
            pltpu.VMEM((2, EARLY, CDOF), BF16),
            pltpu.VMEM((2, LATE, CDOF), BF16),
            pltpu.VMEM((2, CDOF), jnp.int32),
            pltpu.VMEM((2, 2 * ROWS, EARLY), BF16),
            pltpu.VMEM((2, 2 * SENT, LATE), BF16),
            pltpu.VMEM((2, 2 * INNER, LATE), BF16),
            pltpu.VMEM((2, ROWS, STATES), F32),
            pltpu.VMEM((2, 2, CDOF, STATES), F32),
            pltpu.VMEM((2, 64, STATES), F32),
            pltpu.VMEM((2, 256, STATES), F32),
            pltpu.VMEM((2, INNER + 32, STATES), F32),
            pltpu.VMEM((2, 2, 8, STATES), F32),
            pltpu.VMEM((2, 2, 2, 64, STATES), F32),
            pltpu.VMEM((2, 2, 2, 64, STATES), F32),
            pltpu.VMEM((2, 2, 64, STATES), F32),
            pltpu.VMEM((2, 4, 2, 8, STATES), F32),
            pltpu.VMEM((2, 4, 8, STATES), F32),
            pltpu.VMEM((2, 4, 8, STATES), F32),
            pltpu.VMEM((2, 8, STATES), F32),
            pltpu.VMEM((2 * 7 * 7 * 8, 2 * STATES), BF16),
            pltpu.VMEM((STATES, STATES), F32),
            pltpu.VMEM((ring - 1, piece, STATES), F32),
            pltpu.VMEM((others, piece, STATES), F32),
            pltpu.VMEM((STATES, STATES), F32),
            pltpu.SemaphoreType.DMA((4,)),
            pltpu.SemaphoreType.DMA((kinds,)),
            pltpu.SemaphoreType.DMA((2, 2 + kinds)),
            pltpu.SemaphoreType.DMA((3,)),
            pltpu.SemaphoreType.DMA((3,)),
        ],
        compiler_params=pltpu.CompilerParams(
            collective_id=0, has_side_effects=True, vmem_limit_bytes=56 << 20
        ),
    )(wavefunctions, matrices, orders)


def solution(mesh):
    in_specs = (
        P("gx", "gy", "gz", None),
        P("gx", "gy", "gz", None, None),
        P("gx", "gy", "gz", None),
    )
    out_specs = P("gx", "gy", "gz", None)
    return jax.shard_map(
        shards, mesh=mesh, in_specs=in_specs, out_specs=out_specs, check_vma=False
    )
```

```python
import functools
import itertools

import jax
import jax.numpy as jnp
from jax import lax
from jax.experimental import pallas as pl
from jax.experimental.pallas import tpu as pltpu
from jax.sharding import PartitionSpec as P

NPE = 8
CDOF = 512
STATES = 128
DEGREE = 6
NS_STEPS = 12
CENTER = 0.4
HALF_WIDTH = 0.7
AXES = ("gx", "gy", "gz")
MESH = pl.DeviceIdType.MESH
F32 = jnp.float32
BF16 = jnp.bfloat16

ALL = sorted(
    (d for d in itertools.product((-1, 0, 1), repeat=3) if any(d)),
    key=lambda d: -sum(map(abs, d)),
)
NEAR, FAR = 1, 2
CODED = sorted(
    (d for d in itertools.product((-1, 0, 1), (0, NEAR, FAR), (-1, 0, 1)) if any(d)),
    key=lambda d: (-sum(map(bool, d)), (1, 2, 0)[d[1]]),
)
DOWN = [d for d in ALL if max(d) <= 0]
UP = [d for d in ALL if min(d) >= 0]

KINDS = ("x", "z", "xz", "y", "xy", "yz", "xyz")
Y_ROWS, X_ROWS = 0, 128
INNER = 36 * 8
SENT = 64 + 128 + 96
ROWS = SENT + INNER
EARLY, LATE = 384, 256


def split(value):
    high = value.astype(BF16)
    low = (value - high.astype(F32)).astype(BF16)
    return high, low


def product(left, right):
    columns = right.shape[1]
    high, low = split(right)
    upper = jnp.concatenate([high, low], axis=1)
    lower = jnp.concatenate([high, jnp.zeros_like(low)], axis=1)
    sums = jnp.dot(
        jnp.concatenate(split(left), axis=1),
        jnp.concatenate([upper, lower], axis=0),
        preferred_element_type=F32,
    )
    return sums[:, :columns] + sums[:, columns:]


def side(step):
    return (step + 1) // 2


def kind_of(d):
    return "".join(name for name, step in zip("xyz", d) if step)


def kernel(
    sizes,
    wave_hbm,
    ham_hbm,
    order_hbm,
    out_ref,
    wave_ref,
    ham_raw,
    pick,
    early_columns,
    late_columns,
    order_ref,
    ham_early,
    ham_sent,
    ham_inner,
    early,
    field,
    rims,
    faces,
    inner,
    yz_pack,
    r_x,
    r_y,
    r_z,
    r_xy,
    r_xz,
    r_yz,
    r_xyz,
    parts,
    gram,
    r_scatter,
    r_reduce,
    r_gather,
    load_sem,
    send_sem,
    recv_sem,
    sum_send,
    sum_recv,
):
    me = tuple(lax.axis_index(a) for a in AXES)
    nx, ny, nz = sizes
    received = dict(x=r_x, y=r_y, z=r_z, xy=r_xy, xz=r_xz, yz=r_yz, xyz=r_xyz)

    shifted = [
        {s: lax.rem(m + (s + n), n) for s in (-1, 0, 1)} for m, n in zip(me, sizes)
    ]
    neighbours = {
        d: tuple(table[s] for table, s in zip(shifted, d)) for d in ALL
    }

    core = lax.rem(me[1], 2)
    coded_y = {0: me[1], NEAR: me[1] + 1 - 2 * core, FAR: lax.rem(me[1] + 2 * core + 3, 4)}

    def neighbour(d):
        return neighbours[d]

    ring_place = me[0] * 2 + lax.rem(me[1], 2)
    other_place = (me[1] // 2) * nz + me[2]
    ring, others = nx * 2, (ny // 2) * nz

    def turns(*lengths):
        shifts = [j for j in itertools.product(*map(range, lengths)) if any(j)]
        return sorted(shifts, key=lambda j: -sum(min(i, n - i) for i, n in zip(j, lengths)))

    def in_ring(j):
        x = lax.rem(me[0] + j[0], nx)
        core = lax.rem(me[1] + j[1], 2)
        return (x, (me[1] // 2) * 2 + core, me[2]), x * 2 + core

    def across(j):
        y = lax.rem((me[1] // 2) * 2 + me[2] // 4 + j[0], 4)
        z = lax.rem(y, 2) * 4 + lax.rem(me[2] + j[1], 4)
        return (me[0], (y // 2) * 2 + lax.rem(me[1], 2), z)

    barrier = pltpu.get_barrier_semaphore()
    for d in UP + DOWN:
        pl.semaphore_signal(barrier, inc=1, device_id=neighbour(d), device_id_type=MESH)

    loads = [
        pltpu.make_async_copy(wave_hbm, wave_ref, load_sem.at[0]),
        pltpu.make_async_copy(order_hbm, order_ref, load_sem.at[1]),
        pltpu.make_async_copy(ham_hbm.at[0], ham_raw.at[0], load_sem.at[2]),
        pltpu.make_async_copy(ham_hbm.at[1], ham_raw.at[1], load_sem.at[3]),
    ]
    for load in loads:
        load.start()

    def message(d, slot, coded):
        dx, dy, dz = d
        kind = kind_of(d)
        sx, sy, sz = side(dx), side(dy), side(dz)
        device = neighbours[d] if not coded else (shifted[0][dx], coded_y[dy], shifted[2][dz])
        if coded and dy:
            sy = core if dy == FAR else 1 - core
        if kind == "x":
            source, place = faces.at[:, pl.ds(X_ROWS + sx * 64, 64)], sx
        elif kind == "y":
            source, place = faces.at[:, pl.ds(Y_ROWS + sy * 64, 64)], sy
        elif kind == "z":
            source, place = rims.at[sz, pl.ds(0, 64)], sz
        elif kind == "xy":
            source = faces.at[:, pl.ds(X_ROWS + sx * 64 + sy * 56, 8)]
            place = sx * 2 + sy
        elif kind == "xz":
            source = rims.at[sz, pl.ds(sx * 56, 8)]
            place = sx * 2 + sz
        elif kind == "yz":
            source, place = yz_pack.at[sy, sz], sy * 2 + sz
        else:
            source = rims.at[sz, pl.ds(sx * 56 + sy * 7, 1)]
            place = sx * 4 + sy * 2 + sz
        if kind == "xyz":
            target = r_xyz.at[slot, pl.ds(place, 1)]
        else:
            target = received[kind].at[slot, place]
        k = KINDS.index(kind)
        return pltpu.make_async_remote_copy(
            src_ref=source,
            dst_ref=target,
            send_sem=send_sem.at[k],
            recv_sem=recv_sem.at[slot, place if kind == "y" else 2 + k],
            device_id=device,
            device_id_type=MESH,
        )

    def send(directions, slot, coded=False):
        for d in directions:
            message(d, slot, coded).start()

    def every(kind, directions, slot):
        count = sum(kind_of(d) == kind for d in directions)
        whole = received[kind].at[slot, pl.ds(0, count)]
        k = KINDS.index(kind)
        return pltpu.make_async_remote_copy(
            src_ref=whole,
            dst_ref=whole,
            send_sem=send_sem.at[k],
            recv_sem=recv_sem.at[slot, 2 + k],
            device_id=neighbour((1, 0, 0)),
            device_id_type=MESH,
        )

    def wait_sent(directions, slot):
        for kind in KINDS:
            every(kind, directions, slot).wait_send()

    def collect_y(total, slot, place, scale):
        pltpu.make_async_remote_copy(
            src_ref=r_y.at[slot, place],
            dst_ref=r_y.at[slot, place],
            send_sem=send_sem.at[KINDS.index("y")],
            recv_sem=recv_sem.at[slot, place],
            device_id=neighbour((1, 0, 0)),
            device_id_type=MESH,
        ).wait_recv()
        for x in range(NPE):
            rows = pl.ds(pl.multiple_of(x * 64 + 56 * (1 - place), 8), 8)
            total[:, rows, :] += scale * r_y[slot, place, :, x * 8 : x * 8 + 8, :]

    def collect(total, directions, slot, scale):
        for kind in KINDS:
            if kind == "y":
                for d in directions:
                    if kind_of(d) == "y":
                        collect_y(total, slot, side(d[1]), scale)
                continue
            every(kind, directions, slot).wait_recv()
            for dx, dy, dz in directions:
                if kind_of((dx, dy, dz)) != kind:
                    continue
                sx, sy, sz = side(dx), side(dy), side(dz)
                ix, iy = 7 * (1 - sx), 7 * (1 - sy)
                c, iz = (0, 0) if dz > 0 else (1, 7)
                if kind == "x":
                    total[:, ix * 64 : ix * 64 + 64, :] += scale * r_x[slot, sx]
                elif kind == "xy":
                    row = (ix * NPE + iy) * NPE
                    total[:, row : row + 8, :] += scale * r_xy[slot, sx * 2 + sy]
                elif kind == "z":
                    total[c, pl.ds(iz, 64, stride=8), :] += scale * r_z[slot, sz]
                elif kind == "xz":
                    rows = pl.ds(ix * 64 + iz, 8, stride=8)
                    total[c, rows, :] += scale * r_xz[slot, sx * 2 + sz]
                elif kind == "yz":
                    rows = pl.ds(iy * 8 + iz, 8, stride=64)
                    total[c, rows, :] += scale * r_yz[slot, sy * 2 + sz]
                else:
                    row = (ix * NPE + iy) * NPE + iz
                    place = sx * 4 + sy * 2 + sz
                    total[c, row : row + 1, :] += scale * r_xyz[slot, place : place + 1, :]

    def pack_yz():
        for s in range(2):
            for t in range(2):
                yz_pack[t, s] = rims[s, pl.ds(7 * t, 8, stride=8), :]

    loads[0].wait()
    field[0] = jnp.zeros((2, CDOF, STATES), F32)
    for x in range(NPE - 1):
        for y in range(NPE - 1):
            row = (x * NPE + y) * NPE
            field[0, 0, row : row + 8, :] = wave_ref[x, y, 0:8, :]
            field[0, 1, row : row + 7, :] = wave_ref[x, y, 7:14, :]
    rims[0] = field[0, 0, pl.ds(0, 64, stride=8), :]
    for c in range(2):
        faces[c, X_ROWS : X_ROWS + 64, :] = field[0, c, 0:64, :]
        for x in range(NPE):
            faces[c, Y_ROWS + x * 8 : Y_ROWS + x * 8 + 8, :] = field[0, c, x * 64 : x * 64 + 8, :]
    yz_pack[0, 0] = rims[0, pl.ds(0, 8, stride=8), :]
    loads[1].wait()
    near_place = lax.rem(me[1], 2)
    near_y = 7 * (1 - near_place)
    lanes = 128
    row_of = lax.broadcasted_iota(jnp.int32, (CDOF, lanes), 0)
    n, k = row_of[:64], row_of[:48]
    none = jnp.full((48, lanes), -1, jnp.int32)
    for c in range(2):
        order = order_ref[c : c + 1, :]

        def chosen(rows):
            return jnp.concatenate(
                [
                    (rows == order[:, first : first + lanes]).astype(F32).astype(BF16)
                    for first in range(0, CDOF, lanes)
                ],
                axis=1,
            )

        block = (n >> 3) * 64 + (n & 7)
        rows = [n * 8 + 7 * c, block, block + 56, n[8:56], n[8:56] + 448]
        rows += [row_of[x * 64 + 8 : x * 64 + 56] for x in range(1, NPE - 1)]
        pick[c] = chosen(jnp.concatenate(rows, axis=0))
        near_rows = ((k >> 3) + 1) * 64 + near_y * 8 + (k & 7)
        early_rows = [row_of[x * 64 + 8 : x * 64 + 56] for x in range(1, NPE - 1)]
        early_rows = [
            jnp.where((k & 7) == 7 * c, -1, rows) for rows in early_rows + [near_rows]
        ] + [none]
        rim_rows = ((k >> 3) + 1) * 64 + (k & 7) * 8 + 7 * c
        late_rows = [
            n,
            n + 448,
            ((k >> 3) + 1) * 64 + (7 - near_y) * 8 + (k & 7),
            jnp.where((k & 7) == 7 - near_y, -1, rim_rows),
            none[:32],
        ]
        early_columns[c] = chosen(jnp.concatenate(early_rows, axis=0))
        late_columns[c] = chosen(jnp.concatenate(late_rows, axis=0))

    pl.semaphore_wait(barrier, len(UP + DOWN))
    send(DOWN, 0)

    for c in range(2):
        loads[2 + c].wait()
        for part, value in enumerate(split(ham_raw[c])):
            half = jnp.dot(pick[c], value, preferred_element_type=F32).astype(BF16)
            whole = lax.dot_general(
                half, early_columns[c], (((1,), (1,)), ((), ())), preferred_element_type=F32
            ).astype(BF16)
            ham_early[c, part * ROWS : (part + 1) * ROWS, :] = whole
            whole = lax.dot_general(
                half, late_columns[c], (((1,), (1,)), ((), ())), preferred_element_type=F32
            ).astype(BF16)
            ham_sent[c, part * SENT : (part + 1) * SENT, :] = whole[:SENT]
            ham_inner[c, part * INNER : (part + 1) * INNER, :] = whole[SENT:]


    def four(matrix, value):
        rows = matrix.shape[0] // 2
        all_four = jnp.dot(matrix, value, preferred_element_type=F32)
        return (
            all_four[:rows, :STATES]
            + (all_four[:rows, STATES:] + all_four[rows:, :STATES])
            + all_four[rows:, STATES:]
        )

    def join(ref, first, count):
        upper, lower = pl.ds(first + 7, count, stride=8), pl.ds(first, count, stride=8)
        middle = ref[0, upper, :] + ref[1, lower, :]
        ref[0, upper, :] = middle
        ref[1, lower, :] = middle

    def pair(parts):
        return jnp.concatenate(split(jnp.concatenate(parts, axis=0)), axis=1)

    def y_rows(now, c, y):
        return [
            field[now, c, pl.ds(pl.multiple_of(x * 64 + y * 8, 8), 8), :]
            for x in range(1, NPE - 1)
        ]

    def multiply_early(now):
        for c in range(2):
            parts = [field[now, c, x * 64 + 8 : x * 64 + 56, :] for x in range(1, NPE - 1)]
            parts += y_rows(now, c, near_y) + [jnp.zeros((48, STATES), F32)]
            early[c] = four(ham_early[c], pair(parts))

    def late_values(now, c):
        parts = [field[now, c, 0:64, :], field[now, c, 448:512, :]]
        parts += y_rows(now, c, 7 - near_y)
        parts += [field[now, c, pl.ds(64 + 7 * c, 48, stride=8), :]]
        return pair(parts + [jnp.zeros((32, STATES), F32)])

    def gram_of(columns):
        high, low = split(columns)
        both = lax.dot_general(
            high,
            jnp.concatenate([high, low], axis=1),
            (((0,), (0,)), ((), ())),
            preferred_element_type=F32,
        )
        cross = both[:, STATES:]
        return both[:, :STATES] + (cross + cross.T)

    sublane = lax.broadcasted_iota(jnp.int32, (56, STATES), 0) & 7

    def inner_rows(now):
        rows = []
        for c in range(2):
            kept = sublane[:48] < 7 if c else (sublane[:48] > 0) & (sublane[:48] < 7)
            for x in range(1, NPE - 1):
                rows.append(jnp.where(kept, field[now, c, x * 64 + 8 : x * 64 + 56, :], 0.0))
        return jnp.concatenate(rows, axis=0)

    def rim_rows_of(now):
        rows = []
        for c in range(2):
            rows.append(jnp.where(sublane < 7, field[now, c, 0:56, :], 0.0))
            for x in range(1, NPE - 1):
                block = field[now, c, x * 64 : x * 64 + 8, :]
                rows.append(jnp.where(sublane[:8] < 7, block, 0.0))
        kept = (sublane[:48] > 0) & (sublane[:48] < 7)
        rows.append(jnp.where(kept, field[now, 0, pl.ds(64, 48, stride=8), :], 0.0))
        return jnp.concatenate(rows, axis=0)

    def apply(now, directions, factor, keep):
        later = slot = 1 - now
        gain, shift = factor / HALF_WIDTH, -factor * CENTER / HALF_WIDTH
        values = [late_values(now, c) for c in range(2)]
        products = []
        for c in range(2):
            products.append(early[c, :SENT, :] + four(ham_sent[c], values[c]))
            rims[c] = products[c][:64]
        pack_yz()
        coded = directions is ALL
        order = CODED if coded else directions
        first = [d for d in order if kind_of(d) in ("xz", "yz", "xyz")]
        send(first, slot, coded)
        for c in range(2):
            faces[c, Y_ROWS : Y_ROWS + 128, :] = products[c][64:192]
            for t in range(2):
                row = X_ROWS + t * 64
                faces[c, row + 8 : row + 56, :] = products[c][192 + t * 48 : 240 + t * 48]
                for u in range(2):
                    edge = products[c][64 + u * 64 + t * 56 : 72 + u * 64 + t * 56]
                    faces[c, row + u * 56 : row + u * 56 + 8, :] = edge
        join(faces, 0, 32)
        send([d for d in order if d not in first], slot, coded)
        for c in range(2):
            inner[c, :INNER, :] = early[c, SENT:, :] + four(ham_inner[c], values[c])
        join(inner, 0, 36)

        def advance(c, row, count, products):
            rows = slice(row, row + count)
            fresh = gain * products + shift * field[now, c, rows, :]
            if keep:
                fresh = fresh - field[later, c, rows, :]
            field[later, c, rows, :] = fresh

        for c in range(2):
            for x in range(NPE):
                if x in (0, NPE - 1):
                    first = X_ROWS + 64 * (x // 7)
                    advance(c, x * 64, 64, faces[c, first : first + 64, :])
                    continue
                for t in range(2):
                    first = Y_ROWS + 64 * t + x * 8
                    advance(c, x * 64 + 56 * t, 8, faces[c, first : first + 8, :])
                first = (x - 1) * 48
                advance(c, x * 64 + 8, 48, inner[c, first : first + 48, :])
        total = field.at[later]
        if directions is ALL:
            collect_y(total, slot, near_place, gain)
            multiply_early(later)
            wait_sent(directions, slot)
            collect(total, [d for d in ALL if kind_of(d) != "y"], slot, gain)
            collect_y(total, slot, 1 - near_place, gain)
        else:
            gram[...] = gram_of(inner_rows(later))
            wait_sent(directions, slot)
            collect(total, directions, slot, gain)

    @pl.when(near_place == 0)
    def _():
        collect_y(field.at[0], 0, 0, 1.0)

    multiply_early(0)
    wait_sent(DOWN, 0)
    collect(field.at[0], [d for d in DOWN if kind_of(d) != "y"], 0, 1.0)

    @pl.when(near_place == 1)
    def _():
        collect_y(field.at[0], 0, 0, 1.0)

    apply(0, ALL, 1.0, False)

    def two_steps(k, carry):
        apply(1, ALL, 2.0, True)
        apply(0, ALL, 2.0, True)
        return carry

    lax.fori_loop(0, (DEGREE - 2) // 2, two_steps, 0)
    apply(1, UP, 2.0, True)
    last = 0

    gram[...] += gram_of(rim_rows_of(last))

    piece = STATES // ring
    mine = pl.ds(pl.multiple_of(ring_place * piece, piece), piece)

    def scatter(k, j):
        device, place = in_ring(j)
        rows = pl.ds(pl.multiple_of(place * piece, piece), piece)
        return pltpu.make_async_remote_copy(
            src_ref=gram.at[rows],
            dst_ref=r_scatter.at[k],
            send_sem=sum_send.at[0],
            recv_sem=sum_recv.at[0],
            device_id=device,
            device_id_type=MESH,
        )

    def reduce(j):
        return pltpu.make_async_remote_copy(
            src_ref=r_reduce.at[other_place],
            dst_ref=r_reduce.at[other_place],
            send_sem=sum_send.at[1],
            recv_sem=sum_recv.at[1],
            device_id=across(j),
            device_id_type=MESH,
        )

    def gather(j):
        return pltpu.make_async_remote_copy(
            src_ref=r_gather.at[mine],
            dst_ref=r_gather.at[mine],
            send_sem=sum_send.at[2],
            recv_sem=sum_recv.at[2],
            device_id=in_ring(j)[0],
            device_id_type=MESH,
        )

    def waiter(ref, k):
        return pltpu.make_async_remote_copy(
            src_ref=ref,
            dst_ref=ref,
            send_sem=sum_send.at[k],
            recv_sem=sum_recv.at[k],
            device_id=neighbour((1, 0, 0)),
            device_id_type=MESH,
        )

    for k, j in enumerate(turns(nx, 2)):
        scatter(k, j).start()
    blocks = [field[last, c, x * 64 : x * 64 + 56, :] for c in range(2) for x in range(NPE - 1)]
    parts[...] = jnp.concatenate(split(jnp.concatenate(blocks, axis=0)), axis=1)
    waiter(r_scatter, 0).wait_recv()
    r_reduce[other_place] = gram[mine, :] + jnp.sum(r_scatter[...], axis=0)
    for j in turns(4, 4):
        reduce(j).start()
    waiter(r_scatter, 0).wait_send()
    waiter(r_reduce.at[pl.ds(0, others - 1)], 1).wait_recv()
    nodes = 686 * nx * ny * nz
    r_gather[mine, :] = jnp.sum(r_reduce[...], axis=0) * (1.0 / nodes)
    for j in turns(nx, 2):
        gather(j).start()
    waiter(r_reduce.at[pl.ds(0, others - 1)], 1).wait_send()
    rest = r_gather.at[pl.ds(0, piece * (ring - 1))]
    waiter(rest, 2).wait_recv()

    total = r_gather[...]
    diagonal = lax.broadcasted_iota(jnp.int32, (STATES, STATES), 0) == (
        lax.broadcasted_iota(jnp.int32, (STATES, STATES), 1)
    )
    trace = jnp.sum(jnp.where(diagonal, total, 0.0), keepdims=True)
    three = jnp.where(diagonal, 3.0, 0.0)

    def newton(k, pair):
        root, inverse = pair
        middle = three - product(inverse, root)
        return 0.5 * product(root, middle), 0.5 * product(middle, inverse)

    scaled = total / trace
    middle = three - scaled
    root, inverse = lax.fori_loop(
        0, NS_STEPS - 2, newton, (0.5 * product(scaled, middle), 0.5 * middle)
    )
    inverse = 0.5 * product(three - product(inverse, root), inverse)
    high, low = split(inverse / jnp.sqrt(trace))
    upper = jnp.concatenate([high, low], axis=1)
    lower = jnp.concatenate([high, jnp.zeros_like(low)], axis=1)
    both = jnp.dot(
        parts[...], jnp.concatenate([upper, lower], axis=0), preferred_element_type=F32
    )
    turned = both[:, :STATES] + both[:, STATES:]
    for c in range(2):
        for x in range(NPE - 1):
            for y in range(NPE - 1):
                row = ((c * 7 + x) * 7 + y) * 8
                out_ref[x, y, c * 7 : c * 7 + 7, :] = turned[row : row + 7]
    waiter(rest, 2).wait_send()


def shards(wavefunctions, hamiltonians, cell_order):
    sizes = tuple(lax.axis_size(a) for a in AXES)
    ring, others = sizes[0] * 2, sizes[1] // 2 * sizes[2]
    piece = STATES // ring
    matrices = hamiltonians.reshape((2, CDOF, CDOF))
    orders = cell_order.reshape((2, CDOF))
    kinds = len(KINDS)
    return pl.pallas_call(
        functools.partial(kernel, sizes),
        out_shape=pltpu.VMEM(wavefunctions.shape, F32),
        in_specs=[pl.BlockSpec(memory_space=pltpu.HBM)] * 3,
        out_specs=pl.BlockSpec(memory_space=pltpu.VMEM),
        scratch_shapes=[
            pltpu.VMEM(wavefunctions.shape, F32),
            pltpu.VMEM((2, CDOF, CDOF), F32),
            pltpu.VMEM((2, ROWS, CDOF), BF16),
            pltpu.VMEM((2, EARLY, CDOF), BF16),
            pltpu.VMEM((2, LATE, CDOF), BF16),
            pltpu.VMEM((2, CDOF), jnp.int32),
            pltpu.VMEM((2, 2 * ROWS, EARLY), BF16),
            pltpu.VMEM((2, 2 * SENT, LATE), BF16),
            pltpu.VMEM((2, 2 * INNER, LATE), BF16),
            pltpu.VMEM((2, ROWS, STATES), F32),
            pltpu.VMEM((2, 2, CDOF, STATES), F32),
            pltpu.VMEM((2, 64, STATES), F32),
            pltpu.VMEM((2, 256, STATES), F32),
            pltpu.VMEM((2, INNER + 32, STATES), F32),
            pltpu.VMEM((2, 2, 8, STATES), F32),
            pltpu.VMEM((2, 2, 2, 64, STATES), F32),
            pltpu.VMEM((2, 2, 2, 64, STATES), F32),
            pltpu.VMEM((2, 2, 64, STATES), F32),
            pltpu.VMEM((2, 4, 2, 8, STATES), F32),
            pltpu.VMEM((2, 4, 8, STATES), F32),
            pltpu.VMEM((2, 4, 8, STATES), F32),
            pltpu.VMEM((2, 8, STATES), F32),
            pltpu.VMEM((2 * 7 * 7 * 8, 2 * STATES), BF16),
            pltpu.VMEM((STATES, STATES), F32),
            pltpu.VMEM((ring - 1, piece, STATES), F32),
            pltpu.VMEM((others, piece, STATES), F32),
            pltpu.VMEM((STATES, STATES), F32),
            pltpu.SemaphoreType.DMA((4,)),
            pltpu.SemaphoreType.DMA((kinds,)),
            pltpu.SemaphoreType.DMA((2, 2 + kinds)),
            pltpu.SemaphoreType.DMA((3,)),
            pltpu.SemaphoreType.DMA((3,)),
        ],
        compiler_params=pltpu.CompilerParams(
            collective_id=0, has_side_effects=True, vmem_limit_bytes=56 << 20
        ),
    )(wavefunctions, matrices, orders)


def solution(mesh):
    in_specs = (
        P("gx", "gy", "gz", None),
        P("gx", "gy", "gz", None, None),
        P("gx", "gy", "gz", None),
    )
    out_specs = P("gx", "gy", "gz", None)
    return jax.shard_map(
        shards, mesh=mesh, in_specs=in_specs, out_specs=out_specs, check_vma=False
    )
```

```python
import functools
import itertools

import jax
import jax.numpy as jnp
from jax import lax
from jax.experimental import pallas as pl
from jax.experimental.pallas import tpu as pltpu
from jax.sharding import PartitionSpec as P

NPE = 8
CDOF = 512
STATES = 128
DEGREE = 6
NS_STEPS = 12
CENTER = 0.4
HALF_WIDTH = 0.7
AXES = ("gx", "gy", "gz")
MESH = pl.DeviceIdType.MESH
F32 = jnp.float32
BF16 = jnp.bfloat16

ALL = sorted(
    (d for d in itertools.product((-1, 0, 1), repeat=3) if any(d)),
    key=lambda d: -sum(map(abs, d)),
)
NEAR, FAR = 1, 2
CODED = sorted(
    (d for d in itertools.product((-1, 0, 1), (0, NEAR, FAR), (-1, 0, 1)) if any(d)),
    key=lambda d: (-sum(map(bool, d)), (1, 2, 0)[d[1]]),
)
DOWN = [d for d in ALL if max(d) <= 0]
UP = [d for d in ALL if min(d) >= 0]

KINDS = ("x", "z", "xz", "y", "xy", "yz", "xyz")
Y_ROWS, X_ROWS = 0, 128
INNER = 36 * 8
SENT = 64 + 128 + 96
ROWS = SENT + INNER
EARLY, LATE = 384, 256


def split(value):
    high = value.astype(BF16)
    low = (value - high.astype(F32)).astype(BF16)
    return high, low


def product(left, right):
    columns = right.shape[1]
    high, low = split(right)
    upper = jnp.concatenate([high, low], axis=1)
    lower = jnp.concatenate([high, jnp.zeros_like(low)], axis=1)
    sums = jnp.dot(
        jnp.concatenate(split(left), axis=1),
        jnp.concatenate([upper, lower], axis=0),
        preferred_element_type=F32,
    )
    return sums[:, :columns] + sums[:, columns:]


def side(step):
    return (step + 1) // 2


def kind_of(d):
    return "".join(name for name, step in zip("xyz", d) if step)


def kernel(
    sizes,
    wave_hbm,
    ham_hbm,
    order_hbm,
    out_ref,
    wave_ref,
    ham_raw,
    pick,
    early_columns,
    late_columns,
    order_ref,
    ham_early,
    ham_sent,
    ham_inner,
    early,
    field,
    rims,
    faces,
    inner,
    yz_pack,
    r_x,
    r_y,
    r_z,
    r_xy,
    r_xz,
    r_yz,
    r_xyz,
    parts,
    gram,
    r_scatter,
    r_reduce,
    r_gather,
    load_sem,
    send_sem,
    recv_sem,
    sum_send,
    sum_recv,
):
    me = tuple(lax.axis_index(a) for a in AXES)
    nx, ny, nz = sizes
    received = dict(x=r_x, y=r_y, z=r_z, xy=r_xy, xz=r_xz, yz=r_yz, xyz=r_xyz)

    shifted = [
        {s: lax.rem(m + (s + n), n) for s in (-1, 0, 1)} for m, n in zip(me, sizes)
    ]
    neighbours = {
        d: tuple(table[s] for table, s in zip(shifted, d)) for d in ALL
    }

    core = lax.rem(me[1], 2)
    coded_y = {0: me[1], NEAR: me[1] + 1 - 2 * core, FAR: lax.rem(me[1] + 2 * core + 3, 4)}

    def neighbour(d):
        return neighbours[d]

    ring_place = me[0] * 2 + lax.rem(me[1], 2)
    other_place = (me[1] // 2) * nz + me[2]
    ring, others = nx * 2, (ny // 2) * nz

    def turns(*lengths):
        shifts = [j for j in itertools.product(*map(range, lengths)) if any(j)]
        return sorted(shifts, key=lambda j: -sum(min(i, n - i) for i, n in zip(j, lengths)))

    def in_ring(j):
        x = lax.rem(me[0] + j[0], nx)
        core = lax.rem(me[1] + j[1], 2)
        return (x, (me[1] // 2) * 2 + core, me[2]), x * 2 + core

    def across(j):
        y = lax.rem((me[1] // 2) * 2 + me[2] // 4 + j[0], 4)
        z = lax.rem(y, 2) * 4 + lax.rem(me[2] + j[1], 4)
        return (me[0], (y // 2) * 2 + lax.rem(me[1], 2), z)

    barrier = pltpu.get_barrier_semaphore()
    for d in UP + DOWN:
        pl.semaphore_signal(barrier, inc=1, device_id=neighbour(d), device_id_type=MESH)

    loads = [
        pltpu.make_async_copy(wave_hbm, wave_ref, load_sem.at[0]),
        pltpu.make_async_copy(order_hbm, order_ref, load_sem.at[1]),
        pltpu.make_async_copy(ham_hbm.at[0], ham_raw.at[0], load_sem.at[2]),
        pltpu.make_async_copy(ham_hbm.at[1], ham_raw.at[1], load_sem.at[3]),
    ]
    for load in loads:
        load.start()

    def message(d, slot, coded):
        dx, dy, dz = d
        kind = kind_of(d)
        sx, sy, sz = side(dx), side(dy), side(dz)
        device = neighbours[d] if not coded else (shifted[0][dx], coded_y[dy], shifted[2][dz])
        if coded and dy:
            sy = core if dy == FAR else 1 - core
        if kind == "x":
            source, place = faces.at[:, pl.ds(X_ROWS + sx * 64, 64)], sx
        elif kind == "y":
            source, place = faces.at[:, pl.ds(Y_ROWS + sy * 64, 64)], sy
        elif kind == "z":
            source, place = rims.at[sz, pl.ds(0, 64)], sz
        elif kind == "xy":
            source = faces.at[:, pl.ds(X_ROWS + sx * 64 + sy * 56, 8)]
            place = sx * 2 + sy
        elif kind == "xz":
            source = rims.at[sz, pl.ds(sx * 56, 8)]
            place = sx * 2 + sz
        elif kind == "yz":
            source, place = yz_pack.at[sy, sz], sy * 2 + sz
        else:
            source = rims.at[sz, pl.ds(sx * 56 + sy * 7, 1)]
            place = sx * 4 + sy * 2 + sz
        if kind == "xyz":
            target = r_xyz.at[slot, pl.ds(place, 1)]
        else:
            target = received[kind].at[slot, place]
        k = KINDS.index(kind)
        return pltpu.make_async_remote_copy(
            src_ref=source,
            dst_ref=target,
            send_sem=send_sem.at[k],
            recv_sem=recv_sem.at[slot, place if kind == "y" else 2 + k],
            device_id=device,
            device_id_type=MESH,
        )

    def send(directions, slot, coded=False):
        for d in directions:
            message(d, slot, coded).start()

    def every(kind, directions, slot):
        count = sum(kind_of(d) == kind for d in directions)
        whole = received[kind].at[slot, pl.ds(0, count)]
        k = KINDS.index(kind)
        return pltpu.make_async_remote_copy(
            src_ref=whole,
            dst_ref=whole,
            send_sem=send_sem.at[k],
            recv_sem=recv_sem.at[slot, 2 + k],
            device_id=neighbour((1, 0, 0)),
            device_id_type=MESH,
        )

    def wait_sent(directions, slot):
        for kind in KINDS:
            every(kind, directions, slot).wait_send()

    def collect_y(total, slot, place, scale):
        pltpu.make_async_remote_copy(
            src_ref=r_y.at[slot, place],
            dst_ref=r_y.at[slot, place],
            send_sem=send_sem.at[KINDS.index("y")],
            recv_sem=recv_sem.at[slot, place],
            device_id=neighbour((1, 0, 0)),
            device_id_type=MESH,
        ).wait_recv()
        for x in range(NPE):
            rows = pl.ds(pl.multiple_of(x * 64 + 56 * (1 - place), 8), 8)
            total[:, rows, :] += scale * r_y[slot, place, :, x * 8 : x * 8 + 8, :]

    def collect(total, directions, slot, scale):
        for kind in KINDS:
            if kind == "y":
                for d in directions:
                    if kind_of(d) == "y":
                        collect_y(total, slot, side(d[1]), scale)
                continue
            every(kind, directions, slot).wait_recv()
            for dx, dy, dz in directions:
                if kind_of((dx, dy, dz)) != kind:
                    continue
                sx, sy, sz = side(dx), side(dy), side(dz)
                ix, iy = 7 * (1 - sx), 7 * (1 - sy)
                c, iz = (0, 0) if dz > 0 else (1, 7)
                if kind == "x":
                    total[:, ix * 64 : ix * 64 + 64, :] += scale * r_x[slot, sx]
                elif kind == "xy":
                    row = (ix * NPE + iy) * NPE
                    total[:, row : row + 8, :] += scale * r_xy[slot, sx * 2 + sy]
                elif kind == "z":
                    total[c, pl.ds(iz, 64, stride=8), :] += scale * r_z[slot, sz]
                elif kind == "xz":
                    rows = pl.ds(ix * 64 + iz, 8, stride=8)
                    total[c, rows, :] += scale * r_xz[slot, sx * 2 + sz]
                elif kind == "yz":
                    rows = pl.ds(iy * 8 + iz, 8, stride=64)
                    total[c, rows, :] += scale * r_yz[slot, sy * 2 + sz]
                else:
                    row = (ix * NPE + iy) * NPE + iz
                    place = sx * 4 + sy * 2 + sz
                    total[c, row : row + 1, :] += scale * r_xyz[slot, place : place + 1, :]

    def pack_yz():
        for s in range(2):
            for t in range(2):
                yz_pack[t, s] = rims[s, pl.ds(7 * t, 8, stride=8), :]

    loads[0].wait()
    field[0] = jnp.zeros((2, CDOF, STATES), F32)
    for x in range(NPE - 1):
        for y in range(NPE - 1):
            row = (x * NPE + y) * NPE
            field[0, 0, row : row + 8, :] = wave_ref[x, y, 0:8, :]
            field[0, 1, row : row + 7, :] = wave_ref[x, y, 7:14, :]
    rims[0] = field[0, 0, pl.ds(0, 64, stride=8), :]
    for c in range(2):
        faces[c, X_ROWS : X_ROWS + 64, :] = field[0, c, 0:64, :]
        for x in range(NPE):
            faces[c, Y_ROWS + x * 8 : Y_ROWS + x * 8 + 8, :] = field[0, c, x * 64 : x * 64 + 8, :]
    yz_pack[0, 0] = rims[0, pl.ds(0, 8, stride=8), :]
    loads[1].wait()
    near_place = lax.rem(me[1], 2)
    near_y = 7 * (1 - near_place)
    lanes = 128
    row_of = lax.broadcasted_iota(jnp.int32, (CDOF, lanes), 0)
    n, k = row_of[:64], row_of[:48]
    none = jnp.full((48, lanes), -1, jnp.int32)
    for c in range(2):
        order = order_ref[c : c + 1, :]

        def chosen(rows):
            return jnp.concatenate(
                [
                    (rows == order[:, first : first + lanes]).astype(F32).astype(BF16)
                    for first in range(0, CDOF, lanes)
                ],
                axis=1,
            )

        block = (n >> 3) * 64 + (n & 7)
        rows = [n * 8 + 7 * c, block, block + 56, n[8:56], n[8:56] + 448]
        rows += [row_of[x * 64 + 8 : x * 64 + 56] for x in range(1, NPE - 1)]
        pick[c] = chosen(jnp.concatenate(rows, axis=0))
        near_rows = ((k >> 3) + 1) * 64 + near_y * 8 + (k & 7)
        early_rows = [row_of[x * 64 + 8 : x * 64 + 56] for x in range(1, NPE - 1)]
        early_rows = [
            jnp.where((k & 7) == 7 * c, -1, rows) for rows in early_rows + [near_rows]
        ] + [none]
        rim_rows = ((k >> 3) + 1) * 64 + (k & 7) * 8 + 7 * c
        late_rows = [
            n,
            n + 448,
            ((k >> 3) + 1) * 64 + (7 - near_y) * 8 + (k & 7),
            jnp.where((k & 7) == 7 - near_y, -1, rim_rows),
            none[:32],
        ]
        early_columns[c] = chosen(jnp.concatenate(early_rows, axis=0))
        late_columns[c] = chosen(jnp.concatenate(late_rows, axis=0))

    pl.semaphore_wait(barrier, len(UP + DOWN))
    send(DOWN, 0)

    for c in range(2):
        loads[2 + c].wait()
        for part, value in enumerate(split(ham_raw[c])):
            half = jnp.dot(pick[c], value, preferred_element_type=F32).astype(BF16)
            whole = lax.dot_general(
                half, early_columns[c], (((1,), (1,)), ((), ())), preferred_element_type=F32
            ).astype(BF16)
            ham_early[c, part * ROWS : (part + 1) * ROWS, :] = whole
            whole = lax.dot_general(
                half, late_columns[c], (((1,), (1,)), ((), ())), preferred_element_type=F32
            ).astype(BF16)
            ham_sent[c, part * SENT : (part + 1) * SENT, :] = whole[:SENT]
            ham_inner[c, part * INNER : (part + 1) * INNER, :] = whole[SENT:]


    def four(matrix, value):
        rows = matrix.shape[0] // 2
        all_four = jnp.dot(matrix, value, preferred_element_type=F32)
        return (
            all_four[:rows, :STATES]
            + (all_four[:rows, STATES:] + all_four[rows:, :STATES])
            + all_four[rows:, STATES:]
        )

    def join(ref, first, count):
        upper, lower = pl.ds(first + 7, count, stride=8), pl.ds(first, count, stride=8)
        middle = ref[0, upper, :] + ref[1, lower, :]
        ref[0, upper, :] = middle
        ref[1, lower, :] = middle

    def pair(parts):
        return jnp.concatenate(split(jnp.concatenate(parts, axis=0)), axis=1)

    def y_rows(now, c, y):
        return [
            field[now, c, pl.ds(pl.multiple_of(x * 64 + y * 8, 8), 8), :]
            for x in range(1, NPE - 1)
        ]

    def multiply_early(now):
        for c in range(2):
            parts = [field[now, c, x * 64 + 8 : x * 64 + 56, :] for x in range(1, NPE - 1)]
            parts += y_rows(now, c, near_y) + [jnp.zeros((48, STATES), F32)]
            early[c] = four(ham_early[c], pair(parts))

    def late_values(now, c):
        parts = [field[now, c, 0:64, :], field[now, c, 448:512, :]]
        parts += y_rows(now, c, 7 - near_y)
        parts += [field[now, c, pl.ds(64 + 7 * c, 48, stride=8), :]]
        return pair(parts + [jnp.zeros((32, STATES), F32)])

    def apply(now, directions, factor, keep):
        later = slot = 1 - now
        gain, shift = factor / HALF_WIDTH, -factor * CENTER / HALF_WIDTH
        values = [late_values(now, c) for c in range(2)]
        products = []
        for c in range(2):
            rows = [ham_sent[c, 0:64, :], ham_sent[c, SENT : SENT + 64, :]]
            rims[c] = early[c, :64, :] + four(jnp.concatenate(rows, axis=0), values[c])
        pack_yz()
        coded = directions is ALL
        order = CODED if coded else directions
        first = [d for d in order if kind_of(d) in ("xz", "yz", "xyz")]
        send(first, slot, coded)
        for c in range(2):
            rows = [ham_sent[c, 64:SENT, :], ham_sent[c, SENT + 64 :, :]]
            face_rows = four(jnp.concatenate(rows, axis=0), values[c])
            products.append(early[c, 64:SENT, :] + face_rows)
            faces[c, Y_ROWS : Y_ROWS + 128, :] = products[c][0:128]
            for t in range(2):
                row = X_ROWS + t * 64
                faces[c, row + 8 : row + 56, :] = products[c][128 + t * 48 : 176 + t * 48]
                for u in range(2):
                    edge = products[c][u * 64 + t * 56 : 8 + u * 64 + t * 56]
                    faces[c, row + u * 56 : row + u * 56 + 8, :] = edge
        join(faces, 0, 32)
        send([d for d in order if d not in first], slot, coded)
        for c in range(2):
            inner[c, :INNER, :] = early[c, SENT:, :] + four(ham_inner[c], values[c])
        join(inner, 0, 36)

        def advance(c, row, count, products):
            rows = slice(row, row + count)
            fresh = gain * products + shift * field[now, c, rows, :]
            if keep:
                fresh = fresh - field[later, c, rows, :]
            field[later, c, rows, :] = fresh

        for c in range(2):
            for x in range(NPE):
                if x in (0, NPE - 1):
                    first = X_ROWS + 64 * (x // 7)
                    advance(c, x * 64, 64, faces[c, first : first + 64, :])
                    continue
                for t in range(2):
                    first = Y_ROWS + 64 * t + x * 8
                    advance(c, x * 64 + 56 * t, 8, faces[c, first : first + 8, :])
                first = (x - 1) * 48
                advance(c, x * 64 + 8, 48, inner[c, first : first + 48, :])
        total = field.at[later]
        if directions is ALL:
            collect_y(total, slot, near_place, gain)
            multiply_early(later)
            wait_sent(directions, slot)
            collect(total, [d for d in ALL if kind_of(d) != "y"], slot, gain)
            collect_y(total, slot, 1 - near_place, gain)
        else:
            wait_sent(directions, slot)
            collect(total, directions, slot, gain)

    @pl.when(near_place == 0)
    def _():
        collect_y(field.at[0], 0, 0, 1.0)

    multiply_early(0)
    wait_sent(DOWN, 0)
    collect(field.at[0], [d for d in DOWN if kind_of(d) != "y"], 0, 1.0)

    @pl.when(near_place == 1)
    def _():
        collect_y(field.at[0], 0, 0, 1.0)

    apply(0, ALL, 1.0, False)

    def two_steps(k, carry):
        apply(1, ALL, 2.0, True)
        apply(0, ALL, 2.0, True)
        return carry

    lax.fori_loop(0, (DEGREE - 2) // 2, two_steps, 0)
    apply(1, UP, 2.0, True)
    last = 0

    owned_z = lax.broadcasted_iota(jnp.int32, (7 * 8, STATES), 0) % 8 < 7
    blocks = []
    for c in range(2):
        for x in range(NPE - 1):
            block = field[last, c, x * 64 : x * 64 + 56, :]
            blocks.append(jnp.where(owned_z, block, 0.0))
    columns = jnp.concatenate(blocks, axis=0)
    high, low = split(columns)
    parts[...] = jnp.concatenate([high, low], axis=1)
    both = lax.dot_general(
        high,
        parts[...],
        (((0,), (0,)), ((), ())),
        preferred_element_type=F32,
    )
    cross = both[:, STATES:]
    gram[...] = both[:, :STATES] + (cross + cross.T)

    piece = STATES // ring
    mine = pl.ds(pl.multiple_of(ring_place * piece, piece), piece)

    def scatter(k, j):
        device, place = in_ring(j)
        rows = pl.ds(pl.multiple_of(place * piece, piece), piece)
        return pltpu.make_async_remote_copy(
            src_ref=gram.at[rows],
            dst_ref=r_scatter.at[k],
            send_sem=sum_send.at[0],
            recv_sem=sum_recv.at[0],
            device_id=device,
            device_id_type=MESH,
        )

    def reduce(j):
        return pltpu.make_async_remote_copy(
            src_ref=r_reduce.at[other_place],
            dst_ref=r_reduce.at[other_place],
            send_sem=sum_send.at[1],
            recv_sem=sum_recv.at[1],
            device_id=across(j),
            device_id_type=MESH,
        )

    def gather(j):
        return pltpu.make_async_remote_copy(
            src_ref=r_gather.at[mine],
            dst_ref=r_gather.at[mine],
            send_sem=sum_send.at[2],
            recv_sem=sum_recv.at[2],
            device_id=in_ring(j)[0],
            device_id_type=MESH,
        )

    def waiter(ref, k):
        return pltpu.make_async_remote_copy(
            src_ref=ref,
            dst_ref=ref,
            send_sem=sum_send.at[k],
            recv_sem=sum_recv.at[k],
            device_id=neighbour((1, 0, 0)),
            device_id_type=MESH,
        )

    for k, j in enumerate(turns(nx, 2)):
        scatter(k, j).start()
    waiter(r_scatter, 0).wait_recv()
    r_reduce[other_place] = gram[mine, :] + jnp.sum(r_scatter[...], axis=0)
    for j in turns(4, 4):
        reduce(j).start()
    waiter(r_scatter, 0).wait_send()
    waiter(r_reduce.at[pl.ds(0, others - 1)], 1).wait_recv()
    nodes = 686 * nx * ny * nz
    r_gather[mine, :] = jnp.sum(r_reduce[...], axis=0) * (1.0 / nodes)
    for j in turns(nx, 2):
        gather(j).start()
    waiter(r_reduce.at[pl.ds(0, others - 1)], 1).wait_send()
    rest = r_gather.at[pl.ds(0, piece * (ring - 1))]
    waiter(rest, 2).wait_recv()

    total = r_gather[...]
    diagonal = lax.broadcasted_iota(jnp.int32, (STATES, STATES), 0) == (
        lax.broadcasted_iota(jnp.int32, (STATES, STATES), 1)
    )
    trace = jnp.sum(jnp.where(diagonal, total, 0.0), keepdims=True)
    three = jnp.where(diagonal, 3.0, 0.0)

    def newton(k, pair):
        root, inverse = pair
        middle = three - product(inverse, root)
        return 0.5 * product(root, middle), 0.5 * product(middle, inverse)

    scaled = total / trace
    middle = three - scaled
    root, inverse = lax.fori_loop(
        0, NS_STEPS - 2, newton, (0.5 * product(scaled, middle), 0.5 * middle)
    )
    inverse = 0.5 * product(three - product(inverse, root), inverse)
    high, low = split(inverse / jnp.sqrt(trace))
    upper = jnp.concatenate([high, low], axis=1)
    lower = jnp.concatenate([high, jnp.zeros_like(low)], axis=1)
    both = jnp.dot(
        parts[...], jnp.concatenate([upper, lower], axis=0), preferred_element_type=F32
    )
    turned = both[:, :STATES] + both[:, STATES:]
    for c in range(2):
        for x in range(NPE - 1):
            for y in range(NPE - 1):
                row = ((c * 7 + x) * 7 + y) * 8
                out_ref[x, y, c * 7 : c * 7 + 7, :] = turned[row : row + 7]
    waiter(rest, 2).wait_send()


def shards(wavefunctions, hamiltonians, cell_order):
    sizes = tuple(lax.axis_size(a) for a in AXES)
    ring, others = sizes[0] * 2, sizes[1] // 2 * sizes[2]
    piece = STATES // ring
    matrices = hamiltonians.reshape((2, CDOF, CDOF))
    orders = cell_order.reshape((2, CDOF))
    kinds = len(KINDS)
    return pl.pallas_call(
        functools.partial(kernel, sizes),
        out_shape=pltpu.VMEM(wavefunctions.shape, F32),
        in_specs=[pl.BlockSpec(memory_space=pltpu.HBM)] * 3,
        out_specs=pl.BlockSpec(memory_space=pltpu.VMEM),
        scratch_shapes=[
            pltpu.VMEM(wavefunctions.shape, F32),
            pltpu.VMEM((2, CDOF, CDOF), F32),
            pltpu.VMEM((2, ROWS, CDOF), BF16),
            pltpu.VMEM((2, EARLY, CDOF), BF16),
            pltpu.VMEM((2, LATE, CDOF), BF16),
            pltpu.VMEM((2, CDOF), jnp.int32),
            pltpu.VMEM((2, 2 * ROWS, EARLY), BF16),
            pltpu.VMEM((2, 2 * SENT, LATE), BF16),
            pltpu.VMEM((2, 2 * INNER, LATE), BF16),
            pltpu.VMEM((2, ROWS, STATES), F32),
            pltpu.VMEM((2, 2, CDOF, STATES), F32),
            pltpu.VMEM((2, 64, STATES), F32),
            pltpu.VMEM((2, 256, STATES), F32),
            pltpu.VMEM((2, INNER + 32, STATES), F32),
            pltpu.VMEM((2, 2, 8, STATES), F32),
            pltpu.VMEM((2, 2, 2, 64, STATES), F32),
            pltpu.VMEM((2, 2, 2, 64, STATES), F32),
            pltpu.VMEM((2, 2, 64, STATES), F32),
            pltpu.VMEM((2, 4, 2, 8, STATES), F32),
            pltpu.VMEM((2, 4, 8, STATES), F32),
            pltpu.VMEM((2, 4, 8, STATES), F32),
            pltpu.VMEM((2, 8, STATES), F32),
            pltpu.VMEM((2 * 7 * 7 * 8, 2 * STATES), BF16),
            pltpu.VMEM((STATES, STATES), F32),
            pltpu.VMEM((ring - 1, piece, STATES), F32),
            pltpu.VMEM((others, piece, STATES), F32),
            pltpu.VMEM((STATES, STATES), F32),
            pltpu.SemaphoreType.DMA((4,)),
            pltpu.SemaphoreType.DMA((kinds,)),
            pltpu.SemaphoreType.DMA((2, 2 + kinds)),
            pltpu.SemaphoreType.DMA((3,)),
            pltpu.SemaphoreType.DMA((3,)),
        ],
        compiler_params=pltpu.CompilerParams(
            collective_id=0, has_side_effects=True, vmem_limit_bytes=56 << 20
        ),
    )(wavefunctions, matrices, orders)


def solution(mesh):
    in_specs = (
        P("gx", "gy", "gz", None),
        P("gx", "gy", "gz", None, None),
        P("gx", "gy", "gz", None),
    )
    out_specs = P("gx", "gy", "gz", None)
    return jax.shard_map(
        shards, mesh=mesh, in_specs=in_specs, out_specs=out_specs, check_vma=False
    )
```
